32 devices in a mesh: dp: 16 (over z, y, core), blk: 2 (over x).
Axes of the slice: x: 2, y: 2, z: 4, core: 2. Of those that a mesh axis runs over, the one named last changes fastest.
Arguments:
- tokens: bfloat16 [32, 1024, 512], P('dp', 'blk'), may hold values from -6 to 6
- memory: bfloat16 [32, 1024, 512], P('dp', 'blk'), may hold values from -6 to 6
- segments: int32 [32, 1024], P('dp'), may hold values from 0 to 127, as said below
- w_qkv: bfloat16 [512, 1536], replicated, may hold values from -0.25 to 0.25
- w_self_out: bfloat16 [512, 512], replicated, may hold values from -1 to 1
- w_cross_q: bfloat16 [512, 512], replicated, may hold values from -0.25 to 0.25
- w_cross_kv: bfloat16 [512, 1024], replicated, may hold values from -0.25 to 0.25
- w_cross_out: bfloat16 [512, 512], replicated, may hold values from -1 to 1
- w_up: bfloat16 [512, 2048], replicated, may hold values from -0.25 to 0.25
- w_down: bfloat16 [2048, 512], replicated, may hold values from -0.125 to 0.125
- norm_gains: float32 [512, 3], replicated, may hold values from 0.1 to 1.9
- shifts: float32 [512, 10], replicated, may hold values from -2 to 2
- up_shift: float32 [2048], replicated, may hold values from -2 to 2
- cotangent: bfloat16 [32, 1024, 512], P('dp', 'blk'), may hold values from -6 to 6
Outputs:
- output: bfloat16 [32, 1024, 512], P('dp', 'blk')
- grad_tokens: float32 [32, 1024, 512], P('dp', 'blk')
- grad_memory: float32 [32, 1024, 512], P('dp', 'blk')
- grad_w_qkv: float32 [512, 1536], P('blk')
- grad_w_self_out: float32 [512, 512], P('blk')
- grad_w_cross_q: float32 [512, 512], P('blk')
- grad_w_cross_kv: float32 [512, 1024], P('blk')
- grad_w_cross_out: float32 [512, 512], P('blk')
- grad_w_up: float32 [512, 2048], P('blk')
- grad_w_down: float32 [2048, 512], P('blk')
- grad_norm_gains: float32 [512, 3], P('blk')
- grad_shifts: float32 [512, 10], P('blk')
- grad_up_shift: float32 [2048], P('blk')
The draws below stay inside these ranges and needn't reach their ends.
Inputs may be any that keep to these rules, and one draw needn't show every extreme that they name: `segments`: each row's sentence numbers start at 0 and rise by one at each new sentence. In each aligned group of 2 rows (those of one index of dp) one row, which one drawn from the seed, is a single sentence; in the row after it (cyclically within the group) every sentence but the last has exactly max(2, 8) tokens; in the others every sentence has max(2, 8) tokens or more and at most 128 except the last, which may be longer.
All inputs are finite; a program needn't handle non-finite values.
Results may differ from the reference program's by a relative error of at most 0.025.
Values may be sent and summed in bfloat16 or wider, within the bound.
No kernel may reach another device: no remote copies, remote signals or barrier semaphores. Data moves between devices by JAX's collectives and lax.ppermute only.
A program may use at most 384 MiB of HBM per device.

```python
import jax
import jax.numpy as jnp
from jax import lax

D = 512
FF = 2048
HEADS = 8
MEM = 1024
SEQ = 1024
SEQS = 2
NSEQ = 32


def draw_segments(key, part):
    key = jax.random.fold_in(key, 17)
    key_lengths, key_single = jax.random.split(key)
    shortest = max(2, SEQ // 128)
    longest = max(shortest + 1, SEQ // 8 + 1)
    sentence_count = SEQ // shortest + 1
    lengths = jax.random.randint(key_lengths, (NSEQ, sentence_count), shortest, longest)
    sentence_ends = jnp.cumsum(lengths, 1)
    places = jnp.arange(SEQ)
    numbers = jnp.sum((places[None, :, None] >= sentence_ends[:, None, :]).astype(jnp.int32), 2)
    last_number = numbers[:, SEQ - shortest]
    numbers = jnp.minimum(numbers, last_number[:, None])
    dense_numbers = jnp.minimum(places // shortest, (SEQ - shortest) // shortest)
    chosen = jax.random.randint(key_single, (NSEQ // SEQS, 1), 0, SEQS)
    row_numbers = jnp.arange(SEQS)[None, :]
    single_rows = (row_numbers == chosen).reshape(NSEQ)
    dense_rows = (row_numbers == (chosen + 1) % SEQS).reshape(NSEQ)
    numbers = jnp.where(dense_rows[:, None], dense_numbers[None, :], numbers)
    return jnp.where(single_rows[:, None], 0, numbers).astype(jnp.int32)


def spiked(values, stream_key, source, target, shards_of, factor):
    owner, partner = [(jnp.arange(values.shape[axis_at]) // (values.shape[axis_at] // shards_of)).reshape([-1 if axis == axis_at else 1 for axis in range(values.ndim)]) for axis_at in (source, target)]
    chosen = jax.random.permutation(stream_key, shards_of)[partner]
    strong = (owner == chosen) | (owner == (partner + shards_of // 2) % shards_of)
    return jnp.where(strong, factor * values, values)


def steps_of(key, extent, cuts, low, top_value):
    gain, own = 1.0, jax.random.fold_in(key, 6)
    for dim, parts in cuts:
        draws = jnp.exp(jax.random.uniform(jax.random.fold_in(own, dim), (parts,), jnp.float32, low / len(cuts), top_value / len(cuts)))
        gain = gain * jnp.repeat(draws, extent[dim] // parts).reshape([-1 if axis == dim else 1 for axis in range(len(extent))])
    return gain


def scatter_about(rng, dims, scale, most, pieces=(), kind=jnp.bfloat16):
    drawn = scale * jax.random.normal(rng, dims, jnp.float32)
    if pieces:
        drawn = drawn * steps_of(rng, dims, pieces, -0.22, 0.18)
    return jnp.clip(drawn, -most, most).astype(kind)


def bell_draw_with(rng, extent, scale, limit, cuts, heavy, dtype=jnp.bfloat16):
    drawn = scale * jax.random.normal(rng, extent, jnp.float32)
    if cuts:
        drawn = drawn * steps_of(rng, extent, cuts, -0.22, 0.18)
    return jnp.clip(spiked(drawn, jax.random.fold_in(rng, 3), *heavy), -limit, limit).astype(dtype)


def setup_inputs(seed: int = 0) -> dict:
    key_list = jax.random.split(jax.random.key(seed), 15)
    tokens = bell_draw_with(key_list[0], (NSEQ, SEQ, D), 1.0, 6.0, ((0, 16), (1, 2)), (0, 2, 16, 2.0))
    memory = bell_draw_with(key_list[1], (NSEQ, MEM, D), 1.0, 6.0, ((0, 16), (1, 2)), (0, 2, 16, 2.0))
    segments = draw_segments(jax.random.fold_in(key_list[14], 71), 0)
    w_qkv = scatter_about(key_list[3], (D, 3 * D), D ** -0.5, 0.25)
    w_self_out = scatter_about(key_list[4], (D, D), (D // 16) ** -0.5, 1.0)
    w_cross_q = scatter_about(key_list[5], (D, D), D ** -0.5, 0.25)
    w_cross_kv = scatter_about(key_list[6], (D, 2 * D), D ** -0.5, 0.25)
    w_cross_out = scatter_about(key_list[7], (D, D), (D // 16) ** -0.5, 1.0)
    w_up = scatter_about(key_list[8], (D, FF), D ** -0.5, 0.25)
    w_down = scatter_about(key_list[9], (FF, D), FF ** -0.5, 0.125)
    norm_gains = jnp.clip(1.0 + 0.18 * jax.random.normal(key_list[10], (D, 3), jnp.float32), 0.1, 1.9)
    shifts = scatter_about(key_list[11], (D, 10), 0.3, 2.0, (), jnp.float32)
    up_shift = scatter_about(key_list[12], (FF,), 0.3, 2.0, (), jnp.float32)
    cotangent = scatter_about(key_list[13], (NSEQ, SEQ, D), 1.0, 6.0, ((0, 16), (1, 2)))
    return dict(tokens=tokens, memory=memory, segments=segments, w_qkv=w_qkv, w_self_out=w_self_out, w_cross_q=w_cross_q, w_cross_kv=w_cross_kv, w_cross_out=w_cross_out, w_up=w_up, w_down=w_down, norm_gains=norm_gains, shifts=shifts, up_shift=up_shift, cotangent=cotangent)


@jax.custom_vjp
def low(v):
    return lax.optimization_barrier(v.astype(jnp.bfloat16)).astype(jnp.float32)

@jax.custom_vjp
def low_back(v):
    return v

def low_keep(v):
    return (low(v), None)

def low_pass(kept, grad):
    return (grad,)

def back_keep(v):
    return (v, None)

def back_low(kept, grad):
    return (low(grad),)
low.defvjp(low_keep, low_pass)
low_back.defvjp(back_keep, back_low)
precise = lax.Precision.HIGHEST

def layer_norm(values, gain_vec, shift_vec):
    center = values - lax.optimization_barrier(jnp.mean(values, -1, keepdims=True))
    spread = lax.optimization_barrier(jnp.mean(center * center, -1, keepdims=True))
    return center * lax.rsqrt(spread + 1e-05) * gain_vec + shift_vec

def project(values, weight):
    return jnp.einsum('sbd,de->sbe', values, weight, precision=precise)

def split_heads(values):
    return values.reshape(values.shape[0], values.shape[1], HEADS, values.shape[2] // HEADS)

def attend(queries, key_block, value_block, allowed):
    score_scale = (queries.shape[2] // HEADS) ** (-0.5)
    scores = jnp.einsum('gqhe,gkhe->ghqk', split_heads(queries), split_heads(key_block), precision=precise)
    scores = low_back(scores * score_scale)
    scores = jnp.where(allowed[:, None], scores, -1e+30)
    highest = lax.optimization_barrier(jnp.max(scores, -1, keepdims=True))
    raised = jnp.exp(scores - highest)
    weights = low(raised / lax.optimization_barrier(jnp.sum(raised, -1, keepdims=True)))
    mixed = jnp.einsum('ghqk,gkhe->gqhe', weights, split_heads(value_block), precision=precise)
    return low(low_back(mixed.reshape(queries.shape)))

def layer_group(tokens, memory, token_segments, mem_segments, weights):
    w_qkv, w_self_out, w_cross_q, w_cross_kv, w_cross_out, w_up, w_down, norm_gains, shifts, up_shift = weights
    model_width = tokens.shape[2]
    places = jnp.arange(tokens.shape[1])
    self_allowed = (token_segments[:, :, None] == token_segments[:, None, :]) & (places[None, None, :] <= places[None, :, None])
    cross_allowed = token_segments[:, :, None] == mem_segments[:, None, :]
    projected = low_back(project(tokens, w_qkv))
    queries = low(projected[..., :model_width] + shifts[:, 0])
    key_block = low(projected[..., model_width:2 * model_width])
    value_block = low(projected[..., 2 * model_width:] + shifts[:, 1])
    attended = attend(queries, key_block, value_block, self_allowed)
    normed_one = layer_norm(tokens + low_back(project(attended, w_self_out)) + shifts[:, 2], norm_gains[:, 0], shifts[:, 3])
    cross_queries = low(low_back(project(low(normed_one), w_cross_q)) + shifts[:, 4])
    memory_proj = low_back(project(memory, w_cross_kv))
    cross_keys = low(memory_proj[..., :model_width])
    cross_values = low(memory_proj[..., model_width:] + shifts[:, 5])
    cross_out = attend(cross_queries, cross_keys, cross_values, cross_allowed)
    normed_two = layer_norm(normed_one + low_back(project(cross_out, w_cross_out)) + shifts[:, 6], norm_gains[:, 1], shifts[:, 7])
    hidden = low(jax.nn.gelu(low_back(project(low(normed_two), w_up)) + up_shift))
    return layer_norm(normed_two + low_back(project(hidden, w_down)) + shifts[:, 8], norm_gains[:, 2], shifts[:, 9])

def reference(tokens, memory, segments, w_qkv, w_self_out, w_cross_q, w_cross_kv, w_cross_out, w_up, w_down, norm_gains, shifts, up_shift, cotangent):
    weights = (w_qkv.astype(jnp.float32), w_self_out.astype(jnp.float32), w_cross_q.astype(jnp.float32), w_cross_kv.astype(jnp.float32), w_cross_out.astype(jnp.float32), w_up.astype(jnp.float32), w_down.astype(jnp.float32), norm_gains.astype(jnp.float32), shifts.astype(jnp.float32), up_shift.astype(jnp.float32))
    mem_map = jnp.arange(MEM) * SEQ // MEM
    memory_segments = segments[:, mem_map]
    group_count = tokens.shape[0] // 2
    grouped_segments = segments.reshape(group_count, 2, SEQ)
    grouped_memory_segments = memory_segments.reshape(group_count, 2, MEM)

    def forward(token_values, memory_values, weight_values):

        def one_group(inputs):
            return layer_group(inputs[0], inputs[1], inputs[2], inputs[3], weight_values)
        grouped = (token_values.reshape(group_count, 2, SEQ, D), memory_values.reshape(group_count, 2, MEM, D), grouped_segments, grouped_memory_segments)
        return lax.map(jax.checkpoint(one_group), grouped).reshape(token_values.shape)
    result, pullback = jax.vjp(forward, tokens.astype(jnp.float32), memory.astype(jnp.float32), weights)
    grad_tokens, grad_memory, grads = pullback(cotangent.astype(jnp.float32))
    return (result.astype(jnp.bfloat16), grad_tokens, grad_memory, grads[0], grads[1], grads[2], grads[3], grads[4], grads[5], grads[6], grads[7], grads[8], grads[9])
```

```python
import functools

import jax
import jax.numpy as jnp
import numpy as np
from jax import lax
from jax.experimental import pallas as pl
from jax.experimental.pallas import tpu as pltpu
from jax.sharding import PartitionSpec as P

HEADS = 8
NEG = -1e30
F32 = jnp.float32
BF = jnp.bfloat16
GELU_A = 0.7978845608028654
GELU_B = 0.7978845608028654 * 0.044715
ROW = 3
UP = 13
VROWS = 24


def nn(a, b):
    return jnp.dot(a, b, preferred_element_type=F32)


def nt(a, b):
    return lax.dot_general(a, b, (((1,), (1,)), ((), ())), preferred_element_type=F32)


def tn(a, b):
    return lax.dot_general(a, b, (((0,), (0,)), ((), ())), preferred_element_type=F32)


def norm(values):
    center = values - jnp.mean(values, -1, keepdims=True)
    rstd = lax.rsqrt(jnp.mean(center * center, -1, keepdims=True) + 1e-05)
    return center * rstd, rstd


def norm_back(grad, unit, rstd, gain):
    scaled = grad * gain
    return (
        scaled
        - jnp.mean(scaled, -1, keepdims=True)
        - unit * jnp.mean(scaled * unit, -1, keepdims=True)
    ) * rstd


def col_sum(values):
    return jnp.sum(values, 0, keepdims=True)


def whole(shape):
    zeros = (0,) * len(shape)
    return pl.BlockSpec(shape, lambda *_: zeros, pipeline_mode=pl.Buffered(1))


PARAMS = pltpu.CompilerParams(vmem_limit_bytes=60 * 1024 * 1024)


def cost(us):
    return pl.CostEstimate(flops=int(us * 1.1e9), bytes_accessed=0, transcendentals=0)


def shape_of(shape, kind):
    return jax.ShapeDtypeStruct(shape, kind)


PLACE, SIDE, CROSSES, ORDER = 0, 1, 2, 3


def row_spec(shape, row=None):
    block = (1, *shape[1:])
    rest = (0,) * (len(shape) - 1)
    if row is None:
        return pl.BlockSpec(block, lambda r, *_: (r, *rest))
    return pl.BlockSpec(block, lambda *_: (row, *rest))


def arg_spec(shape, row=None):
    block = (1, *shape[1:])
    rest = (0,) * (len(shape) - 1)
    if row is None:
        return pl.BlockSpec(block, lambda r, segs, info: (info[ORDER + r], *rest))
    return pl.BlockSpec(block, lambda r, segs, info: (info[ORDER + row], *rest))


def call(kernel, name, us, grid, in_specs, out_specs, out_shape, scratch):
    return pl.pallas_call(
        kernel,
        grid_spec=pltpu.PrefetchScalarGridSpec(
            num_scalar_prefetch=2, grid=grid, in_specs=in_specs, out_specs=out_specs, scratch_shapes=scratch
        ),
        out_shape=out_shape,
        compiler_params=PARAMS,
        cost_estimate=pl.CostEstimate(flops=int(us * 1.1e9), bytes_accessed=0, transcendentals=0),
        name=name,
    )


def put_keys(found, vec_ref, shift_v, k_ref, v_ref, kt_ref, vt_ref):
    width = found.shape[1] // 2
    k = found[:, :width]
    v = found[:, width:] + vec_ref[ROW + shift_v : ROW + shift_v + 1, :]
    k_ref[0] = k.astype(BF)
    v_ref[0] = v.astype(BF)
    kt_ref[0] = k.T.astype(BF)
    vt_ref[0] = v.T.astype(BF)


def scaled(queries):
    low = queries.astype(BF).astype(F32)
    return (low * (queries.shape[1] // HEADS) ** -0.5).astype(BF)


def project_kernel(segs, info, tok_ref, mem_ref, wqkv_ref, wckv_ref, vec_ref, q_ref, k_ref, v_ref, kt_ref, vt_ref, ck_ref, cv_ref, ckt_ref, cvt_ref):
    width = tok_ref.shape[2]
    found = nn(tok_ref[0], wqkv_ref[...])
    q_ref[0] = scaled(found[:, :width] + vec_ref[ROW : ROW + 1, :])
    put_keys(found[:, width:], vec_ref, 1, k_ref, v_ref, kt_ref, vt_ref)
    put_keys(nn(mem_ref[0], wckv_ref[...]), vec_ref, 5, ck_ref, cv_ref, ckt_ref, cvt_ref)


def project(segs, info, tokens, memory, wqkv, wckv, vec):
    rows, block, width = tokens.shape
    mem_block = memory.shape[1]
    shapes = [(rows, block, width)] * 3 + [(rows, width, block)] * 2
    shapes += [(rows, mem_block, width)] * 2 + [(rows, width, mem_block)] * 2
    return call(
        project_kernel, "project", 7, (rows,),
        [arg_spec(tokens.shape), arg_spec(memory.shape), whole(wqkv.shape), whole(wckv.shape), whole(vec.shape)],
        [row_spec(s) for s in shapes],
        [shape_of(s, BF) for s in shapes],
        [],
    )(segs, info, tokens, memory, wqkv, wckv, vec)


class Dims:
    def __init__(self, rows, block, key_block, blocks, seq_len, width):
        self.rows, self.block, self.key_block, self.blocks, self.seq_len = rows, block, key_block, blocks, seq_len
        self.width = width
        self.tile = min(256, block)
        self.step = min(256, key_block)


def split_pairs(ref, qoff, dims, keep_ref):
    lane = lax.broadcasted_iota(jnp.int32, (1, 128), 1)
    for h in range(HEADS):
        side = (lane < 64) if h % 2 == 0 else (lane >= 64)
        pair = slice(h // 2 * 128, h // 2 * 128 + 128)
        keep_ref[h] = ref[0, pl.ds(qoff, dims.tile), pair] * side.astype(F32).astype(BF)


def over_tiles(causal, dims, row, segs, info, segq_ref, segk_ref, bias_ref, qin, body):
    tile, step_size = dims.tile, dims.step
    mine, at = info[PLACE], info[ORDER + row]
    qoff = pl.multiple_of(mine * dims.block + qin, tile)
    q_first, q_last = segs[at, qoff], segs[at, qoff + tile - 1]
    keys_all = dims.key_block * dims.blocks
    for source in range(dims.blocks):
        owner = lax.rem(mine + source, dims.blocks)

        def step(kt, carry, source=source, owner=owner):
            inner = pl.multiple_of(kt * step_size, step_size)
            koff = pl.multiple_of(owner * dims.key_block + inner, step_size)
            k_first = segs[at, koff * dims.seq_len // keys_all]
            k_last = segs[at, (koff + step_size - 1) * dims.seq_len // keys_all]
            need = (k_first <= q_last) & (k_last >= q_first)
            if causal:
                need = need & (koff < qoff + tile)

            @pl.when(need)
            def _():
                across = jnp.broadcast_to(segk_ref[0, :, pl.ds(koff, step_size)], (tile, step_size))
                allowed = across.T == segq_ref[0, :, pl.ds(qoff, tile)]
                if causal:
                    kpos = lax.broadcasted_iota(jnp.int32, (step_size, tile), 0) + koff
                    qpos = lax.broadcasted_iota(jnp.int32, (step_size, tile), 1) + qoff
                    allowed = allowed & (kpos <= qpos)
                bias_ref[...] = jnp.where(allowed, 0.0, NEG)
                body(source, inner)

            return carry

        lax.fori_loop(0, dims.key_block // step_size, step, 0)


def far_needed(causal, dims, info, row, source):
    need = info[CROSSES] == 1 if dims.rows == 2 and row == 0 else info[CROSSES] >= 0
    if causal:
        need = need & (lax.rem(info[PLACE] + source, dims.blocks) < info[PLACE])
    return need


def forward_scratch(dims):
    return [
        pltpu.VMEM((HEADS, dims.tile, 128), BF),
        pltpu.VMEM((dims.step, dims.tile), F32),
        pltpu.VMEM((HEADS, dims.tile), F32),
        pltpu.VMEM((HEADS, dims.tile), F32),
        pltpu.VMEM((dims.width, dims.tile), F32),
        pltpu.VMEM((HEADS, dims.step, dims.tile), F32),
        pltpu.VMEM((HEADS, dims.step, dims.tile), BF),
    ]


def forward_tiles(causal, dims, row, segs, info, q_ref, segq_ref, segk_ref, k_refs, vt_refs, att_ref, lse_ref, scratch):
    qm_ref, bias_ref, top_ref, total_ref, acc_ref, score_ref, raised_ref = scratch

    def query_tile(i, carry):
        qin = pl.multiple_of(i * dims.tile, dims.tile)
        queries = pl.ds(qin, dims.tile)
        split_pairs(q_ref, qin, dims, qm_ref)
        top_ref[...] = jnp.full_like(top_ref, NEG)
        total_ref[...] = jnp.zeros_like(total_ref)
        acc_ref[...] = jnp.zeros_like(acc_ref)

        def body(source, inner):
            here = pl.ds(inner, dims.step)
            old = top_ref[...]
            new, fade, more = [], [], []
            for h in range(HEADS):
                pair = slice(h // 2 * 128, h // 2 * 128 + 128)
                scores = nt(k_refs[source][0, here, pair], qm_ref[h]) + bias_ref[...]
                score_ref[h] = scores
                new.append(jnp.maximum(old[h : h + 1, :], jnp.max(scores, 0, keepdims=True)))
                fade.append(jnp.exp(old[h : h + 1, :] - new[h]))
            for h in range(HEADS):
                raised = jnp.exp(score_ref[h] - new[h])
                raised_ref[h] = raised.astype(BF)
                more.append(col_sum(raised))
            for h in range(HEADS):
                heads = slice(h * 64, h * 64 + 64)
                acc_ref[heads, :] = acc_ref[heads, :] * fade[h] + nn(vt_refs[source][0, heads, here], raised_ref[h])
            top_ref[...] = jnp.concatenate(new, 0)
            total_ref[...] = total_ref[...] * jnp.concatenate(fade, 0) + jnp.concatenate(more, 0)

        over_tiles(causal, dims, row, segs, info, segq_ref, segk_ref, bias_ref, qin, body)
        total = total_ref[...]
        lse_ref[0, :, queries] = top_ref[...] + jnp.log(total)
        inverse = 1.0 / total
        for h in range(HEADS):
            heads = slice(h * 64, h * 64 + 64)
            acc_ref[heads, :] = acc_ref[heads, :] * inverse[h : h + 1, :]
        att_ref[0, queries, :] = acc_ref[...].T.astype(BF)
        return carry

    lax.fori_loop(0, dims.block // dims.tile, query_tile, 0)


def forward_kernel(causal, dims, far_count, segs, info, q_ref, segq_ref, segk_ref, base_ref, w_kv_ref, w_out_ref, w_cq_ref, vec_ref, k_ref, vt_ref, *refs):
    far_refs, refs = refs[: far_count * (dims.blocks - 1)], refs[far_count * (dims.blocks - 1) :]
    outs = 5 if causal else 4
    att_ref, lse_ref, unit_ref, rstd_ref = refs[:4]
    far_keys = refs[outs : outs + 4 * (dims.blocks - 1)]
    scratch = refs[outs + 4 * (dims.blocks - 1) :]
    row = pl.program_id(0)
    width = dims.width
    k_refs, vt_refs = [k_ref], [vt_ref]
    at = width if causal else 0
    for source in range(1, dims.blocks):
        keys = far_keys[4 * source - 4 : 4 * source]
        for which in range(far_count):
            ref = far_refs[far_count * (source - 1) + which]
            need = far_needed(causal, dims, info, which if far_count == 2 else 1, source)
            if far_count == 2:
                need = need & (row == which)

            @pl.when(need)
            def _(ref=ref, keys=keys):
                put_keys(nn(ref[0], w_kv_ref[:, at:]), vec_ref, 1 if causal else 5, *keys)

        k_refs.append(keys[0])
        vt_refs.append(keys[3])
    forward_tiles(causal, dims, row, segs, info, q_ref, segq_ref, segk_ref, k_refs, vt_refs, att_ref, lse_ref, scratch)
    base = base_ref[0].astype(F32)
    if not causal:
        base = base * vec_ref[0:1, :] + vec_ref[ROW + 3 : ROW + 4, :]
    shift = ROW + 2 if causal else ROW + 6
    unit, rstd = norm(base + nn(att_ref[0], w_out_ref[...]) + vec_ref[shift : shift + 1, :])
    unit_ref[0] = unit
    rstd_ref[0] = jnp.broadcast_to(rstd, rstd_ref.shape[1:])
    if causal:
        normed = (unit * vec_ref[0:1, :] + vec_ref[ROW + 3 : ROW + 4, :]).astype(BF)
        refs[4][0] = scaled(nn(normed, w_cq_ref[...]) + vec_ref[ROW + 4 : ROW + 5, :])


def attend_forward(causal, segs, info, q, segq, segk, base, w_kv, w_out, w_cq, vec, key, value_t, far):
    rows, block, width = q.shape
    key_block = key.shape[1]
    dims = Dims(rows, block, key_block, len(far) + 1, segs.shape[1], width)
    far_count = len(far[0]) if far else 1
    far_arrays = [a for arrays in far for a in arrays]
    base_spec = arg_spec(base.shape) if causal else row_spec(base.shape)
    far_specs = [row_spec(a.shape) if far_count == 1 else row_spec(a.shape, 0) for a in far_arrays]
    out_shape = [
        shape_of(q.shape, BF),
        shape_of((rows, HEADS, block), F32),
        shape_of(q.shape, F32),
        shape_of((rows, block, 128), F32),
    ] + [shape_of(q.shape, BF)] * causal
    keys = [shape_of((rows, key_block, width), BF)] * 2 + [shape_of((rows, width, key_block), BF)] * 2
    out_shape += keys * len(far)
    return call(
        functools.partial(forward_kernel, causal, dims, far_count),
        "attend_self" if causal else "attend_cross",
        14, (rows,),
        [row_spec(q.shape), arg_spec(segq.shape), arg_spec(segk.shape), base_spec]
        + [whole(w.shape) for w in (w_kv, w_out, w_cq, vec)]
        + [row_spec(key.shape), row_spec(value_t.shape)]
        + far_specs,
        [row_spec(s.shape) for s in out_shape],
        out_shape,
        forward_scratch(dims),
    )(segs, info, q, segq, segk, base, w_kv, w_out, w_cq, vec, key, value_t, *far_arrays)


def backward_scratch(dims):
    return [
        pltpu.VMEM((HEADS, dims.tile, 128), BF),
        pltpu.VMEM((HEADS, dims.tile, 128), BF),
        pltpu.VMEM((dims.step, dims.tile), F32),
        pltpu.VMEM((dims.width, dims.block), F32),
        pltpu.VMEM((dims.blocks, dims.key_block, dims.width), F32),
        pltpu.VMEM((dims.blocks, dims.key_block, dims.width), F32),
        pltpu.VMEM((HEADS, dims.step, dims.tile), F32),
        pltpu.VMEM((HEADS, dims.step, dims.tile), BF),
        pltpu.VMEM((HEADS, dims.step, dims.tile), BF),
    ]


def backward_tiles(causal, dims, row, segs, info, q_ref, do_ref, lse_ref, dd_ref, segq_ref, segk_ref, k_refs, kt_refs, v_refs, scratch):
    qm_ref, dm_ref, bias_ref, dq_ref, dk_ref, dv_ref, weight_ref, low_ref, ds_ref = scratch
    dk_ref[...] = jnp.zeros_like(dk_ref)
    dv_ref[...] = jnp.zeros_like(dv_ref)
    dq_ref[...] = jnp.zeros_like(dq_ref)

    def query_tile(i, carry):
        qin = pl.multiple_of(i * dims.tile, dims.tile)
        queries = pl.ds(qin, dims.tile)
        split_pairs(q_ref, qin, dims, qm_ref)
        split_pairs(do_ref, qin, dims, dm_ref)

        def body(source, inner):
            here = pl.ds(inner, dims.step)
            lse, dd = lse_ref[0, :, queries], dd_ref[0, :, queries]
            for h in range(HEADS):
                pair = slice(h // 2 * 128, h // 2 * 128 + 128)
                weights = jnp.exp(nt(k_refs[source][0, here, pair], qm_ref[h]) + bias_ref[...] - lse[h : h + 1, :])
                weight_ref[h] = weights
                low_ref[h] = weights.astype(BF)
            for h in range(HEADS):
                pair = slice(h // 2 * 128, h // 2 * 128 + 128)
                grads = nt(v_refs[source][0, here, pair], dm_ref[h])
                ds_ref[h] = (weight_ref[h] * (grads - dd[h : h + 1, :])).astype(BF)
            for h in range(0, HEADS, 2):
                pair = slice(h // 2 * 128, h // 2 * 128 + 128)
                dv_ref[source, here, pair] += nn(low_ref[h], dm_ref[h]) + nn(low_ref[h + 1], dm_ref[h + 1])
                dk_ref[source, here, pair] += nn(ds_ref[h], qm_ref[h]) + nn(ds_ref[h + 1], qm_ref[h + 1])
            for h in range(HEADS):
                heads = slice(h * 64, h * 64 + 64)
                dq_ref[heads, queries] += nn(kt_refs[source][0, heads, here], ds_ref[h])

        over_tiles(causal, dims, row, segs, info, segq_ref, segk_ref, bias_ref, qin, body)
        return carry

    lax.fori_loop(0, dims.block // dims.tile, query_tile, 0)
    return dq_ref[...].T * (dims.width // HEADS) ** -0.5


def head_products(a, b):
    turned = (a.astype(F32) * b.astype(F32)).T
    return jnp.concatenate([col_sum(turned[h * 64 : h * 64 + 64]) for h in range(HEADS)], 0)


def put(buffer, earlier, at, value, first, part):
    done = 0
    while done < value.shape[0]:
        b, inner = divmod(first + done, part)
        count = min(part - inner, value.shape[0] - done)
        rows = slice(at + inner, at + inner + count)
        piece = value[done : done + count]
        if earlier is not None:
            piece = piece + earlier[b, rows, :].astype(F32)
        buffer[b, rows, :] = piece.astype(BF)
        done += count


def send_halves(info, buffer, outs, sems):
    half = buffer.shape[1] // 2
    side = info[SIDE]
    copies = []
    for k, out in enumerate(outs):
        start = pl.multiple_of((side if k == 0 else 1 - side) * half, 16)
        copies.append(pltpu.make_async_copy(buffer.at[:, pl.ds(start, half), :], out, sems.at[k]))
    for c in copies:
        c.start()
    for c in copies:
        c.wait()


def sum_specs(buffer_shape, last):
    blocks, rows, lanes = buffer_shape
    if last:
        half = shape_of((blocks, rows // 2, lanes), BF)
        return [half] * 2, [pl.BlockSpec(memory_space=pl.ANY)] * 2, [pltpu.VMEM(buffer_shape, BF), pltpu.SemaphoreType.DMA((2,))]
    return [shape_of(buffer_shape, BF)], [whole(buffer_shape)], []


def backward_kernel(causal, dims, row, has_earlier, last, segs, info, *refs):
    take = iter(refs)

    def some(count):
        return [next(take) for _ in range(count)]

    blocks, width = dims.blocks, dims.width
    q_ref, segq_ref, segk_ref, do_ref, lse_ref, dd_ref, vec_ref, vec_in = some(8)
    k_refs, kt_refs, v_refs, x_refs = some(blocks), some(blocks), some(blocks), some(blocks)
    if not causal:
        w_kv_ref = next(take)
        gp2_ref, unit1_ref, rstd1_ref, att_ref, wcq_ref, wso_ref = some(6)
    earlier = next(take) if has_earlier else None
    if not causal:
        gp1_ref, datt_ref, dself_ref = some(3)
    dx_refs = some(blocks)
    if causal:
        dq_out = next(take)
    vec_out = next(take)
    sum_refs = some(2 if last else 1)
    scratch = some(9)
    acc_ref = next(take)
    if last:
        buffer, sems = some(2)
    else:
        buffer = sum_refs[0]
    dk_ref, dv_ref = scratch[4:6]
    vec_out[...] = vec_in[...]
    part = width // blocks

    dq = backward_tiles(causal, dims, row, segs, info, q_ref, do_ref, lse_ref, dd_ref, segq_ref, segk_ref, k_refs, kt_refs, v_refs, scratch)
    low_q = dq.astype(BF)
    if causal:
        vec_out[ROW : ROW + 1, :] += col_sum(dq)
        dq_out[0] = low_q
        shift_v = 1
    else:
        shift_v = 5
        unit1 = unit1_ref[0]
        normed = (unit1 * vec_ref[0:1, :] + vec_ref[ROW + 3 : ROW + 4, :]).astype(BF)
        put(buffer, earlier, 0, tn(normed, low_q), 0, part)
        grad = gp2_ref[0] + nt(low_q, wcq_ref[...])
        gp1 = norm_back(grad, unit1, rstd1_ref[0][:, :1], vec_ref[0:1, :])
        gp1_ref[0] = gp1
        low_one = gp1.astype(BF)
        att = att_ref[0]
        put(buffer, earlier, part, tn(att, low_one), 0, part)
        datt = nt(low_one, wso_ref[...]).astype(BF)
        datt_ref[0] = datt
        dself_ref[0] = head_products(datt, att)
        vec_out[0:1, :] += col_sum(grad * unit1)
        vec_out[ROW + 2 : ROW + 3, :] += col_sum(gp1)
        vec_out[ROW + 3 : ROW + 4, :] += col_sum(grad)
        vec_out[ROW + 4 : ROW + 5, :] += col_sum(dq)

    for source in range(blocks):

        def back(source=source):
            x = x_refs[source][0]
            dv = dv_ref[source]
            low = jnp.concatenate([dk_ref[source].astype(BF), dv.astype(BF)], 1)
            vec_out[ROW + shift_v : ROW + shift_v + 1, :] += col_sum(dv)
            if causal:
                dx_refs[source][0] = low
            else:
                dx_refs[source][0] = nt(low, w_kv_ref[...]).astype(dx_refs[source].dtype)
            more = tn(x, low)
            if source == 0:
                acc_ref[...] = more
            else:
                acc_ref[...] += more

        if source == 0:
            back()
        else:
            pl.when(far_needed(causal, dims, info, row, source))(back)
            if not causal and dims.rows != 2:
                continue

            @pl.when(jnp.logical_not(far_needed(causal, dims, info, row, source)))
            def _(source=source):
                dx_refs[source][...] = jnp.zeros_like(dx_refs[source])

    if causal:
        put(buffer, earlier, 0, tn(x_refs[0][0], low_q), 0, part)
    first = part if causal else 2 * part
    for p in range(2 * width // 512):
        put(buffer, earlier, first + p * part, acc_ref[:, p * 512 : (p + 1) * 512], 0, part)
    if causal and last:
        base = 3 * part * (width // 512)
        buffer[:, base:, :] = jnp.zeros((blocks, buffer.shape[1] - base, 512), BF)
        hidden_part = 4 * 512 // blocks
        for b in range(blocks):
            buffer[b, base : base + UP, :part] = vec_out[:UP, b * part : (b + 1) * part].astype(BF)
            for k in range(max(1, hidden_part // 512)):
                first = b * hidden_part + k * 512
                count = min(512, hidden_part)
                piece = vec_out[UP + first // 512 : UP + first // 512 + 1, first % 512 : first % 512 + count]
                buffer[b, base + UP + k : base + UP + k + 1, :count] = piece.astype(BF)
    if last:
        send_halves(info, buffer, sum_refs, sems)


def attend_backward(causal, row, last, us, segs, info, q, segq, segk, d_out, lse, dd, vec, vec_in, keys, keys_t, values, inputs, w_kv, extra, earlier):
    rows, block, width = q.shape
    blocks, key_block = len(keys), keys[0].shape[1]
    dims = Dims(rows, block, key_block, blocks, segs.shape[1], width)

    def spec(a):
        return row_spec(a.shape, row if a.shape[0] == rows else 0)

    args = [q, segq, segk, d_out, lse, dd, vec, vec_in, *keys, *keys_t, *values, *inputs]
    in_specs = [spec(q), arg_spec(segq.shape, row), arg_spec(segk.shape, row), spec(d_out), spec(lse), spec(dd)]
    in_specs += [whole(vec.shape), whole(vec_in.shape)]
    in_specs += [spec(a) for a in (*keys, *keys_t, *values)]
    in_specs += [arg_spec(inputs[0].shape, row)] + [spec(a) for a in inputs[1:]]
    if not causal:
        args.append(w_kv)
        in_specs.append(whole(w_kv.shape))
    args += extra
    in_specs += [spec(a) for a in extra[:4]] + [whole(a.shape) for a in extra[4:]]
    if earlier is not None:
        args.append(earlier)
        in_specs.append(whole(earlier.shape))
    out_shape = []
    if not causal:
        out_shape += [shape_of((1, block, width), F32), shape_of((1, block, width), BF), shape_of((1, HEADS, block), F32)]
    if causal:
        out_shape += [shape_of((1, key_block, 2 * width), BF) for s in range(blocks)] + [shape_of((1, block, width), BF)]
    else:
        out_shape += [shape_of((1, key_block, width), F32 if s == 0 else BF) for s in range(blocks)]
    out_shape += [shape_of((VROWS, width), F32)]
    out_specs = [whole(s.shape) for s in out_shape]
    buffer_rows = (3 if causal else 4) * width // blocks * (width // 512) + (32 if causal and last else 0)
    shapes, specs, more = sum_specs((blocks, buffer_rows, 512), last)
    return call(
        functools.partial(backward_kernel, causal, dims, row, earlier is not None, last),
        "attend_self_back" if causal else "attend_cross_back",
        us, (1,), in_specs, out_specs + specs, out_shape + shapes,
        backward_scratch(dims) + [pltpu.VMEM((width, 2 * width), F32)] + more,
    )(segs, info, *args)


def tokens_back_kernel(rows, blocks, segs, info, *refs):
    take = iter(refs)
    per_row = [[next(take) for _ in range(2 + blocks)] for _ in range(rows)]
    w_ref = next(take)
    outs = [[next(take) for _ in range(blocks)] for _ in range(rows)]
    width = w_ref.shape[0]
    for (dq_ref, base_ref, *dkv_refs), out_refs in zip(per_row, outs):
        for source in range(blocks):
            grad = nt(dkv_refs[source][0], w_ref[:, width:])
            if source == 0:
                grad = grad + nt(dq_ref[0], w_ref[:, :width]) + base_ref[0]
            out_refs[source][0] = grad.astype(out_refs[source].dtype)


def tokens_back(segs, info, found, gp1, w):
    rows, blocks = len(found), len(found[0]) - 1
    args, out_shape = [], []
    for (*dkv, dq), base in zip(found, gp1):
        args += [dq, base, *dkv]
        out_shape += [shape_of(base.shape, F32 if s == 0 else BF) for s in range(blocks)]
    args.append(w)
    got = call(
        functools.partial(tokens_back_kernel, rows, blocks), "tokens_back", 8, (1,),
        [whole(a.shape) for a in args], [whole(s.shape) for s in out_shape], out_shape, [],
    )(segs, info, *args)
    return [got[r * blocks : (r + 1) * blocks] for r in range(rows)]


def feed_kernel(blocks, segs, info, unit2_ref, rstd2_ref, cot_ref, co_ref, wup_ref, wdown_ref, wco_ref, upshift_ref, vec_ref, *refs):
    out_ref, gp2_ref, dco_ref, dcross_ref, vec_out, keep_ref, send_ref = refs[:7]
    hid_ref, slope_ref, low_up_ref, normed_ref, low3_ref, co_all_ref, low2_ref, buffer, sems = refs[7:]
    width, hidden_width = wup_ref.shape
    panels = hidden_width // 512
    block = unit2_ref.shape[1]
    row = pl.program_id(0)
    here = pl.ds(pl.multiple_of(row * block, block), block)

    @pl.when(row == 0)
    def _():
        vec_out[...] = jnp.zeros_like(vec_out)

    unit2 = unit2_ref[0]
    normed = unit2 * vec_ref[1:2, :] + vec_ref[ROW + 7 : ROW + 8, :]
    normed_low = normed.astype(BF)
    normed_ref[here, :] = normed_low
    for p in range(panels):
        cols = slice(p * 512, (p + 1) * 512)
        up = nn(normed_low, wup_ref[:, cols]) + upshift_ref[p : p + 1, :]
        square = up * up
        bent = jnp.tanh(up * (GELU_A + GELU_B * square))
        half = 0.5 * up
        hid_ref[here, cols] = (half + half * bent).astype(BF)
        slope_ref[:, cols] = 0.5 + 0.5 * bent + half * (1.0 - bent * bent) * (GELU_A + 3 * GELU_B * square)
    pre = normed + nn(hid_ref[here, :], wdown_ref[...]) + vec_ref[ROW + 8 : ROW + 9, :]
    unit3, rstd3 = norm(pre)
    out_ref[0] = (unit3 * vec_ref[2:3, :] + vec_ref[ROW + 9 : ROW + 10, :]).astype(BF)
    cot = cot_ref[0].astype(F32)
    gp3 = norm_back(cot, unit3, rstd3, vec_ref[2:3, :])
    low3 = gp3.astype(BF)
    low3_ref[here, :] = low3
    vec_out[2:3, :] += col_sum(cot * unit3)
    vec_out[ROW + 8 : ROW + 9, :] += col_sum(gp3)
    vec_out[ROW + 9 : ROW + 10, :] += col_sum(cot)
    for p in range(panels):
        cols = slice(p * 512, (p + 1) * 512)
        grad_up = nt(low3, wdown_ref[cols, :]) * slope_ref[:, cols]
        low_up_ref[here, cols] = grad_up.astype(BF)
        vec_out[UP + p : UP + p + 1, :] += col_sum(grad_up)
    grad = gp3 + nt(low_up_ref[here, :], wup_ref[...])
    gp2 = norm_back(grad, unit2, rstd2_ref[0][:, :1], vec_ref[1:2, :])
    gp2_ref[0] = gp2
    low2 = gp2.astype(BF)
    low2_ref[here, :] = low2
    co = co_ref[0]
    co_all_ref[here, :] = co
    dco = nt(low2, wco_ref[...]).astype(BF)
    dco_ref[0] = dco
    dcross_ref[0] = head_products(dco, co)
    vec_out[1:2, :] += col_sum(grad * unit2)
    vec_out[ROW + 6 : ROW + 7, :] += col_sum(gp2)
    vec_out[ROW + 7 : ROW + 8, :] += col_sum(grad)

    @pl.when(row == pl.num_programs(0) - 1)
    def _():
        down, part = hidden_width // blocks, width // blocks
        for p in range(panels):
            cols = slice(p * 512, (p + 1) * 512)
            put(buffer, None, 0, tn(hid_ref[:, cols], low3_ref[...]), p * 512, down)
            put(buffer, None, down + p * part, tn(normed_ref[...], low_up_ref[:, cols]), 0, part)
        put(buffer, None, down + panels * part, tn(co_all_ref[...], low2_ref[...]), 0, part)
        send_halves(info, buffer, (keep_ref, send_ref), sems)


def feed(segs, info, unit2, rstd2, cot, co, wup, wdown, wco, up_rows, vec, blocks):
    rows, block, width = unit2.shape
    hidden = wup.shape[1]
    tokens = rows * block
    buffer_shape = (blocks, (2 * hidden + width) // blocks, width)
    shapes, specs, more = sum_specs(buffer_shape, True)
    out_shape = [
        shape_of(unit2.shape, BF),
        shape_of(unit2.shape, F32),
        shape_of(unit2.shape, BF),
        shape_of((rows, HEADS, block), F32),
        shape_of((VROWS, width), F32),
    ]
    out_specs = [arg_spec(unit2.shape)] + [row_spec(s.shape) for s in out_shape[1:4]] + [whole((VROWS, width))]
    return call(
        functools.partial(feed_kernel, blocks), "feed", 22, (rows,),
        [row_spec(unit2.shape), row_spec(rstd2.shape), arg_spec(cot.shape), row_spec(co.shape)]
        + [whole(a.shape) for a in (wup, wdown, wco, up_rows, vec)],
        out_specs + specs,
        out_shape + shapes,
        [
            pltpu.VMEM((tokens, hidden), BF),
            pltpu.VMEM((block, hidden), F32),
            pltpu.VMEM((tokens, hidden), BF),
            pltpu.VMEM((tokens, width), BF),
            pltpu.VMEM((tokens, width), BF),
            pltpu.VMEM((tokens, width), BF),
            pltpu.VMEM((tokens, width), BF),
        ]
        + more,
    )(segs, info, unit2, rstd2, cot, co, wup, wdown, wco, up_rows, vec)


def bits(size):
    return size.bit_length() - 1


def all_pairs(mask):
    return [(i, i ^ mask) for i in range(lax.axis_size("dp") * lax.axis_size("blk"))]


def swap(values, mask):
    return lax.ppermute(values, ("dp", "blk"), all_pairs(mask))


def place():
    return lax.axis_index("dp") * lax.axis_size("blk") + lax.axis_index("blk")


def by_place(parts, at, count):
    for bit in range(count):
        side = ((at >> bit) & 1) == 1
        parts = [jnp.where(side, parts[j ^ (1 << bit)], parts[j]) for j in range(len(parts))]
    return parts


class Sum:
    def __init__(self, keep, send):
        self.values = [keep, send]
        self.near = bits(lax.axis_size("blk"))
        self.far = bits(lax.axis_size("dp")) - 2
        self.steps = [self.core, self.near_scatter, self.far_scatter, self.far_gather, self.near_gather, self.core_gather]

    def step(self):
        if self.steps:
            self.values = self.steps.pop(0)(*self.values)

    def core(self, keep, send):
        return [(keep.astype(F32) + swap(send, 1 << self.near).astype(F32)).astype(BF)]

    def near_scatter(self, now):
        blocks = now.shape[0]
        cut = now.reshape(blocks, 2, now.shape[1] // 2, now.shape[2])
        mine, side = lax.axis_index("blk"), (lax.axis_index("dp") >> 1) & 1

        def piece(b, s):
            return lax.dynamic_slice(cut, (mine ^ b, side ^ s, 0, 0), (1, 1, *cut.shape[2:]))[0, 0]

        total = piece(0, 0).astype(F32)
        for s in range(2):
            for b in range(blocks):
                if s or b:
                    total = total + swap(piece(b, s), (2 * s << self.near) | b).astype(F32)
        return [total.astype(BF)]

    def far_scatter(self, now):
        at = lax.axis_index("dp") >> 2
        cut = now.reshape(1 << self.far, -1, now.shape[1])
        total = lax.dynamic_index_in_dim(cut, at, 0, False).astype(F32)
        for k in range(1, 1 << self.far):
            piece = lax.dynamic_index_in_dim(cut, at ^ k, 0, False)
            total = total + swap(piece, (k << 2) << self.near).astype(F32)
        return [total.astype(BF)]

    def far_gather(self, now):
        at = lax.axis_index("dp") >> 2
        parts = [now] + [swap(now, (k << 2) << self.near) for k in range(1, 1 << self.far)]
        return [jnp.concatenate(by_place(parts, at, self.far), 0)]

    def near_gather(self, now):
        at = (lax.axis_index("dp") >> 1) & 1
        return [jnp.concatenate(by_place([now, swap(now, 2 << self.near)], at, 1), 0)]

    def core_gather(self, now):
        at = lax.axis_index("dp") & 1
        return [jnp.concatenate(by_place([now, swap(now, 1 << self.near)], at, 1), 0)]


def advance(sums, anchor):
    for s in sums:
        s.step()
    flat, anchor = lax.optimization_barrier(([s.values for s in sums], anchor))
    for s, values in zip(sums, flat):
        s.values = values
    return anchor


def from_next(values, step):
    size = lax.axis_size("blk")
    return lax.ppermute(values, "blk", [((i + step) % size, i) for i in range(size)])


def to_next(values, step):
    size = lax.axis_size("blk")
    return lax.ppermute(values, "blk", [(i, (i + step) % size) for i in range(size)])


def unpanel(part, columns):
    panels = columns // 512
    rows = part.shape[0] // panels
    return jnp.concatenate([part[p * rows : (p + 1) * rows] for p in range(panels)], 1).astype(F32)


def body(tokens, memory, segments, w_qkv, w_self_out, w_cross_q, w_cross_kv, w_cross_out, w_up, w_down, norm_gains, shifts, up_shift, cotangent):
    rows, block, width = tokens.shape
    mem_block = memory.shape[1]
    blocks = lax.axis_size("blk")
    mine = lax.axis_index("blk")
    seq_len = segments.shape[1]
    mem_len = mem_block * blocks
    hidden = w_up.shape[1]
    far = range(1, blocks)

    pick = rows == 2
    if pick:
        single = (segments[0, -1] != 0).astype(jnp.int32)
        order = jnp.stack([1 - single, single])
        edges = np.arange(1, blocks) * block
        crosses = jnp.any((segments[:, edges - 1] == segments[:, edges]) & (jnp.arange(2) != single)[:, None])
    else:
        order, crosses = jnp.arange(rows), jnp.array(True)
    head = jnp.stack([mine, lax.axis_index("dp") & 1, crosses.astype(jnp.int32)])
    info = jnp.concatenate([head, order]).astype(jnp.int32)

    def fetch(arrays):
        if not pick:
            return [[[from_next(a, k)] for k in far] for a in arrays]
        ones = [[from_next(lax.dynamic_index_in_dim(a, single, 0, True), k) for k in far] for a in arrays]
        others = [lax.dynamic_index_in_dim(a, 1 - single, 0, True) for a in arrays]
        others = lax.cond(
            crosses,
            lambda vs: [[from_next(v, k) for k in far] for v in vs],
            lambda vs: [[v for _ in far] for v in vs],
            others,
        )
        return [[[o, g] for o, g in zip(*pair)] for pair in zip(others, ones)]

    far_toks, far_mems = fetch([tokens, memory])

    vec = jnp.concatenate([norm_gains.T, shifts.T, jnp.zeros((3, width), F32)], 0)
    up_rows = up_shift.reshape(-1, 512)
    seg_rows = segments.astype(F32)[:, None, :]
    mem_seg = seg_rows[:, :, np.arange(mem_len) * seq_len // mem_len] if mem_len != seq_len else seg_rows

    q, k, v, kt, vt, ck, cv, ckt, cvt = project(segments, info, tokens, memory, w_qkv, w_cross_kv, vec)
    att, lse1, unit1, rstd1, cq, *keys = attend_forward(
        True, segments, info, q, seg_rows, seg_rows, tokens, w_qkv, w_self_out, w_cross_q, vec, k, vt, far_toks
    )
    k1, v1, kt1 = [[own] + keys[at::4] for at, own in enumerate((k, v, kt))]
    co, lse2, unit2, rstd2, *keys = attend_forward(
        False, segments, info, cq, seg_rows, mem_seg, unit1, w_cross_kv, w_cross_out, w_cross_q, vec, ck, cvt, far_mems
    )
    k2, v2, kt2 = [[own] + keys[at::4] for at, own in enumerate((ck, cv, ckt))]
    out, gp2, dco, dd2, vectors, keep, send = feed(
        segments, info, unit2, rstd2, cotangent, co, w_up, w_down, w_cross_out, up_rows, vec, blocks
    )
    sums = [Sum(keep, send)]

    def far_of(found, r):
        return [f[r] if len(f) > 1 else f[0] for f in found]

    def give(found):
        if not pick:
            return [[to_next(o, k) for k, o in zip(far, others[1:])] for others in found]
        others, ones = found
        got = [to_next(o, k) for k, o in zip(far, ones[1:])]
        more = lax.cond(
            crosses,
            lambda vs: [to_next(o, k) for k, o in zip(far, vs)],
            lambda vs: list(vs),
            list(others[1:]),
        )
        return [more, got]

    def total(found, got):
        sums = []
        for r, (own, more) in enumerate(zip(found, got)):
            total = own[0]
            for a in more:
                a = a.astype(F32)
                total = total + (jnp.where(crosses, a, 0.0) if pick and r == 0 else a)
            sums.append(total)
        if not pick:
            return jnp.concatenate(sums, 0)
        return jnp.where((jnp.arange(2) == single)[:, None, None], sums[1], sums[0])

    earlier, rows_gp1, dmem = None, [], []
    for r in range(rows):
        last = r == rows - 1
        gp1, datt, dd1, *rest = attend_backward(
            False, r, last, 24 if last else 14, segments, info, cq, seg_rows, mem_seg, dco, lse2, dd2, vec, vectors,
            k2, kt2, v2, [memory] + far_of(far_mems, r), w_cross_kv,
            [gp2, unit1, rstd1, att, w_cross_q, w_self_out], earlier,
        )
        dmem.append(rest[:blocks])
        vectors, earlier = rest[blocks], rest[-1]
        rows_gp1.append((gp1, datt, dd1))
        vectors = advance(sums, vectors)
    sums.append(Sum(*rest[-2:]))
    got_mem = give(dmem)
    earlier, dkv = None, []
    for r in range(rows):
        last = r == rows - 1
        _, datt, dd1 = rows_gp1[r]
        rest = attend_backward(
            True, r, last, 14 if last else 11, segments, info, q, seg_rows, seg_rows, datt, lse1, dd1, vec, vectors,
            k1, kt1, v1, [tokens] + far_of(far_toks, r), None, [], earlier,
        )
        dkv.append(rest[: blocks + 1])
        vectors, earlier = rest[blocks + 1], rest[-1]
        if not last:
            vectors, got_mem = advance(sums, (vectors, got_mem))
    dkv = advance(sums, dkv)
    sums.append(Sum(*rest[-2:]))
    dtok = tokens_back(segments, info, dkv, [g[0] for g in rows_gp1], w_qkv)
    dtok = advance(sums, dtok)
    got_tok = give(dtok)
    while any(s.steps for s in sums):
        got_tok = advance(sums, got_tok)
    grad_memory = total(dmem, got_mem)
    grad_tokens = total(dtok, got_tok)

    part, hidden_part = width // blocks, hidden // blocks
    feed_sum, other_sum, qkv_sum = [s.values[0] for s in sums]
    vectors = qkv_sum[3 * part * (width // 512) :].astype(F32)
    up_at = hidden_part + (hidden // 512) * part
    grad_up_shift = vectors[UP : UP + max(1, hidden_part // 512), : min(512, hidden_part)].reshape(-1)
    return (
        out,
        grad_tokens,
        grad_memory,
        unpanel(qkv_sum[: 3 * part * (width // 512)], 3 * width),
        other_sum[part : 2 * part].astype(F32),
        other_sum[:part].astype(F32),
        unpanel(other_sum[2 * part :], 2 * width),
        feed_sum[up_at:].astype(F32),
        unpanel(feed_sum[hidden_part:up_at], hidden),
        feed_sum[:hidden_part].astype(F32),
        vectors[:ROW, :part].T,
        vectors[ROW:UP, :part].T,
        grad_up_shift,
    )


def solution(mesh):
    split = P("dp", "blk", None)
    in_specs = (split, split, P("dp", None)) + (P(),) * 10 + (split,)
    out_specs = (split,) * 3 + (P("blk", None),) * 9 + (P("blk"),)
    return jax.shard_map(body, mesh=mesh, in_specs=in_specs, out_specs=out_specs, check_vma=False)
```

```python
import functools

import jax
import jax.numpy as jnp
import numpy as np
from jax import lax
from jax.experimental import pallas as pl
from jax.experimental.pallas import tpu as pltpu
from jax.sharding import PartitionSpec as P

HEADS = 8
NEG = -1e30
F32 = jnp.float32
BF = jnp.bfloat16
GELU_A = 0.7978845608028654
GELU_B = 0.7978845608028654 * 0.044715
ROW = 3
UP = 13
VROWS = 24
VECTOR_ROWS = 128


def nn(a, b):
    return jnp.dot(a, b, preferred_element_type=F32)


def nt(a, b):
    return lax.dot_general(a, b, (((1,), (1,)), ((), ())), preferred_element_type=F32)


def tn(a, b):
    return lax.dot_general(a, b, (((0,), (0,)), ((), ())), preferred_element_type=F32)


def norm(values):
    center = values - jnp.mean(values, -1, keepdims=True)
    rstd = lax.rsqrt(jnp.mean(center * center, -1, keepdims=True) + 1e-05)
    return center * rstd, rstd


def norm_back(grad, unit, rstd, gain):
    scaled = grad * gain
    return (
        scaled
        - jnp.mean(scaled, -1, keepdims=True)
        - unit * jnp.mean(scaled * unit, -1, keepdims=True)
    ) * rstd


def col_sum(values):
    return jnp.sum(values, 0, keepdims=True)


def whole(shape):
    zeros = (0,) * len(shape)
    return pl.BlockSpec(shape, lambda *_: zeros, pipeline_mode=pl.Buffered(1))


MIB, SELF_MIB = 54, 46


def cost(us):
    return pl.CostEstimate(flops=int(us * 1.1e9), bytes_accessed=0, transcendentals=0)


def shape_of(shape, kind):
    return jax.ShapeDtypeStruct(shape, kind)


PLACE, SIDE, CROSSES, ORDER = 0, 1, 2, 3


def row_spec(shape, row=None):
    block = (1, *shape[1:])
    rest = (0,) * (len(shape) - 1)
    if row is None:
        return pl.BlockSpec(block, lambda r, *_: (r, *rest))
    return pl.BlockSpec(block, lambda *_: (row, *rest))


def arg_spec(shape, row=None):
    block = (1, *shape[1:])
    rest = (0,) * (len(shape) - 1)
    if row is None:
        return pl.BlockSpec(block, lambda r, segs, info: (info[ORDER + r], *rest))
    return pl.BlockSpec(block, lambda r, segs, info: (info[ORDER + row], *rest))


def call(kernel, name, us, grid, in_specs, out_specs, out_shape, scratch, mib=60):
    return pl.pallas_call(
        kernel,
        grid_spec=pltpu.PrefetchScalarGridSpec(
            num_scalar_prefetch=2, grid=grid, in_specs=in_specs, out_specs=out_specs, scratch_shapes=scratch
        ),
        out_shape=out_shape,
        compiler_params=pltpu.CompilerParams(vmem_limit_bytes=mib * 1024 * 1024),
        cost_estimate=pl.CostEstimate(flops=int(us * 1.1e9), bytes_accessed=0, transcendentals=0),
        name=name,
    )


class Fetch:
    def __init__(self, source, ref, sem, index, need=None):
        if index is not None:
            source = source.at[pl.ds(index, 1)]
        self.copy, self.ref, self.need = pltpu.make_async_copy(source, ref, sem), ref, need

    def start(self):
        if self.need is None:
            self.copy.start()
        else:
            pl.when(self.need)(self.copy.start)

    def wait(self):
        if self.need is None:
            self.copy.wait()
        else:
            pl.when(self.need)(self.copy.wait)
        return self.ref


def put_keys(found, vec_ref, shift_v, k_ref, v_ref, kt_ref, vt_ref):
    width = found.shape[1] // 2
    k = found[:, :width]
    v = found[:, width:] + vec_ref[ROW + shift_v : ROW + shift_v + 1, :]
    k_ref[0] = k.astype(BF)
    v_ref[0] = v.astype(BF)
    kt_ref[0] = k.T.astype(BF)
    vt_ref[0] = v.T.astype(BF)


def scaled(queries):
    low = queries.astype(BF).astype(F32)
    return (low * (queries.shape[1] // HEADS) ** -0.5).astype(BF)


def project_kernel(segs, info, tok_ref, mem_ref, wqkv_ref, wckv_ref, vec_ref, q_ref, k_ref, v_ref, kt_ref, vt_ref, ck_ref, cv_ref, ckt_ref, cvt_ref):
    width = tok_ref.shape[2]
    found = nn(tok_ref[0], wqkv_ref[...])
    q_ref[0] = scaled(found[:, :width] + vec_ref[ROW : ROW + 1, :])
    put_keys(found[:, width:], vec_ref, 1, k_ref, v_ref, kt_ref, vt_ref)
    put_keys(nn(mem_ref[0], wckv_ref[...]), vec_ref, 5, ck_ref, cv_ref, ckt_ref, cvt_ref)


def project(segs, info, tokens, memory, wqkv, wckv, vec):
    rows, block, width = tokens.shape
    mem_block = memory.shape[1]
    shapes = [(rows, block, width)] * 3 + [(rows, width, block)] * 2
    shapes += [(rows, mem_block, width)] * 2 + [(rows, width, mem_block)] * 2
    return call(
        project_kernel, "project", 7, (rows,),
        [arg_spec(tokens.shape), arg_spec(memory.shape), whole(wqkv.shape), whole(wckv.shape), whole(vec.shape)],
        [row_spec(s) for s in shapes],
        [shape_of(s, BF) for s in shapes],
        [],
    )(segs, info, tokens, memory, wqkv, wckv, vec)


class Dims:
    def __init__(self, rows, block, key_block, blocks, seq_len, width):
        self.rows, self.block, self.key_block, self.blocks, self.seq_len = rows, block, key_block, blocks, seq_len
        self.width = width
        self.tile = min(256, block)
        self.step = min(256, key_block)


def split_pairs(ref, qoff, dims, keep_ref):
    lane = lax.broadcasted_iota(jnp.int32, (1, 128), 1)
    for h in range(HEADS):
        side = (lane < 64) if h % 2 == 0 else (lane >= 64)
        pair = slice(h // 2 * 128, h // 2 * 128 + 128)
        keep_ref[h] = ref[0, pl.ds(qoff, dims.tile), pair] * side.astype(F32).astype(BF)


def over_tiles(causal, dims, row, segs, info, segq_ref, segk_ref, bias_ref, qin, body):
    tile, step_size = dims.tile, dims.step
    mine, at = info[PLACE], info[ORDER + row]
    qoff = pl.multiple_of(mine * dims.block + qin, tile)
    q_first, q_last = segs[at, qoff], segs[at, qoff + tile - 1]
    keys_all = dims.key_block * dims.blocks
    for source in range(dims.blocks):
        owner = lax.rem(mine + source, dims.blocks)

        def step(kt, carry, source=source, owner=owner):
            inner = pl.multiple_of(kt * step_size, step_size)
            koff = pl.multiple_of(owner * dims.key_block + inner, step_size)
            k_first = segs[at, koff * dims.seq_len // keys_all]
            k_last = segs[at, (koff + step_size - 1) * dims.seq_len // keys_all]
            need = (k_first <= q_last) & (k_last >= q_first)
            if causal:
                need = need & (koff < qoff + tile)

            @pl.when(need)
            def _():
                across = jnp.broadcast_to(segk_ref[0, :, pl.ds(koff, step_size)], (tile, step_size))
                allowed = across.T == segq_ref[0, :, pl.ds(qoff, tile)]
                if causal:
                    kpos = lax.broadcasted_iota(jnp.int32, (step_size, tile), 0) + koff
                    qpos = lax.broadcasted_iota(jnp.int32, (step_size, tile), 1) + qoff
                    allowed = allowed & (kpos <= qpos)
                bias_ref[...] = jnp.where(allowed, 0.0, NEG)
                body(source, inner)

            return carry

        lax.fori_loop(0, dims.key_block // step_size, step, 0)


def far_needed(causal, dims, info, row, source):
    need = info[CROSSES] == 1 if dims.rows == 2 and row == 0 else info[CROSSES] >= 0
    if causal:
        need = need & (lax.rem(info[PLACE] + source, dims.blocks) < info[PLACE])
    return need


def forward_scratch(dims):
    return [
        pltpu.VMEM((HEADS, dims.tile, 128), BF),
        pltpu.VMEM((dims.step, dims.tile), F32),
        pltpu.VMEM((HEADS, dims.tile), F32),
        pltpu.VMEM((HEADS, dims.tile), F32),
        pltpu.VMEM((dims.width, dims.tile), F32),
        pltpu.VMEM((HEADS, dims.step, dims.tile), F32),
        pltpu.VMEM((HEADS, dims.step, dims.tile), BF),
    ]


def forward_tiles(causal, dims, row, segs, info, q_ref, segq_ref, segk_ref, k_refs, vt_refs, att_ref, lse_ref, scratch):
    qm_ref, bias_ref, top_ref, total_ref, acc_ref, score_ref, raised_ref = scratch

    def query_tile(i, carry):
        qin = pl.multiple_of(i * dims.tile, dims.tile)
        queries = pl.ds(qin, dims.tile)
        split_pairs(q_ref, qin, dims, qm_ref)
        top_ref[...] = jnp.full_like(top_ref, NEG)
        total_ref[...] = jnp.zeros_like(total_ref)
        acc_ref[...] = jnp.zeros_like(acc_ref)

        def body(source, inner):
            here = pl.ds(inner, dims.step)
            old = top_ref[...]
            new, fade, more = [], [], []
            for h in range(HEADS):
                pair = slice(h // 2 * 128, h // 2 * 128 + 128)
                scores = nt(k_refs[source][0, here, pair], qm_ref[h]) + bias_ref[...]
                score_ref[h] = scores
                new.append(jnp.maximum(old[h : h + 1, :], jnp.max(scores, 0, keepdims=True)))
                fade.append(jnp.exp(old[h : h + 1, :] - new[h]))
            for h in range(HEADS):
                raised = jnp.exp(score_ref[h] - new[h])
                raised_ref[h] = raised.astype(BF)
                more.append(col_sum(raised))
            for h in range(HEADS):
                heads = slice(h * 64, h * 64 + 64)
                acc_ref[heads, :] = acc_ref[heads, :] * fade[h] + nn(vt_refs[source][0, heads, here], raised_ref[h])
            top_ref[...] = jnp.concatenate(new, 0)
            total_ref[...] = total_ref[...] * jnp.concatenate(fade, 0) + jnp.concatenate(more, 0)

        over_tiles(causal, dims, row, segs, info, segq_ref, segk_ref, bias_ref, qin, body)
        total = total_ref[...]
        lse_ref[0, :, queries] = top_ref[...] + jnp.log(total)
        inverse = 1.0 / total
        for h in range(HEADS):
            heads = slice(h * 64, h * 64 + 64)
            acc_ref[heads, :] = acc_ref[heads, :] * inverse[h : h + 1, :]
        att_ref[0, queries, :] = acc_ref[...].T.astype(BF)
        return carry

    lax.fori_loop(0, dims.block // dims.tile, query_tile, 0)


def forward_kernel(causal, dims, far_count, segs, info, q_ref, segq_ref, segk_ref, base_ref, w_kv_ref, w_out_ref, w_cq_ref, vec_ref, k_ref, vt_ref, *refs):
    far_refs, refs = refs[: far_count * (dims.blocks - 1)], refs[far_count * (dims.blocks - 1) :]
    outs = 5 if causal else 4
    att_ref, lse_ref, unit_ref, rstd_ref = refs[:4]
    far_keys = refs[outs : outs + 4 * (dims.blocks - 1)]
    scratch = refs[outs + 4 * (dims.blocks - 1) :]
    row = pl.program_id(0)
    width = dims.width
    k_refs, vt_refs = [k_ref], [vt_ref]
    at = width if causal else 0
    for source in range(1, dims.blocks):
        keys = far_keys[4 * source - 4 : 4 * source]
        for which in range(far_count):
            ref = far_refs[far_count * (source - 1) + which]
            need = far_needed(causal, dims, info, which if far_count == 2 else 1, source)
            if far_count == 2:
                need = need & (row == which)

            @pl.when(need)
            def _(ref=ref, keys=keys):
                put_keys(nn(ref[0], w_kv_ref[:, at:]), vec_ref, 1 if causal else 5, *keys)

        k_refs.append(keys[0])
        vt_refs.append(keys[3])
    forward_tiles(causal, dims, row, segs, info, q_ref, segq_ref, segk_ref, k_refs, vt_refs, att_ref, lse_ref, scratch)
    base = base_ref[0].astype(F32)
    if not causal:
        base = base * vec_ref[0:1, :] + vec_ref[ROW + 3 : ROW + 4, :]
    shift = ROW + 2 if causal else ROW + 6
    unit, rstd = norm(base + nn(att_ref[0], w_out_ref[...]) + vec_ref[shift : shift + 1, :])
    unit_ref[0] = unit
    rstd_ref[0] = jnp.broadcast_to(rstd, rstd_ref.shape[1:])
    if causal:
        normed = (unit * vec_ref[0:1, :] + vec_ref[ROW + 3 : ROW + 4, :]).astype(BF)
        refs[4][0] = scaled(nn(normed, w_cq_ref[...]) + vec_ref[ROW + 4 : ROW + 5, :])


def attend_forward(causal, segs, info, q, segq, segk, base, w_kv, w_out, w_cq, vec, key, value_t, far):
    rows, block, width = q.shape
    key_block = key.shape[1]
    dims = Dims(rows, block, key_block, len(far) + 1, segs.shape[1], width)
    far_count = len(far[0]) if far else 1
    far_arrays = [a for arrays in far for a in arrays]
    base_spec = arg_spec(base.shape) if causal else row_spec(base.shape)
    far_specs = [row_spec(a.shape) if far_count == 1 else row_spec(a.shape, 0) for a in far_arrays]
    out_shape = [
        shape_of(q.shape, BF),
        shape_of((rows, HEADS, block), F32),
        shape_of(q.shape, F32),
        shape_of((rows, block, 128), F32),
    ] + [shape_of(q.shape, BF)] * causal
    keys = [shape_of((rows, key_block, width), BF)] * 2 + [shape_of((rows, width, key_block), BF)] * 2
    out_shape += keys * len(far)
    return call(
        functools.partial(forward_kernel, causal, dims, far_count),
        "attend_self" if causal else "attend_cross",
        14, (rows,),
        [row_spec(q.shape), arg_spec(segq.shape), arg_spec(segk.shape), base_spec]
        + [whole(w.shape) for w in (w_kv, w_out, w_cq, vec)]
        + [row_spec(key.shape), row_spec(value_t.shape)]
        + far_specs,
        [row_spec(s.shape) for s in out_shape],
        out_shape,
        forward_scratch(dims),
    )(segs, info, q, segq, segk, base, w_kv, w_out, w_cq, vec, key, value_t, *far_arrays)


def backward_scratch(dims):
    return [
        pltpu.VMEM((HEADS, dims.tile, 128), BF),
        pltpu.VMEM((HEADS, dims.tile, 128), BF),
        pltpu.VMEM((dims.step, dims.tile), F32),
        pltpu.VMEM((dims.width, dims.block), F32),
        pltpu.VMEM((dims.blocks, dims.key_block, dims.width), F32),
        pltpu.VMEM((dims.blocks, dims.key_block, dims.width), F32),
        pltpu.VMEM((HEADS, dims.step, dims.tile), F32),
        pltpu.VMEM((HEADS, dims.step, dims.tile), BF),
        pltpu.VMEM((HEADS, dims.step, dims.tile), BF),
    ]


def backward_tiles(causal, dims, row, segs, info, q_ref, do_ref, lse_ref, dd_ref, segq_ref, segk_ref, k_refs, kt_refs, v_refs, scratch):
    qm_ref, dm_ref, bias_ref, dq_ref, dk_ref, dv_ref, weight_ref, low_ref, ds_ref = scratch
    dk_ref[...] = jnp.zeros_like(dk_ref)
    dv_ref[...] = jnp.zeros_like(dv_ref)
    dq_ref[...] = jnp.zeros_like(dq_ref)

    def query_tile(i, carry):
        qin = pl.multiple_of(i * dims.tile, dims.tile)
        queries = pl.ds(qin, dims.tile)
        split_pairs(q_ref, qin, dims, qm_ref)
        split_pairs(do_ref, qin, dims, dm_ref)

        def body(source, inner):
            here = pl.ds(inner, dims.step)
            lse, dd = lse_ref[0, :, queries], dd_ref[0, :, queries]
            for h in range(HEADS):
                pair = slice(h // 2 * 128, h // 2 * 128 + 128)
                weights = jnp.exp(nt(k_refs[source][0, here, pair], qm_ref[h]) + bias_ref[...] - lse[h : h + 1, :])
                weight_ref[h] = weights
                low_ref[h] = weights.astype(BF)
            for h in range(HEADS):
                pair = slice(h // 2 * 128, h // 2 * 128 + 128)
                grads = nt(v_refs[source][0, here, pair], dm_ref[h])
                ds_ref[h] = (weight_ref[h] * (grads - dd[h : h + 1, :])).astype(BF)
            for h in range(0, HEADS, 2):
                pair = slice(h // 2 * 128, h // 2 * 128 + 128)
                dv_ref[source, here, pair] += nn(low_ref[h], dm_ref[h]) + nn(low_ref[h + 1], dm_ref[h + 1])
                dk_ref[source, here, pair] += nn(ds_ref[h], qm_ref[h]) + nn(ds_ref[h + 1], qm_ref[h + 1])
            for h in range(HEADS):
                heads = slice(h * 64, h * 64 + 64)
                dq_ref[heads, queries] += nn(kt_refs[source][0, heads, here], ds_ref[h])

        over_tiles(causal, dims, row, segs, info, segq_ref, segk_ref, bias_ref, qin, body)
        return carry

    lax.fori_loop(0, dims.block // dims.tile, query_tile, 0)
    return dq_ref[...].T * (dims.width // HEADS) ** -0.5


def head_products(a, b):
    turned = (a.astype(F32) * b.astype(F32)).T
    return jnp.concatenate([col_sum(turned[h * 64 : h * 64 + 64]) for h in range(HEADS)], 0)


def put(buffer, earlier, at, value, first, part):
    done = 0
    while done < value.shape[0]:
        b, inner = divmod(first + done, part)
        count = min(part - inner, value.shape[0] - done)
        rows = slice(at + inner, at + inner + count)
        piece = value[done : done + count]
        if earlier is not None:
            piece = piece + earlier[b, rows, :].astype(F32)
        buffer[b, rows, :] = piece.astype(BF)
        done += count


def send_halves(info, buffer, outs, sems):
    half = buffer.shape[1] // 2
    side = info[SIDE]
    copies = []
    for k, out in enumerate(outs):
        start = pl.multiple_of((side if k == 0 else 1 - side) * half, 16)
        copies.append(pltpu.make_async_copy(buffer.at[:, pl.ds(start, half), :], out, sems.at[k]))
    for c in copies:
        c.start()
    for c in copies:
        c.wait()


def sum_specs(buffer_shape, last):
    blocks, rows, lanes = buffer_shape
    if last:
        half = shape_of((blocks, rows // 2, lanes), BF)
        return [half] * 2, [pl.BlockSpec(memory_space=pl.ANY)] * 2, [pltpu.VMEM(buffer_shape, BF), pltpu.SemaphoreType.DMA((2,))]
    return [shape_of(buffer_shape, BF)], [whole(buffer_shape)], []


def backward_kernel(causal, dims, row, pickers, has_earlier, last, segs, info, *refs):
    take = iter(refs)

    def some(count):
        return [next(take) for _ in range(count)]

    blocks, width = dims.blocks, dims.width
    segq_ref, segk_ref, lse_ref, dd_ref, vec_ref, vec_in = some(6)
    sources = some(len(pickers))
    outs = some((0 if causal else 3) + blocks + (1 if causal else 0))
    vec_out = next(take)
    sum_outs = some(2 if last else 1)
    scratch = some(9)
    acc_ref, buffer, in_sems, out_sems, sum_sems = some(5)
    places = some(len(pickers))
    out_refs = some(len(outs))

    needs = [None] + [far_needed(causal, dims, info, row, source) for source in range(1, blocks)]
    fetches = []
    for k, (source, place, picker) in enumerate(zip(sources, places, pickers)):
        index, of_source = picker
        if index == "arg":
            index = info[ORDER + row]
        fetches.append(Fetch(source, place, in_sems.at[k], index, None if of_source is None else needs[of_source]))
    take = iter(fetches)
    q_get, do_get = some(2)
    own = some(3)
    others = [some(3) for _ in range(1, blocks)]
    x_gets = some(blocks)
    early = 5 + 3 * (blocks - 1)
    for f in fetches[:early]:
        f.start()
    if not causal:
        w_kv_get, unit1_get, rstd1_get, wcq_get, gp2_get, att_get, wso_get = some(7)
    earlier_get = next(take) if has_earlier else None

    leaving = []

    def leave(k):
        leaving.append(pltpu.make_async_copy(out_refs[k], outs[k], out_sems.at[k]))
        leaving[-1].start()

    vec_out[...] = vec_in[...]
    part = width // blocks
    dk_ref, dv_ref = scratch[4:6]
    q_ref, do_ref = q_get.wait(), do_get.wait()
    k_refs, v_refs, kt_refs = zip(*[[g.wait() for g in gets] for gets in (own, *others)])
    for f in fetches[early:]:
        f.start()
    dq = backward_tiles(causal, dims, row, segs, info, q_ref, do_ref, lse_ref, dd_ref, segq_ref, segk_ref, k_refs, kt_refs, v_refs, scratch)
    low_q = dq.astype(BF)
    x_refs = [g.wait() for g in x_gets]
    if causal:
        out_refs[blocks][0] = low_q
        leave(blocks)
        shift_v, first_dx, first = 1, 0, part
    else:
        shift_v, first_dx, first = 5, 3, 2 * part
        w_kv = w_kv_get.wait()

    for source in range(blocks):
        place = out_refs[first_dx + source]

        def back(source=source, place=place):
            x = x_refs[source][0]
            dv = dv_ref[source]
            low = jnp.concatenate([dk_ref[source].astype(BF), dv.astype(BF)], 1)
            vec_out[ROW + shift_v : ROW + shift_v + 1, :] += col_sum(dv)
            if causal:
                place[0] = low
            else:
                place[0] = nt(low, w_kv[...]).astype(place.dtype)
            more = tn(x, low)
            if source == 0:
                acc_ref[...] = more
            else:
                acc_ref[...] += more

        if source == 0:
            back()
        else:
            pl.when(needs[source])(back)

            @pl.when(jnp.logical_not(needs[source]))
            def _(place=place):
                place[...] = jnp.zeros_like(place)

        leave(first_dx + source)

    earlier = earlier_get.wait() if has_earlier else None
    for p in range(2 * width // 512):
        put(buffer, earlier, first + p * part, acc_ref[:, p * 512 : (p + 1) * 512], 0, part)
    if causal:
        vec_out[ROW : ROW + 1, :] += col_sum(dq)
        put(buffer, earlier, 0, tn(x_refs[0][0], low_q), 0, part)
    else:
        unit1 = unit1_get.wait()[0]
        rstd1 = rstd1_get.wait()[0]
        wcq, gp2 = wcq_get.wait(), gp2_get.wait()
        grad = gp2[0] + nt(low_q, wcq[...])
        gp1 = norm_back(grad, unit1, rstd1[:, :1], vec_ref[0:1, :])
        out_refs[0][0] = gp1
        leave(0)
        low_one = gp1.astype(BF)
        att, wso = att_get.wait()[0], wso_get.wait()
        put(buffer, earlier, part, tn(att, low_one), 0, part)
        normed = (unit1 * vec_ref[0:1, :] + vec_ref[ROW + 3 : ROW + 4, :]).astype(BF)
        put(buffer, earlier, 0, tn(normed, low_q), 0, part)
        if not last:
            leaving.append(pltpu.make_async_copy(buffer, sum_outs[0], sum_sems.at[0]))
            leaving[-1].start()
        datt = nt(low_one, wso[...]).astype(BF)
        out_refs[1][0] = datt
        leave(1)
        out_refs[2][0] = head_products(datt, att)
        leave(2)
        vec_out[0:1, :] += col_sum(grad * unit1)
        vec_out[ROW + 2 : ROW + 3, :] += col_sum(gp1)
        vec_out[ROW + 3 : ROW + 4, :] += col_sum(grad)
        vec_out[ROW + 4 : ROW + 5, :] += col_sum(dq)

    if causal and last:
        base = 3 * part * (width // 512)
        buffer[:, base:, :] = jnp.zeros((blocks, buffer.shape[1] - base, 512), BF)
        hidden_part = 4 * 512 // blocks
        for b in range(blocks):
            buffer[b, base : base + UP, :part] = vec_out[:UP, b * part : (b + 1) * part].astype(BF)
            for k in range(max(1, hidden_part // 512)):
                at = b * hidden_part + k * 512
                count = min(512, hidden_part)
                piece = vec_out[UP + at // 512 : UP + at // 512 + 1, at % 512 : at % 512 + count]
                buffer[b, base + UP + k : base + UP + k + 1, :count] = piece.astype(BF)
    if last:
        send_halves(info, buffer, sum_outs, sum_sems)
    elif causal:
        leaving.append(pltpu.make_async_copy(buffer, sum_outs[0], sum_sems.at[0]))
        leaving[-1].start()
    for c in leaving:
        c.wait()


def attend_backward(causal, row, last, us, segs, info, q, segq, segk, d_out, lse, dd, vec, vec_in, keys, keys_t, values, inputs, w_kv, extra, earlier):
    rows, block, width = q.shape
    blocks, key_block = len(keys), keys[0].shape[1]
    dims = Dims(rows, block, key_block, blocks, segs.shape[1], width)

    def at(a):
        return row if a.shape[0] == rows else 0

    def spec(a):
        return row_spec(a.shape, at(a))

    small = [segq, segk, lse, dd, vec, vec_in]
    small_specs = [arg_spec(segq.shape, row), arg_spec(segk.shape, row), spec(lse), spec(dd), whole(vec.shape), whole(vec_in.shape)]
    large = [(q, (row, None)), (d_out, (at(d_out), None))]
    for s in range(blocks):
        large += [(a[s], (row, None if s == 0 else s)) for a in (keys, values, keys_t)]
    large += [(a, ("arg" if s == 0 else at(a), None if s == 0 else s)) for s, a in enumerate(inputs)]
    if not causal:
        gp2, unit1, rstd1, att, wcq, wso = extra
        large += [(w_kv, (None, None)), (unit1, (row, None)), (rstd1, (row, None)), (wcq, (None, None))]
        large += [(gp2, (row, None)), (att, (row, None)), (wso, (None, None))]
    if earlier is not None:
        large.append((earlier, (None, None)))
    out_shape = []
    if not causal:
        out_shape += [shape_of((1, block, width), F32), shape_of((1, block, width), BF), shape_of((1, HEADS, block), F32)]
    if causal:
        out_shape += [shape_of((1, key_block, 2 * width), BF) for s in range(blocks)] + [shape_of((1, block, width), BF)]
    else:
        out_shape += [shape_of((1, key_block, width), F32 if s == 0 else BF) for s in range(blocks)]
    vec_shape = shape_of((VROWS, width), F32)
    buffer_rows = (3 if causal else 4) * width // blocks * (width // 512) + (VECTOR_ROWS if causal and last else 0)
    buffer_shape = (blocks, buffer_rows, 512)
    sum_shapes = [shape_of((blocks, buffer_rows // 2, 512), BF)] * 2 if last else [shape_of(buffer_shape, BF)]
    anywhere = pl.BlockSpec(memory_space=pl.ANY)
    places = [pltpu.VMEM(a.shape if p[0] is None else (1, *a.shape[1:]), a.dtype) for a, p in large]
    return call(
        functools.partial(backward_kernel, causal, dims, row, [p for _, p in large], earlier is not None, last),
        "attend_self_back" if causal else "attend_cross_back",
        us, (1,),
        small_specs + [anywhere] * len(large),
        [anywhere] * len(out_shape) + [whole(vec_shape.shape)] + [anywhere] * len(sum_shapes),
        out_shape + [vec_shape] + sum_shapes,
        backward_scratch(dims)
        + [
            pltpu.VMEM((width, 2 * width), F32),
            pltpu.VMEM(buffer_shape, BF),
            pltpu.SemaphoreType.DMA((len(large),)),
            pltpu.SemaphoreType.DMA((len(out_shape),)),
            pltpu.SemaphoreType.DMA((2,)),
        ]
        + places
        + [pltpu.VMEM(s.shape, s.dtype) for s in out_shape],
        SELF_MIB if causal else MIB,
    )(segs, info, *small, *[a for a, _ in large])


def tokens_back_kernel(rows, blocks, segs, info, *refs):
    take = iter(refs)
    per_row = [[next(take) for _ in range(2 + blocks)] for _ in range(rows)]
    w_ref = next(take)
    outs = [[next(take) for _ in range(blocks)] for _ in range(rows)]
    width = w_ref.shape[0]
    for (dq_ref, base_ref, *dkv_refs), out_refs in zip(per_row, outs):
        for source in range(blocks):
            grad = nt(dkv_refs[source][0], w_ref[:, width:])
            if source == 0:
                grad = grad + nt(dq_ref[0], w_ref[:, :width]) + base_ref[0]
            out_refs[source][0] = grad.astype(out_refs[source].dtype)


def tokens_back(segs, info, found, gp1, w):
    rows, blocks = len(found), len(found[0]) - 1
    args, out_shape = [], []
    for (*dkv, dq), base in zip(found, gp1):
        args += [dq, base, *dkv]
        out_shape += [shape_of(base.shape, F32 if s == 0 else BF) for s in range(blocks)]
    args.append(w)
    got = call(
        functools.partial(tokens_back_kernel, rows, blocks), "tokens_back", 8, (1,),
        [whole(a.shape) for a in args], [whole(s.shape) for s in out_shape], out_shape, [], SELF_MIB,
    )(segs, info, *args)
    return [got[r * blocks : (r + 1) * blocks] for r in range(rows)]


def feed_kernel(blocks, segs, info, unit2_ref, rstd2_ref, cot_ref, co_ref, wup_ref, wdown_ref, wco_ref, upshift_ref, vec_ref, *refs):
    out_ref, gp2_ref, dco_ref, dcross_ref, vec_out, keep_ref, send_ref = refs[:7]
    hid_ref, slope_ref, low_up_ref, normed_ref, low3_ref, co_all_ref, low2_ref, buffer, sems = refs[7:]
    width, hidden_width = wup_ref.shape
    panels = hidden_width // 512
    block = unit2_ref.shape[1]
    row = pl.program_id(0)
    here = pl.ds(pl.multiple_of(row * block, block), block)

    @pl.when(row == 0)
    def _():
        vec_out[...] = jnp.zeros_like(vec_out)

    unit2 = unit2_ref[0]
    normed = unit2 * vec_ref[1:2, :] + vec_ref[ROW + 7 : ROW + 8, :]
    normed_low = normed.astype(BF)
    normed_ref[here, :] = normed_low
    for p in range(panels):
        cols = slice(p * 512, (p + 1) * 512)
        up = nn(normed_low, wup_ref[:, cols]) + upshift_ref[p : p + 1, :]
        square = up * up
        bent = jnp.tanh(up * (GELU_A + GELU_B * square))
        half = 0.5 * up
        hid_ref[here, cols] = (half + half * bent).astype(BF)
        slope_ref[:, cols] = 0.5 + 0.5 * bent + half * (1.0 - bent * bent) * (GELU_A + 3 * GELU_B * square)
    pre = normed + nn(hid_ref[here, :], wdown_ref[...]) + vec_ref[ROW + 8 : ROW + 9, :]
    unit3, rstd3 = norm(pre)
    out_ref[0] = (unit3 * vec_ref[2:3, :] + vec_ref[ROW + 9 : ROW + 10, :]).astype(BF)
    cot = cot_ref[0].astype(F32)
    gp3 = norm_back(cot, unit3, rstd3, vec_ref[2:3, :])
    low3 = gp3.astype(BF)
    low3_ref[here, :] = low3
    vec_out[2:3, :] += col_sum(cot * unit3)
    vec_out[ROW + 8 : ROW + 9, :] += col_sum(gp3)
    vec_out[ROW + 9 : ROW + 10, :] += col_sum(cot)
    for p in range(panels):
        cols = slice(p * 512, (p + 1) * 512)
        grad_up = nt(low3, wdown_ref[cols, :]) * slope_ref[:, cols]
        low_up_ref[here, cols] = grad_up.astype(BF)
        vec_out[UP + p : UP + p + 1, :] += col_sum(grad_up)
    grad = gp3 + nt(low_up_ref[here, :], wup_ref[...])
    gp2 = norm_back(grad, unit2, rstd2_ref[0][:, :1], vec_ref[1:2, :])
    gp2_ref[0] = gp2
    low2 = gp2.astype(BF)
    low2_ref[here, :] = low2
    co = co_ref[0]
    co_all_ref[here, :] = co
    dco = nt(low2, wco_ref[...]).astype(BF)
    dco_ref[0] = dco
    dcross_ref[0] = head_products(dco, co)
    vec_out[1:2, :] += col_sum(grad * unit2)
    vec_out[ROW + 6 : ROW + 7, :] += col_sum(gp2)
    vec_out[ROW + 7 : ROW + 8, :] += col_sum(grad)

    @pl.when(row == pl.num_programs(0) - 1)
    def _():
        down, part = hidden_width // blocks, width // blocks
        for p in range(panels):
            cols = slice(p * 512, (p + 1) * 512)
            put(buffer, None, 0, tn(hid_ref[:, cols], low3_ref[...]), p * 512, down)
            put(buffer, None, down + p * part, tn(normed_ref[...], low_up_ref[:, cols]), 0, part)
        put(buffer, None, down + panels * part, tn(co_all_ref[...], low2_ref[...]), 0, part)
        send_halves(info, buffer, (keep_ref, send_ref), sems)


def feed(segs, info, unit2, rstd2, cot, co, wup, wdown, wco, up_rows, vec, blocks):
    rows, block, width = unit2.shape
    hidden = wup.shape[1]
    tokens = rows * block
    buffer_shape = (blocks, (2 * hidden + width) // blocks, width)
    shapes, specs, more = sum_specs(buffer_shape, True)
    out_shape = [
        shape_of(unit2.shape, BF),
        shape_of(unit2.shape, F32),
        shape_of(unit2.shape, BF),
        shape_of((rows, HEADS, block), F32),
        shape_of((VROWS, width), F32),
    ]
    out_specs = [arg_spec(unit2.shape)] + [row_spec(s.shape) for s in out_shape[1:4]] + [whole((VROWS, width))]
    return call(
        functools.partial(feed_kernel, blocks), "feed", 22, (rows,),
        [row_spec(unit2.shape), row_spec(rstd2.shape), arg_spec(cot.shape), row_spec(co.shape)]
        + [whole(a.shape) for a in (wup, wdown, wco, up_rows, vec)],
        out_specs + specs,
        out_shape + shapes,
        [
            pltpu.VMEM((tokens, hidden), BF),
            pltpu.VMEM((block, hidden), F32),
            pltpu.VMEM((tokens, hidden), BF),
            pltpu.VMEM((tokens, width), BF),
            pltpu.VMEM((tokens, width), BF),
            pltpu.VMEM((tokens, width), BF),
            pltpu.VMEM((tokens, width), BF),
        ]
        + more,
    )(segs, info, unit2, rstd2, cot, co, wup, wdown, wco, up_rows, vec)


def bits(size):
    return size.bit_length() - 1


def all_pairs(mask):
    return [(i, i ^ mask) for i in range(lax.axis_size("dp") * lax.axis_size("blk"))]


def swap(values, mask):
    return lax.ppermute(values, ("dp", "blk"), all_pairs(mask))


def place():
    return lax.axis_index("dp") * lax.axis_size("blk") + lax.axis_index("blk")


def by_place(parts, at, count):
    for bit in range(count):
        side = ((at >> bit) & 1) == 1
        parts = [jnp.where(side, parts[j ^ (1 << bit)], parts[j]) for j in range(len(parts))]
    return parts


class Sum:
    def __init__(self, keep, send):
        self.values = [keep, send]
        self.near = bits(lax.axis_size("blk"))
        self.far = bits(lax.axis_size("dp")) - 2
        self.steps = [self.core, self.near_scatter, self.far_scatter, self.far_gather, self.near_gather, self.core_gather]

    def step(self):
        if self.steps:
            self.values = self.steps.pop(0)(*self.values)

    def core(self, keep, send):
        return [(keep.astype(F32) + swap(send, 1 << self.near).astype(F32)).astype(BF)]

    def near_scatter(self, now):
        blocks = now.shape[0]
        cut = now.reshape(blocks, 2, now.shape[1] // 2, now.shape[2])
        mine, side = lax.axis_index("blk"), (lax.axis_index("dp") >> 1) & 1

        def piece(b, s):
            return lax.dynamic_slice(cut, (mine ^ b, side ^ s, 0, 0), (1, 1, *cut.shape[2:]))[0, 0]

        total = piece(0, 0).astype(F32)
        for s in range(2):
            for b in range(blocks):
                if s or b:
                    total = total + swap(piece(b, s), (2 * s << self.near) | b).astype(F32)
        return [total.astype(BF)]

    def far_scatter(self, now):
        at = lax.axis_index("dp") >> 2
        cut = now.reshape(1 << self.far, -1, now.shape[1])
        total = lax.dynamic_index_in_dim(cut, at, 0, False).astype(F32)
        for k in range(1, 1 << self.far):
            piece = lax.dynamic_index_in_dim(cut, at ^ k, 0, False)
            total = total + swap(piece, (k << 2) << self.near).astype(F32)
        return [total.astype(BF)]

    def far_gather(self, now):
        at = lax.axis_index("dp") >> 2
        parts = [now] + [swap(now, (k << 2) << self.near) for k in range(1, 1 << self.far)]
        return [jnp.concatenate(by_place(parts, at, self.far), 0)]

    def near_gather(self, now):
        at = (lax.axis_index("dp") >> 1) & 1
        return [jnp.concatenate(by_place([now, swap(now, 2 << self.near)], at, 1), 0)]

    def core_gather(self, now):
        at = lax.axis_index("dp") & 1
        return [jnp.concatenate(by_place([now, swap(now, 1 << self.near)], at, 1), 0)]


def advance(sums, anchor):
    for s in sums:
        s.step()
    flat, anchor = lax.optimization_barrier(([s.values for s in sums], anchor))
    for s, values in zip(sums, flat):
        s.values = values
    return anchor


def from_next(values, step):
    size = lax.axis_size("blk")
    return lax.ppermute(values, "blk", [((i + step) % size, i) for i in range(size)])


def to_next(values, step):
    size = lax.axis_size("blk")
    return lax.ppermute(values, "blk", [(i, (i + step) % size) for i in range(size)])


def unpanel(part, columns):
    panels = columns // 512
    rows = part.shape[0] // panels
    return jnp.concatenate([part[p * rows : (p + 1) * rows] for p in range(panels)], 1).astype(F32)


def body(tokens, memory, segments, w_qkv, w_self_out, w_cross_q, w_cross_kv, w_cross_out, w_up, w_down, norm_gains, shifts, up_shift, cotangent):
    rows, block, width = tokens.shape
    mem_block = memory.shape[1]
    blocks = lax.axis_size("blk")
    mine = lax.axis_index("blk")
    seq_len = segments.shape[1]
    mem_len = mem_block * blocks
    hidden = w_up.shape[1]
    far = range(1, blocks)

    pick = rows == 2
    if pick:
        single = (segments[0, -1] != 0).astype(jnp.int32)
        order = jnp.stack([1 - single, single])
        edges = np.arange(1, blocks) * block
        crosses = jnp.any((segments[:, edges - 1] == segments[:, edges]) & (jnp.arange(2) != single)[:, None])
    else:
        order, crosses = jnp.arange(rows), jnp.array(True)
    head = jnp.stack([mine, lax.axis_index("dp") & 1, crosses.astype(jnp.int32)])
    info = jnp.concatenate([head, order]).astype(jnp.int32)

    def fetch(arrays):
        if not pick:
            return [[[from_next(a, k)] for k in far] for a in arrays]
        ones = [[from_next(lax.dynamic_index_in_dim(a, single, 0, True), k) for k in far] for a in arrays]
        others = [lax.dynamic_index_in_dim(a, 1 - single, 0, True) for a in arrays]
        others = lax.cond(
            crosses,
            lambda vs: [[from_next(v, k) for k in far] for v in vs],
            lambda vs: [[v for _ in far] for v in vs],
            others,
        )
        return [[[o, g] for o, g in zip(*pair)] for pair in zip(others, ones)]

    far_toks, far_mems = fetch([tokens, memory])

    vec = jnp.concatenate([norm_gains.T, shifts.T, jnp.zeros((3, width), F32)], 0)
    up_rows = up_shift.reshape(-1, 512)
    seg_rows = segments.astype(F32)[:, None, :]
    mem_seg = seg_rows[:, :, np.arange(mem_len) * seq_len // mem_len] if mem_len != seq_len else seg_rows

    q, k, v, kt, vt, ck, cv, ckt, cvt = project(segments, info, tokens, memory, w_qkv, w_cross_kv, vec)
    att, lse1, unit1, rstd1, cq, *keys = attend_forward(
        True, segments, info, q, seg_rows, seg_rows, tokens, w_qkv, w_self_out, w_cross_q, vec, k, vt, far_toks
    )
    k1, v1, kt1 = [[own] + keys[at::4] for at, own in enumerate((k, v, kt))]
    co, lse2, unit2, rstd2, *keys = attend_forward(
        False, segments, info, cq, seg_rows, mem_seg, unit1, w_cross_kv, w_cross_out, w_cross_q, vec, ck, cvt, far_mems
    )
    k2, v2, kt2 = [[own] + keys[at::4] for at, own in enumerate((ck, cv, ckt))]
    out, gp2, dco, dd2, vectors, keep, send = feed(
        segments, info, unit2, rstd2, cotangent, co, w_up, w_down, w_cross_out, up_rows, vec, blocks
    )
    sums = [Sum(keep, send)]

    def far_of(found, r):
        return [f[r] if len(f) > 1 else f[0] for f in found]

    def give(found):
        if not pick:
            return [[to_next(o, k) for k, o in zip(far, others[1:])] for others in found]
        others, ones = found
        got = [to_next(o, k) for k, o in zip(far, ones[1:])]
        more = lax.cond(
            crosses,
            lambda vs: [to_next(o, k) for k, o in zip(far, vs)],
            lambda vs: list(vs),
            list(others[1:]),
        )
        return [more, got]

    def total(found, got):
        sums = []
        for r, (own, more) in enumerate(zip(found, got)):
            total = own[0]
            for a in more:
                a = a.astype(F32)
                total = total + (jnp.where(crosses, a, 0.0) if pick and r == 0 else a)
            sums.append(total)
        if not pick:
            return jnp.concatenate(sums, 0)
        return jnp.where((jnp.arange(2) == single)[:, None, None], sums[1], sums[0])

    earlier, rows_gp1, dmem = None, [], []
    for r in range(rows):
        last = r == rows - 1
        gp1, datt, dd1, *rest = attend_backward(
            False, r, last, 24 if last else 14, segments, info, cq, seg_rows, mem_seg, dco, lse2, dd2, vec, vectors,
            k2, kt2, v2, [memory] + far_of(far_mems, r), w_cross_kv,
            [gp2, unit1, rstd1, att, w_cross_q, w_self_out], earlier,
        )
        dmem.append(rest[:blocks])
        vectors, earlier = rest[blocks], rest[-1]
        rows_gp1.append((gp1, datt, dd1))
        vectors = advance(sums, vectors)
    sums.append(Sum(*rest[-2:]))
    got_mem = give(dmem)
    earlier, dkv = None, []
    for r in range(rows):
        last = r == rows - 1
        _, datt, dd1 = rows_gp1[r]
        rest = attend_backward(
            True, r, last, 14 if last else 11, segments, info, q, seg_rows, seg_rows, datt, lse1, dd1, vec, vectors,
            k1, kt1, v1, [tokens] + far_of(far_toks, r), None, [], earlier,
        )
        dkv.append(rest[: blocks + 1])
        vectors, earlier = rest[blocks + 1], rest[-1]
        if not last:
            vectors, got_mem = advance(sums, (vectors, got_mem))
    dkv = advance(sums, dkv)
    sums.append(Sum(*rest[-2:]))
    dtok = tokens_back(segments, info, dkv, [g[0] for g in rows_gp1], w_qkv)
    first, second, third = sums
    dtok = advance(sums, dtok)

    part, hidden_part = width // blocks, hidden // blocks
    got_tok = give(dtok)
    dmem, got_mem = advance(sums, (dmem, got_mem))
    up_at = hidden_part + (hidden // 512) * part
    feed_sum = first.values[0]
    found = (
        total(dmem, got_mem),
        feed_sum[up_at:].astype(F32),
        unpanel(feed_sum[hidden_part:up_at], hidden),
        feed_sum[:hidden_part].astype(F32),
    )
    found, got_tok = advance([second, third], (found, got_tok))
    grad_memory, grad_cross_out, grad_up, grad_down = found
    grad_tokens = advance([second, third], total(dtok, got_tok))
    other_sum = second.values[0]
    found = (
        other_sum[part : 2 * part].astype(F32),
        other_sum[:part].astype(F32),
        unpanel(other_sum[2 * part :], 2 * width),
    )
    grad_self_out, grad_cross_q, grad_cross_kv = advance([third], found)
    while third.steps:
        third.step()
    qkv_sum = third.values[0]
    qkv_rows = 3 * part * (width // 512)
    vectors = qkv_sum[qkv_rows:].astype(F32)
    return (
        out,
        grad_tokens,
        grad_memory,
        unpanel(qkv_sum[:qkv_rows], 3 * width),
        grad_self_out,
        grad_cross_q,
        grad_cross_kv,
        grad_cross_out,
        grad_up,
        grad_down,
        vectors[:ROW, :part].T,
        vectors[ROW:UP, :part].T,
        vectors[UP : UP + max(1, hidden_part // 512), : min(512, hidden_part)].reshape(-1),
    )


def solution(mesh):
    split = P("dp", "blk", None)
    in_specs = (split, split, P("dp", None)) + (P(),) * 10 + (split,)
    out_specs = (split,) * 3 + (P("blk", None),) * 9 + (P("blk"),)
    return jax.shard_map(body, mesh=mesh, in_specs=in_specs, out_specs=out_specs, check_vma=False)
```

```python
import functools

import jax
import jax.numpy as jnp
import numpy as np
from jax import lax
from jax.experimental import pallas as pl
from jax.experimental.pallas import tpu as pltpu
from jax.sharding import PartitionSpec as P

HEADS = 8
NEG = -1e30
F32 = jnp.float32
BF = jnp.bfloat16
GELU_A = 0.7978845608028654
GELU_B = 0.7978845608028654 * 0.044715
ROW = 3
UP = 13
VROWS = 24
VECTOR_ROWS = 128


def nn(a, b):
    return jnp.dot(a, b, preferred_element_type=F32)


def nt(a, b):
    return lax.dot_general(a, b, (((1,), (1,)), ((), ())), preferred_element_type=F32)


def tn(a, b):
    return lax.dot_general(a, b, (((0,), (0,)), ((), ())), preferred_element_type=F32)


def norm(values):
    center = values - jnp.mean(values, -1, keepdims=True)
    rstd = lax.rsqrt(jnp.mean(center * center, -1, keepdims=True) + 1e-05)
    return center * rstd, rstd


def norm_back(grad, unit, rstd, gain):
    scaled = grad * gain
    return (
        scaled
        - jnp.mean(scaled, -1, keepdims=True)
        - unit * jnp.mean(scaled * unit, -1, keepdims=True)
    ) * rstd


def col_sum(values):
    return jnp.sum(values, 0, keepdims=True)


def whole(shape):
    zeros = (0,) * len(shape)
    return pl.BlockSpec(shape, lambda *_: zeros, pipeline_mode=pl.Buffered(1))


MIB, SELF_MIB = 54, 46


def cost(us):
    return pl.CostEstimate(flops=int(us * 1.1e9), bytes_accessed=0, transcendentals=0)


def shape_of(shape, kind):
    return jax.ShapeDtypeStruct(shape, kind)


PLACE, SIDE, CROSSES, ORDER = 0, 1, 2, 3


def row_spec(shape, row=None):
    block = (1, *shape[1:])
    rest = (0,) * (len(shape) - 1)
    if row is None:
        return pl.BlockSpec(block, lambda r, *_: (r, *rest))
    return pl.BlockSpec(block, lambda *_: (row, *rest))


def arg_spec(shape, row=None):
    block = (1, *shape[1:])
    rest = (0,) * (len(shape) - 1)
    if row is None:
        return pl.BlockSpec(block, lambda r, segs, info: (info[ORDER + r], *rest))
    return pl.BlockSpec(block, lambda r, segs, info: (info[ORDER + row], *rest))


def call(kernel, name, us, grid, in_specs, out_specs, out_shape, scratch, mib=60, aliases={}):
    return pl.pallas_call(
        kernel,
        grid_spec=pltpu.PrefetchScalarGridSpec(
            num_scalar_prefetch=2, grid=grid, in_specs=in_specs, out_specs=out_specs, scratch_shapes=scratch
        ),
        out_shape=out_shape,
        input_output_aliases=aliases,
        compiler_params=pltpu.CompilerParams(vmem_limit_bytes=mib * 1024 * 1024),
        cost_estimate=pl.CostEstimate(flops=int(us * 1.1e9), bytes_accessed=0, transcendentals=0),
        name=name,
    )


class Fetch:
    def __init__(self, source, ref, sem, index, need=None):
        if index is not None:
            source = source.at[pl.ds(index, 1)]
        self.copy, self.ref, self.need = pltpu.make_async_copy(source, ref, sem), ref, need

    def start(self):
        if self.need is None:
            self.copy.start()
        else:
            pl.when(self.need)(self.copy.start)

    def wait(self):
        if self.need is None:
            self.copy.wait()
        else:
            pl.when(self.need)(self.copy.wait)
        return self.ref


def put_keys(found, vec_ref, shift_v, k_ref, v_ref, kt_ref, vt_ref):
    width = found.shape[1] // 2
    k = found[:, :width]
    v = found[:, width:] + vec_ref[ROW + shift_v : ROW + shift_v + 1, :]
    k_ref[0] = k.astype(BF)
    v_ref[0] = v.astype(BF)
    kt_ref[0] = k.T.astype(BF)
    vt_ref[0] = v.T.astype(BF)


def scaled(queries):
    low = queries.astype(BF).astype(F32)
    return (low * (queries.shape[1] // HEADS) ** -0.5).astype(BF)


def project_kernel(segs, info, tok_ref, mem_ref, wqkv_ref, wckv_ref, vec_ref, q_ref, k_ref, v_ref, kt_ref, vt_ref, ck_ref, cv_ref, ckt_ref, cvt_ref):
    width = tok_ref.shape[2]
    found = nn(tok_ref[0], wqkv_ref[...])
    q_ref[0] = scaled(found[:, :width] + vec_ref[ROW : ROW + 1, :])
    put_keys(found[:, width:], vec_ref, 1, k_ref, v_ref, kt_ref, vt_ref)
    put_keys(nn(mem_ref[0], wckv_ref[...]), vec_ref, 5, ck_ref, cv_ref, ckt_ref, cvt_ref)


def project(segs, info, tokens, memory, wqkv, wckv, vec):
    rows, block, width = tokens.shape
    mem_block = memory.shape[1]
    shapes = [(rows, block, width)] * 3 + [(rows, width, block)] * 2
    shapes += [(rows, mem_block, width)] * 2 + [(rows, width, mem_block)] * 2
    return call(
        project_kernel, "project", 7, (rows,),
        [arg_spec(tokens.shape), arg_spec(memory.shape), whole(wqkv.shape), whole(wckv.shape), whole(vec.shape)],
        [row_spec(s) for s in shapes],
        [shape_of(s, BF) for s in shapes],
        [],
    )(segs, info, tokens, memory, wqkv, wckv, vec)


class Dims:
    def __init__(self, rows, block, key_block, blocks, seq_len, width):
        self.rows, self.block, self.key_block, self.blocks, self.seq_len = rows, block, key_block, blocks, seq_len
        self.width = width
        self.tile = min(256, block)
        self.step = min(256, key_block)


def split_pairs(ref, qoff, dims, keep_ref):
    lane = lax.broadcasted_iota(jnp.int32, (1, 128), 1)
    for h in range(HEADS):
        side = (lane < 64) if h % 2 == 0 else (lane >= 64)
        pair = slice(h // 2 * 128, h // 2 * 128 + 128)
        keep_ref[h] = ref[0, pl.ds(qoff, dims.tile), pair] * side.astype(F32).astype(BF)


def over_tiles(causal, dims, row, segs, info, segq_ref, segk_ref, bias_ref, qin, body):
    tile, step_size = dims.tile, dims.step
    mine, at = info[PLACE], info[ORDER + row]
    qoff = pl.multiple_of(mine * dims.block + qin, tile)
    q_first, q_last = segs[at, qoff], segs[at, qoff + tile - 1]
    keys_all = dims.key_block * dims.blocks
    for source in range(dims.blocks):
        owner = lax.rem(mine + source, dims.blocks)

        def step(kt, carry, source=source, owner=owner):
            inner = pl.multiple_of(kt * step_size, step_size)
            koff = pl.multiple_of(owner * dims.key_block + inner, step_size)
            k_first = segs[at, koff * dims.seq_len // keys_all]
            k_last = segs[at, (koff + step_size - 1) * dims.seq_len // keys_all]
            need = (k_first <= q_last) & (k_last >= q_first)
            if causal:
                need = need & (koff < qoff + tile)

            @pl.when(need)
            def _():
                across = jnp.broadcast_to(segk_ref[0, :, pl.ds(koff, step_size)], (tile, step_size))
                allowed = across.T == segq_ref[0, :, pl.ds(qoff, tile)]
                if causal:
                    kpos = lax.broadcasted_iota(jnp.int32, (step_size, tile), 0) + koff
                    qpos = lax.broadcasted_iota(jnp.int32, (step_size, tile), 1) + qoff
                    allowed = allowed & (kpos <= qpos)
                bias_ref[...] = jnp.where(allowed, 0.0, NEG)
                body(source, inner)

            return carry

        lax.fori_loop(0, dims.key_block // step_size, step, 0)


def far_needed(causal, dims, info, row, source):
    need = info[CROSSES] == 1 if dims.rows == 2 and row == 0 else info[CROSSES] >= 0
    if causal:
        need = need & (lax.rem(info[PLACE] + source, dims.blocks) < info[PLACE])
    return need


def forward_scratch(dims):
    return [
        pltpu.VMEM((HEADS, dims.tile, 128), BF),
        pltpu.VMEM((dims.step, dims.tile), F32),
        pltpu.VMEM((HEADS, dims.tile), F32),
        pltpu.VMEM((HEADS, dims.tile), F32),
        pltpu.VMEM((dims.width, dims.tile), F32),
        pltpu.VMEM((HEADS, dims.step, dims.tile), F32),
        pltpu.VMEM((HEADS, dims.step, dims.tile), BF),
    ]


def forward_tiles(causal, dims, row, segs, info, q_ref, segq_ref, segk_ref, k_refs, vt_refs, att_ref, lse_ref, scratch):
    qm_ref, bias_ref, top_ref, total_ref, acc_ref, score_ref, raised_ref = scratch

    def query_tile(i, carry):
        qin = pl.multiple_of(i * dims.tile, dims.tile)
        queries = pl.ds(qin, dims.tile)
        split_pairs(q_ref, qin, dims, qm_ref)
        top_ref[...] = jnp.full_like(top_ref, NEG)
        total_ref[...] = jnp.zeros_like(total_ref)
        acc_ref[...] = jnp.zeros_like(acc_ref)

        def body(source, inner):
            here = pl.ds(inner, dims.step)
            old = top_ref[...]
            new, fade, more = [], [], []
            for h in range(HEADS):
                pair = slice(h // 2 * 128, h // 2 * 128 + 128)
                scores = nt(k_refs[source][0, here, pair], qm_ref[h]) + bias_ref[...]
                score_ref[h] = scores
                new.append(jnp.maximum(old[h : h + 1, :], jnp.max(scores, 0, keepdims=True)))
                fade.append(jnp.exp(old[h : h + 1, :] - new[h]))
            for h in range(HEADS):
                raised = jnp.exp(score_ref[h] - new[h])
                raised_ref[h] = raised.astype(BF)
                more.append(col_sum(raised))
            for h in range(HEADS):
                heads = slice(h * 64, h * 64 + 64)
                acc_ref[heads, :] = acc_ref[heads, :] * fade[h] + nn(vt_refs[source][0, heads, here], raised_ref[h])
            top_ref[...] = jnp.concatenate(new, 0)
            total_ref[...] = total_ref[...] * jnp.concatenate(fade, 0) + jnp.concatenate(more, 0)

        over_tiles(causal, dims, row, segs, info, segq_ref, segk_ref, bias_ref, qin, body)
        total = total_ref[...]
        lse_ref[0, :, queries] = top_ref[...] + jnp.log(total)
        inverse = 1.0 / total
        for h in range(HEADS):
            heads = slice(h * 64, h * 64 + 64)
            acc_ref[heads, :] = acc_ref[heads, :] * inverse[h : h + 1, :]
        att_ref[0, queries, :] = acc_ref[...].T.astype(BF)
        return carry

    lax.fori_loop(0, dims.block // dims.tile, query_tile, 0)


def forward_kernel(causal, dims, far_count, segs, info, q_ref, segq_ref, segk_ref, base_ref, w_kv_ref, w_out_ref, w_cq_ref, vec_ref, k_ref, vt_ref, *refs):
    far_refs, refs = refs[: far_count * (dims.blocks - 1)], refs[far_count * (dims.blocks - 1) :]
    outs = 5 if causal else 4
    att_ref, lse_ref, unit_ref, rstd_ref = refs[:4]
    far_keys = refs[outs : outs + 4 * (dims.blocks - 1)]
    scratch = refs[outs + 4 * (dims.blocks - 1) :]
    row = pl.program_id(0)
    width = dims.width
    k_refs, vt_refs = [k_ref], [vt_ref]
    at = width if causal else 0
    for source in range(1, dims.blocks):
        keys = far_keys[4 * source - 4 : 4 * source]
        for which in range(far_count):
            ref = far_refs[far_count * (source - 1) + which]
            need = far_needed(causal, dims, info, which if far_count == 2 else 1, source)
            if far_count == 2:
                need = need & (row == which)

            @pl.when(need)
            def _(ref=ref, keys=keys):
                put_keys(nn(ref[0], w_kv_ref[:, at:]), vec_ref, 1 if causal else 5, *keys)

        k_refs.append(keys[0])
        vt_refs.append(keys[3])
    forward_tiles(causal, dims, row, segs, info, q_ref, segq_ref, segk_ref, k_refs, vt_refs, att_ref, lse_ref, scratch)
    base = base_ref[0].astype(F32)
    if not causal:
        base = base * vec_ref[0:1, :] + vec_ref[ROW + 3 : ROW + 4, :]
    shift = ROW + 2 if causal else ROW + 6
    unit, rstd = norm(base + nn(att_ref[0], w_out_ref[...]) + vec_ref[shift : shift + 1, :])
    unit_ref[0] = unit
    rstd_ref[0] = jnp.broadcast_to(rstd, rstd_ref.shape[1:])
    if causal:
        normed = (unit * vec_ref[0:1, :] + vec_ref[ROW + 3 : ROW + 4, :]).astype(BF)
        refs[4][0] = scaled(nn(normed, w_cq_ref[...]) + vec_ref[ROW + 4 : ROW + 5, :])


def attend_forward(causal, segs, info, q, segq, segk, base, w_kv, w_out, w_cq, vec, key, value_t, far):
    rows, block, width = q.shape
    key_block = key.shape[1]
    dims = Dims(rows, block, key_block, len(far) + 1, segs.shape[1], width)
    far_count = len(far[0]) if far else 1
    far_arrays = [a for arrays in far for a in arrays]
    base_spec = arg_spec(base.shape) if causal else row_spec(base.shape)
    far_specs = [row_spec(a.shape) if far_count == 1 else row_spec(a.shape, 0) for a in far_arrays]
    out_shape = [
        shape_of(q.shape, BF),
        shape_of((rows, HEADS, block), F32),
        shape_of(q.shape, F32),
        shape_of((rows, block, 128), F32),
    ] + [shape_of(q.shape, BF)] * causal
    keys = [shape_of((rows, key_block, width), BF)] * 2 + [shape_of((rows, width, key_block), BF)] * 2
    out_shape += keys * len(far)
    return call(
        functools.partial(forward_kernel, causal, dims, far_count),
        "attend_self" if causal else "attend_cross",
        14, (rows,),
        [row_spec(q.shape), arg_spec(segq.shape), arg_spec(segk.shape), base_spec]
        + [whole(w.shape) for w in (w_kv, w_out, w_cq, vec)]
        + [row_spec(key.shape), row_spec(value_t.shape)]
        + far_specs,
        [row_spec(s.shape) for s in out_shape],
        out_shape,
        forward_scratch(dims),
    )(segs, info, q, segq, segk, base, w_kv, w_out, w_cq, vec, key, value_t, *far_arrays)


def backward_scratch(dims):
    return [
        pltpu.VMEM((HEADS, dims.tile, 128), BF),
        pltpu.VMEM((HEADS, dims.tile, 128), BF),
        pltpu.VMEM((dims.step, dims.tile), F32),
        pltpu.VMEM((dims.width, dims.block), F32),
        pltpu.VMEM((dims.blocks, dims.key_block, dims.width), F32),
        pltpu.VMEM((dims.blocks, dims.key_block, dims.width), F32),
        pltpu.VMEM((HEADS, dims.step, dims.tile), F32),
        pltpu.VMEM((HEADS, dims.step, dims.tile), BF),
        pltpu.VMEM((HEADS, dims.step, dims.tile), BF),
    ]


def backward_tiles(causal, dims, row, segs, info, q_ref, do_ref, lse_ref, dd_ref, segq_ref, segk_ref, k_refs, kt_refs, v_refs, scratch):
    qm_ref, dm_ref, bias_ref, dq_ref, dk_ref, dv_ref, weight_ref, low_ref, ds_ref = scratch
    dk_ref[...] = jnp.zeros_like(dk_ref)
    dv_ref[...] = jnp.zeros_like(dv_ref)
    dq_ref[...] = jnp.zeros_like(dq_ref)

    def query_tile(i, carry):
        qin = pl.multiple_of(i * dims.tile, dims.tile)
        queries = pl.ds(qin, dims.tile)
        split_pairs(q_ref, qin, dims, qm_ref)
        split_pairs(do_ref, qin, dims, dm_ref)

        def body(source, inner):
            here = pl.ds(inner, dims.step)
            lse, dd = lse_ref[0, :, queries], dd_ref[0, :, queries]
            for h in range(HEADS):
                pair = slice(h // 2 * 128, h // 2 * 128 + 128)
                weights = jnp.exp(nt(k_refs[source][0, here, pair], qm_ref[h]) + bias_ref[...] - lse[h : h + 1, :])
                weight_ref[h] = weights
                low_ref[h] = weights.astype(BF)
            for h in range(HEADS):
                pair = slice(h // 2 * 128, h // 2 * 128 + 128)
                grads = nt(v_refs[source][0, here, pair], dm_ref[h])
                ds_ref[h] = (weight_ref[h] * (grads - dd[h : h + 1, :])).astype(BF)
            for h in range(0, HEADS, 2):
                pair = slice(h // 2 * 128, h // 2 * 128 + 128)
                dv_ref[source, here, pair] += nn(low_ref[h], dm_ref[h]) + nn(low_ref[h + 1], dm_ref[h + 1])
                dk_ref[source, here, pair] += nn(ds_ref[h], qm_ref[h]) + nn(ds_ref[h + 1], qm_ref[h + 1])
            for h in range(HEADS):
                heads = slice(h * 64, h * 64 + 64)
                dq_ref[heads, queries] += nn(kt_refs[source][0, heads, here], ds_ref[h])

        over_tiles(causal, dims, row, segs, info, segq_ref, segk_ref, bias_ref, qin, body)
        return carry

    lax.fori_loop(0, dims.block // dims.tile, query_tile, 0)
    return dq_ref[...].T * (dims.width // HEADS) ** -0.5


def head_products(a, b):
    turned = (a.astype(F32) * b.astype(F32)).T
    return jnp.concatenate([col_sum(turned[h * 64 : h * 64 + 64]) for h in range(HEADS)], 0)


def put(buffer, earlier, at, value, first, part):
    done = 0
    while done < value.shape[0]:
        b, inner = divmod(first + done, part)
        count = min(part - inner, value.shape[0] - done)
        rows = slice(at + inner, at + inner + count)
        piece = value[done : done + count]
        if earlier is not None:
            piece = piece + earlier[b, rows, :].astype(F32)
        buffer[b, rows, :] = piece.astype(BF)
        done += count


class Halves:
    def __init__(self, info, buffer, outs, sems):
        self.side, self.buffer, self.outs, self.sems = info[SIDE], buffer, outs, sems
        self.half = buffer.shape[1] // 2

    def each(self, h, what):
        source = self.buffer.at[:, h * self.half : (h + 1) * self.half, :]
        for k, here in enumerate((self.side == h, self.side != h)):
            pl.when(here)(what(pltpu.make_async_copy(source, self.outs[k], self.sems.at[h])))

    def start(self, h):
        self.each(h, lambda copy: copy.start)

    def wait(self):
        for h in range(2):
            self.each(h, lambda copy: copy.wait)


def sum_specs(buffer_shape, last):
    blocks, rows, lanes = buffer_shape
    if last:
        half = shape_of((blocks, rows // 2, lanes), BF)
        return [half] * 2, [pl.BlockSpec(memory_space=pl.ANY)] * 2, [pltpu.VMEM(buffer_shape, BF), pltpu.SemaphoreType.DMA((2,))]
    return [shape_of(buffer_shape, BF)], [whole(buffer_shape)], []


def backward_kernel(causal, dims, row, pickers, has_earlier, has_base, last, segs, info, *refs):
    take = iter(refs)

    def some(count):
        return [next(take) for _ in range(count)]

    blocks, width = dims.blocks, dims.width
    segq_ref, segk_ref, lse_ref, dd_ref, vec_ref, vec_in = some(6)
    sources = some(len(pickers))
    if has_base:
        next(take)
    outs = some((0 if causal else 3) + blocks + (1 if causal else 0))
    vec_out = next(take)
    sum_outs = some(2 if last else 1)
    scratch = some(9)
    acc_ref, buffer, in_sems, out_sems, sum_sems = some(5)
    places = some(len(pickers))
    out_refs = some(len(outs))

    needs = [None] + [far_needed(causal, dims, info, row, source) for source in range(1, blocks)]
    fetches = []
    for k, (source, place, picker) in enumerate(zip(sources, places, pickers)):
        index, of_source = picker
        if index == "arg":
            index = info[ORDER + row]
        fetches.append(Fetch(source, place, in_sems.at[k], index, None if of_source is None else needs[of_source]))
    take = iter(fetches)
    q_get, do_get = some(2)
    own = some(3)
    others = [some(3) for _ in range(1, blocks)]
    x_gets = some(blocks)
    early = 5 + 3 * (blocks - 1)
    for f in fetches[:early]:
        f.start()
    if not causal:
        w_kv_get, unit1_get, rstd1_get, wcq_get, gp2_get, att_get, wso_get = some(7)
    earlier_get = next(take) if has_earlier else None

    leaving = []

    def leave(k):
        out = outs[k]
        if not causal and k == 3:
            out = out.at[pl.ds(info[ORDER + row], 1)]
        leaving.append(pltpu.make_async_copy(out_refs[k], out, out_sems.at[k]))
        leaving[-1].start()

    vec_out[...] = vec_in[...]
    part = width // blocks
    dk_ref, dv_ref = scratch[4:6]
    q_ref, do_ref = q_get.wait(), do_get.wait()
    k_refs, v_refs, kt_refs = zip(*[[g.wait() for g in gets] for gets in (own, *others)])
    for f in fetches[early:]:
        f.start()
    dq = backward_tiles(causal, dims, row, segs, info, q_ref, do_ref, lse_ref, dd_ref, segq_ref, segk_ref, k_refs, kt_refs, v_refs, scratch)
    low_q = dq.astype(BF)
    x_refs = [g.wait() for g in x_gets]
    if causal:
        out_refs[blocks][0] = low_q
        leave(blocks)
        shift_v, first_dx, first = 1, 0, part
    else:
        shift_v, first_dx, first = 5, 3, 2 * part
        w_kv = w_kv_get.wait()

    for source in range(blocks):
        place = out_refs[first_dx + source]

        def back(source=source, place=place):
            x = x_refs[source][0]
            dv = dv_ref[source]
            low = jnp.concatenate([dk_ref[source].astype(BF), dv.astype(BF)], 1)
            vec_out[ROW + shift_v : ROW + shift_v + 1, :] += col_sum(dv)
            if causal:
                place[0] = low
            else:
                place[0] = nt(low, w_kv[...]).astype(place.dtype)
            more = tn(x, low)
            if source == 0:
                acc_ref[...] = more
            else:
                acc_ref[...] += more

        if source == 0:
            back()
        else:
            pl.when(needs[source])(back)

            @pl.when(jnp.logical_not(needs[source]))
            def _(place=place):
                place[...] = jnp.zeros_like(place)

        leave(first_dx + source)

    earlier = earlier_get.wait() if has_earlier else None
    for p in range(2 * width // 512):
        put(buffer, earlier, first + p * part, acc_ref[:, p * 512 : (p + 1) * 512], 0, part)
    if causal:
        vec_out[ROW : ROW + 1, :] += col_sum(dq)
        put(buffer, earlier, 0, tn(x_refs[0][0], low_q), 0, part)
    else:
        unit1 = unit1_get.wait()[0]
        rstd1 = rstd1_get.wait()[0]
        wcq, gp2 = wcq_get.wait(), gp2_get.wait()
        grad = gp2[0] + nt(low_q, wcq[...])
        gp1 = norm_back(grad, unit1, rstd1[:, :1], vec_ref[0:1, :])
        out_refs[0][0] = gp1
        leave(0)
        low_one = gp1.astype(BF)
        att, wso = att_get.wait()[0], wso_get.wait()
        put(buffer, earlier, part, tn(att, low_one), 0, part)
        normed = (unit1 * vec_ref[0:1, :] + vec_ref[ROW + 3 : ROW + 4, :]).astype(BF)
        put(buffer, earlier, 0, tn(normed, low_q), 0, part)
        if not last:
            leaving.append(pltpu.make_async_copy(buffer, sum_outs[0], sum_sems.at[0]))
            leaving[-1].start()
        datt = nt(low_one, wso[...]).astype(BF)
        out_refs[1][0] = datt
        leave(1)
        out_refs[2][0] = head_products(datt, att)
        leave(2)
        vec_out[0:1, :] += col_sum(grad * unit1)
        vec_out[ROW + 2 : ROW + 3, :] += col_sum(gp1)
        vec_out[ROW + 3 : ROW + 4, :] += col_sum(grad)
        vec_out[ROW + 4 : ROW + 5, :] += col_sum(dq)

    if causal and last:
        base = 3 * part * (width // 512)
        buffer[:, base:, :] = jnp.zeros((blocks, buffer.shape[1] - base, 512), BF)
        hidden_part = 4 * 512 // blocks
        for b in range(blocks):
            buffer[b, base : base + UP, :part] = vec_out[:UP, b * part : (b + 1) * part].astype(BF)
            for k in range(max(1, hidden_part // 512)):
                at = b * hidden_part + k * 512
                count = min(512, hidden_part)
                piece = vec_out[UP + at // 512 : UP + at // 512 + 1, at % 512 : at % 512 + count]
                buffer[b, base + UP + k : base + UP + k + 1, :count] = piece.astype(BF)
    if last:
        halves = Halves(info, buffer, sum_outs, sum_sems)
        halves.start(0)
        halves.start(1)
        halves.wait()
    elif causal:
        leaving.append(pltpu.make_async_copy(buffer, sum_outs[0], sum_sems.at[0]))
        leaving[-1].start()
    for c in leaving:
        c.wait()


def attend_backward(causal, row, last, us, segs, info, q, segq, segk, d_out, lse, dd, vec, vec_in, keys, keys_t, values, inputs, w_kv, extra, earlier, base):
    rows, block, width = q.shape
    blocks, key_block = len(keys), keys[0].shape[1]
    dims = Dims(rows, block, key_block, blocks, segs.shape[1], width)

    def at(a):
        return row if a.shape[0] == rows else 0

    def spec(a):
        return row_spec(a.shape, at(a))

    small = [segq, segk, lse, dd, vec, vec_in]
    small_specs = [arg_spec(segq.shape, row), arg_spec(segk.shape, row), spec(lse), spec(dd), whole(vec.shape), whole(vec_in.shape)]
    large = [(q, (row, None)), (d_out, (at(d_out), None))]
    for s in range(blocks):
        large += [(a[s], (row, None if s == 0 else s)) for a in (keys, values, keys_t)]
    large += [(a, ("arg" if s == 0 else at(a), None if s == 0 else s)) for s, a in enumerate(inputs)]
    if not causal:
        gp2, unit1, rstd1, att, wcq, wso = extra
        large += [(w_kv, (None, None)), (unit1, (row, None)), (rstd1, (row, None)), (wcq, (None, None))]
        large += [(gp2, (row, None)), (att, (row, None)), (wso, (None, None))]
    if earlier is not None:
        large.append((earlier, (None, None)))
    out_shape = []
    if not causal:
        out_shape += [shape_of((1, block, width), F32), shape_of((1, block, width), BF), shape_of((1, HEADS, block), F32)]
    if causal:
        out_shape += [shape_of((1, key_block, 2 * width), BF) for s in range(blocks)] + [shape_of((1, block, width), BF)]
    else:
        out_shape += [shape_of((1, key_block, width), F32 if s == 0 else BF) for s in range(blocks)]
    vec_shape = shape_of((VROWS, width), F32)
    buffer_rows = (3 if causal else 4) * width // blocks * (width // 512) + (VECTOR_ROWS if causal and last else 0)
    buffer_shape = (blocks, buffer_rows, 512)
    sum_shapes = [shape_of((blocks, buffer_rows // 2, 512), BF)] * 2 if last else [shape_of(buffer_shape, BF)]
    anywhere = pl.BlockSpec(memory_space=pl.ANY)
    out_places = [pltpu.VMEM(s.shape, s.dtype) for s in out_shape]
    if not causal:
        out_shape[3] = shape_of((rows, key_block, width), F32)
    bases = [] if base is None else [base]
    aliases = {2 + len(small) + len(large): 3} if bases else {}
    places = [pltpu.VMEM(a.shape if p[0] is None else (1, *a.shape[1:]), a.dtype) for a, p in large]
    return call(
        functools.partial(backward_kernel, causal, dims, row, [p for _, p in large], earlier is not None, base is not None, last),
        "attend_self_back" if causal else "attend_cross_back",
        us, (1,),
        small_specs + [anywhere] * (len(large) + len(bases)),
        [anywhere] * len(out_shape) + [whole(vec_shape.shape)] + [anywhere] * len(sum_shapes),
        out_shape + [vec_shape] + sum_shapes,
        backward_scratch(dims)
        + [
            pltpu.VMEM((width, 2 * width), F32),
            pltpu.VMEM(buffer_shape, BF),
            pltpu.SemaphoreType.DMA((len(large),)),
            pltpu.SemaphoreType.DMA((len(out_shape),)),
            pltpu.SemaphoreType.DMA((2,)),
        ]
        + places
        + out_places,
        SELF_MIB if causal else MIB,
        aliases,
    )(segs, info, *small, *[a for a, _ in large], *bases)


def tokens_back_kernel(rows, blocks, segs, info, *refs):
    take = iter(refs)
    per_row = [[next(take) for _ in range(2 + blocks)] for _ in range(rows)]
    w_ref, base_out = next(take), next(take)
    outs = [[next(take) for _ in range(1, blocks)] for _ in range(rows)]
    width = w_ref.shape[0]
    for r, (dq_ref, base_ref, *dkv_refs) in enumerate(per_row):
        for source in range(blocks):
            grad = nt(dkv_refs[source][0], w_ref[:, width:])
            if source == 0:
                base_out[info[ORDER + r]] = grad + nt(dq_ref[0], w_ref[:, :width]) + base_ref[0]
            else:
                outs[r][source - 1][0] = grad.astype(BF)


def tokens_back(segs, info, found, gp1, w):
    rows, blocks = len(found), len(found[0]) - 1
    args = []
    for (*dkv, dq), base in zip(found, gp1):
        args += [dq, base, *dkv]
    args.append(w)
    block = gp1[0].shape[1:]
    out_shape = [shape_of((rows, *block), F32)] + [shape_of((1, *block), BF)] * (rows * (blocks - 1))
    base, *got = call(
        functools.partial(tokens_back_kernel, rows, blocks), "tokens_back", 8, (1,),
        [whole(a.shape) for a in args], [whole(s.shape) for s in out_shape], out_shape, [], SELF_MIB,
    )(segs, info, *args)
    return base, *[got[r * (blocks - 1) : (r + 1) * (blocks - 1)] for r in range(rows)]


def feed_kernel(dims, far_count, segs, info, q_ref, segq_ref, segk_ref, unit1_ref, cot_ref, upshift_ref, vec_ref, k_ref, vt_ref, wckv_ref, wco_ref, wup_any, wdown_any, *refs):
    take = iter(refs)

    def some(count):
        return [next(take) for _ in range(count)]

    blocks = dims.blocks
    far_refs = some(far_count * (blocks - 1))
    lse_ref, out_ref, gp2_ref, dco_ref, dcross_ref, vec_out, keep_ref, send_ref = some(8)
    far_keys = [some(3) for _ in range(1, blocks)]
    hid_ref, slope_ref, low_up_ref, normed_ref, low3_ref, co_all_ref, low2_ref, buffer, sems = some(9)
    wup_ref, wdown_ref, w_sems, att_ref = some(4)
    far_vt = some(blocks - 1)
    scratch = some(7)
    width, hidden_width = wup_ref.shape
    panels = hidden_width // 512
    block = dims.block
    row = pl.program_id(0)
    here = pl.ds(pl.multiple_of(row * block, block), block)
    weights = [pltpu.make_async_copy(wup_any, wup_ref, w_sems.at[0]), pltpu.make_async_copy(wdown_any, wdown_ref, w_sems.at[1])]

    @pl.when(row == 0)
    def _():
        vec_out[...] = jnp.zeros_like(vec_out)
        for w in weights:
            w.start()

    k_refs, vt_refs = [k_ref], [vt_ref]
    for source in range(1, blocks):
        keys = (*far_keys[source - 1], far_vt[source - 1])
        for which in range(far_count):
            ref = far_refs[far_count * (source - 1) + which]
            need = far_needed(False, dims, info, which if far_count == 2 else 1, source)
            if far_count == 2:
                need = need & (row == which)

            @pl.when(need)
            def _(ref=ref, keys=keys):
                put_keys(nn(ref[0], wckv_ref[...]), vec_ref, 5, *keys)

        k_refs.append(keys[0])
        vt_refs.append(keys[3])
    forward_tiles(False, dims, row, segs, info, q_ref, segq_ref, segk_ref, k_refs, vt_refs, att_ref, lse_ref, scratch)
    co = att_ref[0]
    co_all_ref[here, :] = co
    normed_one = unit1_ref[0] * vec_ref[0:1, :] + vec_ref[ROW + 3 : ROW + 4, :]
    unit2, rstd2 = norm(normed_one + nn(co, wco_ref[...]) + vec_ref[ROW + 6 : ROW + 7, :])

    @pl.when(row == 0)
    def _():
        for w in weights:
            w.wait()

    normed = unit2 * vec_ref[1:2, :] + vec_ref[ROW + 7 : ROW + 8, :]
    normed_low = normed.astype(BF)
    normed_ref[here, :] = normed_low
    for p in range(panels):
        cols = slice(p * 512, (p + 1) * 512)
        up = nn(normed_low, wup_ref[:, cols]) + upshift_ref[p : p + 1, :]
        square = up * up
        bent = jnp.tanh(up * (GELU_A + GELU_B * square))
        half = 0.5 * up
        hid_ref[here, cols] = (half + half * bent).astype(BF)
        slope_ref[:, cols] = 0.5 + 0.5 * bent + half * (1.0 - bent * bent) * (GELU_A + 3 * GELU_B * square)
    pre = normed + nn(hid_ref[here, :], wdown_ref[...]) + vec_ref[ROW + 8 : ROW + 9, :]
    unit3, rstd3 = norm(pre)
    out_ref[0] = (unit3 * vec_ref[2:3, :] + vec_ref[ROW + 9 : ROW + 10, :]).astype(BF)
    cot = cot_ref[0].astype(F32)
    gp3 = norm_back(cot, unit3, rstd3, vec_ref[2:3, :])
    low3 = gp3.astype(BF)
    low3_ref[here, :] = low3
    vec_out[2:3, :] += col_sum(cot * unit3)
    vec_out[ROW + 8 : ROW + 9, :] += col_sum(gp3)
    vec_out[ROW + 9 : ROW + 10, :] += col_sum(cot)
    for p in range(panels):
        cols = slice(p * 512, (p + 1) * 512)
        grad_up = nt(low3, wdown_ref[cols, :]) * slope_ref[:, cols]
        low_up_ref[here, cols] = grad_up.astype(BF)
        vec_out[UP + p : UP + p + 1, :] += col_sum(grad_up)
    grad = gp3 + nt(low_up_ref[here, :], wup_ref[...])
    gp2 = norm_back(grad, unit2, rstd2, vec_ref[1:2, :])
    gp2_ref[0] = gp2
    low2 = gp2.astype(BF)
    low2_ref[here, :] = low2
    dco = nt(low2, wco_ref[...]).astype(BF)
    dco_ref[0] = dco
    dcross_ref[0] = head_products(dco, co)
    vec_out[1:2, :] += col_sum(grad * unit2)
    vec_out[ROW + 6 : ROW + 7, :] += col_sum(gp2)
    vec_out[ROW + 7 : ROW + 8, :] += col_sum(grad)

    @pl.when(row == pl.num_programs(0) - 1)
    def _():
        down, part = hidden_width // blocks, width // blocks
        halves = Halves(info, buffer, (keep_ref, send_ref), sems)
        started = False
        for p in range(panels):
            cols = slice(p * 512, (p + 1) * 512)
            put(buffer, None, 0, tn(hid_ref[:, cols], low3_ref[...]), p * 512, down)
        for p in range(panels):
            cols = slice(p * 512, (p + 1) * 512)
            put(buffer, None, down + p * part, tn(normed_ref[...], low_up_ref[:, cols]), 0, part)
            if not started and down + (p + 1) * part >= halves.half:
                halves.start(0)
                started = True
        put(buffer, None, down + panels * part, tn(co_all_ref[...], low2_ref[...]), 0, part)
        halves.start(1)
        halves.wait()


def feed(segs, info, q, segq, segk, unit1, cot, up_rows, vec, key, value_t, wckv, wco, wup, wdown, far):
    rows, block, width = unit1.shape
    hidden = wup.shape[1]
    tokens = rows * block
    key_block = key.shape[1]
    blocks = len(far) + 1
    dims = Dims(rows, block, key_block, blocks, segs.shape[1], width)
    far_count = len(far[0]) if far else 1
    far_arrays = [a for arrays in far for a in arrays]
    far_specs = [row_spec(a.shape) if far_count == 1 else row_spec(a.shape, 0) for a in far_arrays]
    buffer_shape = (blocks, (2 * hidden + width) // blocks, width)
    shapes, specs, more = sum_specs(buffer_shape, True)
    rest = [
        shape_of(unit1.shape, BF),
        shape_of(unit1.shape, F32),
        shape_of(unit1.shape, BF),
        shape_of((rows, HEADS, block), F32),
    ]
    lse_shape, vec_shape = shape_of((rows, HEADS, block), F32), shape_of((VROWS, width), F32)
    keys = ([shape_of((rows, key_block, width), BF)] * 2 + [shape_of((rows, width, key_block), BF)]) * (blocks - 1)
    anywhere = pl.BlockSpec(memory_space=pl.ANY)
    return call(
        functools.partial(feed_kernel, dims, far_count), "attend_cross_feed", 40, (rows,),
        [row_spec(q.shape), arg_spec(segq.shape), arg_spec(segk.shape), row_spec(unit1.shape), arg_spec(cot.shape)]
        + [whole(up_rows.shape), whole(vec.shape), row_spec(key.shape), row_spec(value_t.shape)]
        + [whole(wckv.shape), whole(wco.shape), anywhere, anywhere]
        + far_specs,
        [row_spec(lse_shape.shape), arg_spec(unit1.shape)]
        + [row_spec(s.shape) for s in rest[1:]]
        + [whole(vec_shape.shape)]
        + specs
        + [row_spec(s.shape) for s in keys],
        [lse_shape] + rest + [vec_shape] + shapes + keys,
        [
            pltpu.VMEM((tokens, hidden), BF),
            pltpu.VMEM((block, hidden), F32),
            pltpu.VMEM((tokens, hidden), BF),
            pltpu.VMEM((tokens, width), BF),
            pltpu.VMEM((tokens, width), BF),
            pltpu.VMEM((tokens, width), BF),
            pltpu.VMEM((tokens, width), BF),
        ]
        + more
        + [pltpu.VMEM(wup.shape, BF), pltpu.VMEM(wdown.shape, BF), pltpu.SemaphoreType.DMA((2,)), pltpu.VMEM((1, block, width), BF)]
        + [pltpu.VMEM((1, width, key_block), BF)] * (blocks - 1)
        + forward_scratch(dims),
    )(segs, info, q, segq, segk, unit1, cot, up_rows, vec, key, value_t, wckv, wco, wup, wdown, *far_arrays)


def bits(size):
    return size.bit_length() - 1


def all_pairs(mask):
    return [(i, i ^ mask) for i in range(lax.axis_size("dp") * lax.axis_size("blk"))]


def swap(values, mask):
    return lax.ppermute(values, ("dp", "blk"), all_pairs(mask))


def place():
    return lax.axis_index("dp") * lax.axis_size("blk") + lax.axis_index("blk")


def by_place(parts, at, count):
    for bit in range(count):
        side = ((at >> bit) & 1) == 1
        parts = [jnp.where(side, parts[j ^ (1 << bit)], parts[j]) for j in range(len(parts))]
    return parts


class Sum:
    def __init__(self, keep, send):
        self.values = [keep, send]
        self.near = bits(lax.axis_size("blk"))
        self.far = bits(lax.axis_size("dp")) - 2
        self.steps = [self.core, self.near_scatter, self.far_scatter, self.far_gather, self.near_gather, self.core_gather]

    def step(self):
        if self.steps:
            self.values = self.steps.pop(0)(*self.values)

    def core(self, keep, send):
        return [(keep.astype(F32) + swap(send, 1 << self.near).astype(F32)).astype(BF)]

    def near_scatter(self, now):
        blocks = now.shape[0]
        cut = now.reshape(blocks, 2, now.shape[1] // 2, now.shape[2])
        mine, side = lax.axis_index("blk"), (lax.axis_index("dp") >> 1) & 1

        def piece(b, s):
            return lax.dynamic_slice(cut, (mine ^ b, side ^ s, 0, 0), (1, 1, *cut.shape[2:]))[0, 0]

        total = piece(0, 0).astype(F32)
        for s in range(2):
            for b in range(blocks):
                if s or b:
                    total = total + swap(piece(b, s), (2 * s << self.near) | b).astype(F32)
        return [total.astype(BF)]

    def far_scatter(self, now):
        at = lax.axis_index("dp") >> 2
        cut = now.reshape(1 << self.far, -1, now.shape[1])
        total = lax.dynamic_index_in_dim(cut, at, 0, False).astype(F32)
        for k in range(1, 1 << self.far):
            piece = lax.dynamic_index_in_dim(cut, at ^ k, 0, False)
            total = total + swap(piece, (k << 2) << self.near).astype(F32)
        return [total.astype(BF)]

    def far_gather(self, now):
        at = lax.axis_index("dp") >> 2
        parts = [now] + [swap(now, (k << 2) << self.near) for k in range(1, 1 << self.far)]
        return [jnp.concatenate(by_place(parts, at, self.far), 0)]

    def near_gather(self, now):
        at = (lax.axis_index("dp") >> 1) & 1
        return [jnp.concatenate(by_place([now, swap(now, 2 << self.near)], at, 1), 0)]

    def core_gather(self, now):
        return [now, swap(now, 1 << self.near)]

    def rows(self):
        return jnp.concatenate(by_place(self.values, lax.axis_index("dp") & 1, 1), 0)


def advance(sums, anchor):
    for s in sums:
        s.step()
    flat, anchor = lax.optimization_barrier(([s.values for s in sums], anchor))
    for s, values in zip(sums, flat):
        s.values = values
    return anchor


def from_next(values, step):
    size = lax.axis_size("blk")
    return lax.ppermute(values, "blk", [((i + step) % size, i) for i in range(size)])


def to_next(values, step):
    size = lax.axis_size("blk")
    return lax.ppermute(values, "blk", [(i, (i + step) % size) for i in range(size)])


def unpanel(part, columns):
    panels = columns // 512
    rows = part.shape[0] // panels
    return jnp.concatenate([part[p * rows : (p + 1) * rows] for p in range(panels)], 1).astype(F32)


def body(tokens, memory, segments, w_qkv, w_self_out, w_cross_q, w_cross_kv, w_cross_out, w_up, w_down, norm_gains, shifts, up_shift, cotangent):
    rows, block, width = tokens.shape
    mem_block = memory.shape[1]
    blocks = lax.axis_size("blk")
    mine = lax.axis_index("blk")
    seq_len = segments.shape[1]
    mem_len = mem_block * blocks
    hidden = w_up.shape[1]
    far = range(1, blocks)

    pick = rows == 2
    if pick:
        single = (segments[0, -1] != 0).astype(jnp.int32)
        order = jnp.stack([1 - single, single])
        edges = np.arange(1, blocks) * block
        crosses = jnp.any((segments[:, edges - 1] == segments[:, edges]) & (jnp.arange(2) != single)[:, None])
    else:
        order, crosses = jnp.arange(rows), jnp.array(True)
    head = jnp.stack([mine, lax.axis_index("dp") & 1, crosses.astype(jnp.int32)])
    info = jnp.concatenate([head, order]).astype(jnp.int32)

    def fetch(arrays):
        if not pick:
            return [[[from_next(a, k)] for k in far] for a in arrays]
        ones = [[from_next(lax.dynamic_index_in_dim(a, single, 0, True), k) for k in far] for a in arrays]
        others = [lax.dynamic_index_in_dim(a, 1 - single, 0, True) for a in arrays]
        others = lax.cond(
            crosses,
            lambda vs: [[from_next(v, k) for k in far] for v in vs],
            lambda vs: [[v for _ in far] for v in vs],
            others,
        )
        return [[[o, g] for o, g in zip(*pair)] for pair in zip(others, ones)]

    far_toks, far_mems = fetch([tokens, memory])

    vec = jnp.concatenate([norm_gains.T, shifts.T, jnp.zeros((3, width), F32)], 0)
    up_rows = up_shift.reshape(-1, 512)
    seg_rows = segments.astype(F32)[:, None, :]
    mem_seg = seg_rows[:, :, np.arange(mem_len) * seq_len // mem_len] if mem_len != seq_len else seg_rows

    q, k, v, kt, vt, ck, cv, ckt, cvt = project(segments, info, tokens, memory, w_qkv, w_cross_kv, vec)
    att, lse1, unit1, rstd1, cq, *keys = attend_forward(
        True, segments, info, q, seg_rows, seg_rows, tokens, w_qkv, w_self_out, w_cross_q, vec, k, vt, far_toks
    )
    k1, v1, kt1 = [[own] + keys[at::4] for at, own in enumerate((k, v, kt))]
    lse2, out, gp2, dco, dd2, vectors, keep, send, *keys = feed(
        segments, info, cq, seg_rows, mem_seg, unit1, cotangent, up_rows, vec, ck, cvt, w_cross_kv, w_cross_out, w_up, w_down, far_mems
    )
    k2, v2, kt2 = [[own] + keys[at::3] for at, own in enumerate((ck, cv, ckt))]
    sums = [Sum(keep, send)]

    def far_of(found, r):
        return [f[r] if len(f) > 1 else f[0] for f in found]

    def give(found):
        if not pick:
            return [[to_next(o, k) for k, o in zip(far, others)] for others in found]
        others, ones = found
        got = [to_next(o, k) for k, o in zip(far, ones)]
        more = lax.cond(
            crosses,
            lambda vs: [to_next(o, k) for k, o in zip(far, vs)],
            lambda vs: list(vs),
            list(others),
        )
        return [more, got]

    def total(base, got):
        if pick:
            is_one = (jnp.arange(2) == single)[:, None, None]
            parts = [jnp.where(is_one, one, other) for other, one in zip(*got)]
        else:
            parts = [jnp.concatenate([row[k] for row in got], 0) for k in range(blocks - 1)]
        return functools.reduce(lambda a, b: a + b.astype(F32), parts, base)

    earlier, rows_gp1, dmem, memory_base = None, [], [], None
    for r in range(rows):
        last = r == rows - 1
        gp1, datt, dd1, *rest = attend_backward(
            False, r, last, 24 if last else 14, segments, info, cq, seg_rows, mem_seg, dco, lse2, dd2, vec, vectors,
            k2, kt2, v2, [memory] + far_of(far_mems, r), w_cross_kv,
            [gp2, unit1, rstd1, att, w_cross_q, w_self_out], earlier, memory_base,
        )
        memory_base = rest[0]
        dmem.append(rest[1:blocks])
        vectors, earlier = rest[blocks], rest[-1]
        rows_gp1.append((gp1, datt, dd1))
        vectors = advance(sums, vectors)
    sums.append(Sum(*rest[-2:]))
    got_mem = give(dmem)
    earlier, dkv = None, []
    for r in range(rows):
        last = r == rows - 1
        _, datt, dd1 = rows_gp1[r]
        rest = attend_backward(
            True, r, last, 14 if last else 11, segments, info, q, seg_rows, seg_rows, datt, lse1, dd1, vec, vectors,
            k1, kt1, v1, [tokens] + far_of(far_toks, r), None, [], earlier, None,
        )
        dkv.append(rest[: blocks + 1])
        vectors, earlier = rest[blocks + 1], rest[-1]
        if not last:
            vectors, got_mem = advance(sums, (vectors, got_mem))
    dkv = advance(sums, dkv)
    sums.append(Sum(*rest[-2:]))
    tokens_base, *dtok = tokens_back(segments, info, dkv, [g[0] for g in rows_gp1], w_qkv)
    first, second, third = sums
    dtok = advance(sums, dtok)

    part, hidden_part = width // blocks, hidden // blocks
    dtok, got_mem = advance(sums, (dtok, got_mem))
    got_tok = give(dtok)
    up_at = hidden_part + (hidden // 512) * part
    feed_sum = first.rows()
    found = (
        total(memory_base, got_mem),
        feed_sum[up_at:].astype(F32),
        unpanel(feed_sum[hidden_part:up_at], hidden),
        feed_sum[:hidden_part].astype(F32),
    )
    grad_memory, grad_cross_out, grad_up, grad_down = advance([second, third], found)
    got_tok = advance([second, third], got_tok)
    other_sum = second.rows()
    found = (
        total(tokens_base, got_tok),
        other_sum[part : 2 * part].astype(F32),
        other_sum[:part].astype(F32),
        unpanel(other_sum[2 * part :], 2 * width),
    )
    grad_tokens, grad_self_out, grad_cross_q, grad_cross_kv = advance([third], found)
    while third.steps:
        third.step()
    qkv_sum = third.rows()
    qkv_rows = 3 * part * (width // 512)
    vectors = qkv_sum[qkv_rows:].astype(F32)
    return (
        out,
        grad_tokens,
        grad_memory,
        unpanel(qkv_sum[:qkv_rows], 3 * width),
        grad_self_out,
        grad_cross_q,
        grad_cross_kv,
        grad_cross_out,
        grad_up,
        grad_down,
        vectors[:ROW, :part].T,
        vectors[ROW:UP, :part].T,
        vectors[UP : UP + max(1, hidden_part // 512), : min(512, hidden_part)].reshape(-1),
    )


def solution(mesh):
    split = P("dp", "blk", None)
    in_specs = (split, split, P("dp", None)) + (P(),) * 10 + (split,)
    out_specs = (split,) * 3 + (P("blk", None),) * 9 + (P("blk"),)
    return jax.shard_map(body, mesh=mesh, in_specs=in_specs, out_specs=out_specs, check_vma=False)
```

```python
import functools

import jax
import jax.numpy as jnp
import numpy as np
from jax import lax
from jax.experimental import pallas as pl
from jax.experimental.pallas import tpu as pltpu
from jax.sharding import PartitionSpec as P

HEADS = 8
NEG = -1e30
F32 = jnp.float32
BF = jnp.bfloat16
GELU_A = 0.7978845608028654
GELU_B = 0.7978845608028654 * 0.044715
ROW = 3
UP = 13
VROWS = 24
VECTOR_ROWS = 128


def nn(a, b):
    return jnp.dot(a, b, preferred_element_type=F32)


def nt(a, b):
    return lax.dot_general(a, b, (((1,), (1,)), ((), ())), preferred_element_type=F32)


def tn(a, b):
    return lax.dot_general(a, b, (((0,), (0,)), ((), ())), preferred_element_type=F32)


def norm(values):
    center = values - jnp.mean(values, -1, keepdims=True)
    rstd = lax.rsqrt(jnp.mean(center * center, -1, keepdims=True) + 1e-05)
    return center * rstd, rstd


def norm_back(grad, unit, rstd, gain):
    scaled = grad * gain
    return (
        scaled
        - jnp.mean(scaled, -1, keepdims=True)
        - unit * jnp.mean(scaled * unit, -1, keepdims=True)
    ) * rstd


def col_sum(values):
    return jnp.sum(values, 0, keepdims=True)


def whole(shape):
    zeros = (0,) * len(shape)
    return pl.BlockSpec(shape, lambda *_: zeros, pipeline_mode=pl.Buffered(1))


MIB, SELF_MIB = 54, 46


def cost(us):
    return pl.CostEstimate(flops=int(us * 1.1e9), bytes_accessed=0, transcendentals=0)


def shape_of(shape, kind):
    return jax.ShapeDtypeStruct(shape, kind)


PLACE, SIDE, CROSSES, ORDER = 0, 1, 2, 3


def row_spec(shape, row=None):
    block = (1, *shape[1:])
    rest = (0,) * (len(shape) - 1)
    if row is None:
        return pl.BlockSpec(block, lambda r, *_: (r, *rest))
    return pl.BlockSpec(block, lambda *_: (row, *rest))


def arg_spec(shape, row=None):
    block = (1, *shape[1:])
    rest = (0,) * (len(shape) - 1)
    if row is None:
        return pl.BlockSpec(block, lambda r, segs, info: (info[ORDER + r], *rest))
    return pl.BlockSpec(block, lambda r, segs, info: (info[ORDER + row], *rest))


def call(kernel, name, us, grid, in_specs, out_specs, out_shape, scratch, mib=60, aliases={}):
    return pl.pallas_call(
        kernel,
        grid_spec=pltpu.PrefetchScalarGridSpec(
            num_scalar_prefetch=2, grid=grid, in_specs=in_specs, out_specs=out_specs, scratch_shapes=scratch
        ),
        out_shape=out_shape,
        input_output_aliases=aliases,
        compiler_params=pltpu.CompilerParams(vmem_limit_bytes=mib * 1024 * 1024),
        cost_estimate=pl.CostEstimate(flops=int(us * 1.1e9), bytes_accessed=0, transcendentals=0),
        name=name,
    )


class Fetch:
    def __init__(self, source, ref, sem, index, need=None):
        if index is not None:
            source = source.at[pl.ds(index, 1)]
        self.copy, self.ref, self.need = pltpu.make_async_copy(source, ref, sem), ref, need

    def start(self):
        if self.need is None:
            self.copy.start()
        else:
            pl.when(self.need)(self.copy.start)

    def wait(self):
        if self.need is None:
            self.copy.wait()
        else:
            pl.when(self.need)(self.copy.wait)
        return self.ref


def put_keys(found, vec_ref, shift_v, k_ref, v_ref, kt_ref, vt_ref):
    width = found.shape[1] // 2
    k = found[:, :width]
    v = found[:, width:] + vec_ref[ROW + shift_v : ROW + shift_v + 1, :]
    k_ref[0] = k.astype(BF)
    v_ref[0] = v.astype(BF)
    kt_ref[0] = k.T.astype(BF)
    vt_ref[0] = v.T.astype(BF)


def scaled(queries):
    low = queries.astype(BF).astype(F32)
    return (low * (queries.shape[1] // HEADS) ** -0.5).astype(BF)


def project_kernel(segs, info, tok_ref, mem_ref, wqkv_ref, wckv_ref, vec_ref, q_ref, k_ref, v_ref, kt_ref, vt_ref, ck_ref, cv_ref, ckt_ref, cvt_ref):
    width = tok_ref.shape[2]
    found = nn(tok_ref[0], wqkv_ref[...])
    q_ref[0] = scaled(found[:, :width] + vec_ref[ROW : ROW + 1, :])
    put_keys(found[:, width:], vec_ref, 1, k_ref, v_ref, kt_ref, vt_ref)
    put_keys(nn(mem_ref[0], wckv_ref[...]), vec_ref, 5, ck_ref, cv_ref, ckt_ref, cvt_ref)


def project(segs, info, tokens, memory, wqkv, wckv, vec):
    rows, block, width = tokens.shape
    mem_block = memory.shape[1]
    shapes = [(rows, block, width)] * 3 + [(rows, width, block)] * 2
    shapes += [(rows, mem_block, width)] * 2 + [(rows, width, mem_block)] * 2
    return call(
        project_kernel, "project", 7, (rows,),
        [arg_spec(tokens.shape), arg_spec(memory.shape), whole(wqkv.shape), whole(wckv.shape), whole(vec.shape)],
        [row_spec(s) for s in shapes],
        [shape_of(s, BF) for s in shapes],
        [],
    )(segs, info, tokens, memory, wqkv, wckv, vec)


class Dims:
    def __init__(self, rows, block, key_block, blocks, seq_len, width):
        self.rows, self.block, self.key_block, self.blocks, self.seq_len = rows, block, key_block, blocks, seq_len
        self.width = width
        self.tile = min(256, block)
        self.step = min(256, key_block)


def split_pairs(ref, qoff, dims, keep_ref):
    lane = lax.broadcasted_iota(jnp.int32, (1, 128), 1)
    for h in range(HEADS):
        side = (lane < 64) if h % 2 == 0 else (lane >= 64)
        pair = slice(h // 2 * 128, h // 2 * 128 + 128)
        keep_ref[h] = ref[0, pl.ds(qoff, dims.tile), pair] * side.astype(F32).astype(BF)


def over_tiles(causal, dims, row, segs, info, segq_ref, segk_ref, bias_ref, qin, body):
    tile, step_size = dims.tile, dims.step
    mine, at = info[PLACE], info[ORDER + row]
    qoff = pl.multiple_of(mine * dims.block + qin, tile)
    q_first, q_last = segs[at, qoff], segs[at, qoff + tile - 1]
    keys_all = dims.key_block * dims.blocks
    for source in range(dims.blocks):
        owner = lax.rem(mine + source, dims.blocks)

        def step(kt, carry, source=source, owner=owner):
            inner = pl.multiple_of(kt * step_size, step_size)
            koff = pl.multiple_of(owner * dims.key_block + inner, step_size)
            k_first = segs[at, koff * dims.seq_len // keys_all]
            k_last = segs[at, (koff + step_size - 1) * dims.seq_len // keys_all]
            need = (k_first <= q_last) & (k_last >= q_first)
            if causal:
                need = need & (koff < qoff + tile)

            @pl.when(need)
            def _():
                across = jnp.broadcast_to(segk_ref[0, :, pl.ds(koff, step_size)], (tile, step_size))
                allowed = across.T == segq_ref[0, :, pl.ds(qoff, tile)]
                if causal:
                    kpos = lax.broadcasted_iota(jnp.int32, (step_size, tile), 0) + koff
                    qpos = lax.broadcasted_iota(jnp.int32, (step_size, tile), 1) + qoff
                    allowed = allowed & (kpos <= qpos)
                bias_ref[...] = jnp.where(allowed, 0.0, NEG)
                body(source, inner)

            return carry

        lax.fori_loop(0, dims.key_block // step_size, step, 0)


def far_needed(causal, dims, info, row, source):
    need = info[CROSSES] == 1 if dims.rows == 2 and row == 0 else info[CROSSES] >= 0
    if causal:
        need = need & (lax.rem(info[PLACE] + source, dims.blocks) < info[PLACE])
    return need


def forward_scratch(dims):
    return [
        pltpu.VMEM((HEADS, dims.tile, 128), BF),
        pltpu.VMEM((dims.step, dims.tile), F32),
        pltpu.VMEM((HEADS, dims.tile), F32),
        pltpu.VMEM((HEADS, dims.tile), F32),
        pltpu.VMEM((dims.width, dims.tile), F32),
        pltpu.VMEM((HEADS, dims.step, dims.tile), F32),
        pltpu.VMEM((HEADS, dims.step, dims.tile), BF),
    ]


def forward_tiles(causal, dims, row, segs, info, q_ref, segq_ref, segk_ref, k_refs, vt_refs, att_ref, lse_ref, scratch):
    qm_ref, bias_ref, top_ref, total_ref, acc_ref, score_ref, raised_ref = scratch

    def query_tile(i, carry):
        qin = pl.multiple_of(i * dims.tile, dims.tile)
        queries = pl.ds(qin, dims.tile)
        split_pairs(q_ref, qin, dims, qm_ref)
        top_ref[...] = jnp.full_like(top_ref, NEG)
        total_ref[...] = jnp.zeros_like(total_ref)
        acc_ref[...] = jnp.zeros_like(acc_ref)

        def body(source, inner):
            here = pl.ds(inner, dims.step)
            old = top_ref[...]
            new, fade, more = [], [], []
            for h in range(HEADS):
                pair = slice(h // 2 * 128, h // 2 * 128 + 128)
                scores = nt(k_refs[source][0, here, pair], qm_ref[h]) + bias_ref[...]
                score_ref[h] = scores
                new.append(jnp.maximum(old[h : h + 1, :], jnp.max(scores, 0, keepdims=True)))
                fade.append(jnp.exp(old[h : h + 1, :] - new[h]))
            for h in range(HEADS):
                raised = jnp.exp(score_ref[h] - new[h])
                raised_ref[h] = raised.astype(BF)
                more.append(col_sum(raised))
            for h in range(HEADS):
                heads = slice(h * 64, h * 64 + 64)
                acc_ref[heads, :] = acc_ref[heads, :] * fade[h] + nn(vt_refs[source][0, heads, here], raised_ref[h])
            top_ref[...] = jnp.concatenate(new, 0)
            total_ref[...] = total_ref[...] * jnp.concatenate(fade, 0) + jnp.concatenate(more, 0)

        over_tiles(causal, dims, row, segs, info, segq_ref, segk_ref, bias_ref, qin, body)
        total = total_ref[...]
        lse_ref[0, :, queries] = top_ref[...] + jnp.log(total)
        inverse = 1.0 / total
        for h in range(HEADS):
            heads = slice(h * 64, h * 64 + 64)
            acc_ref[heads, :] = acc_ref[heads, :] * inverse[h : h + 1, :]
        att_ref[0, queries, :] = acc_ref[...].T.astype(BF)
        return carry

    lax.fori_loop(0, dims.block // dims.tile, query_tile, 0)


def forward_kernel(causal, dims, far_count, segs, info, q_ref, segq_ref, segk_ref, base_ref, w_kv_ref, w_out_ref, w_cq_ref, vec_ref, k_ref, vt_ref, *refs):
    far_refs, refs = refs[: far_count * (dims.blocks - 1)], refs[far_count * (dims.blocks - 1) :]
    outs = 5 if causal else 4
    att_ref, lse_ref, unit_ref, rstd_ref = refs[:4]
    far_keys = refs[outs : outs + 4 * (dims.blocks - 1)]
    scratch = refs[outs + 4 * (dims.blocks - 1) :]
    row = pl.program_id(0)
    width = dims.width
    k_refs, vt_refs = [k_ref], [vt_ref]
    at = width if causal else 0
    for source in range(1, dims.blocks):
        keys = far_keys[4 * source - 4 : 4 * source]
        for which in range(far_count):
            ref = far_refs[far_count * (source - 1) + which]
            need = far_needed(causal, dims, info, which if far_count == 2 else 1, source)
            if far_count == 2:
                need = need & (row == which)

            @pl.when(need)
            def _(ref=ref, keys=keys):
                put_keys(nn(ref[0], w_kv_ref[:, at:]), vec_ref, 1 if causal else 5, *keys)

        k_refs.append(keys[0])
        vt_refs.append(keys[3])
    forward_tiles(causal, dims, row, segs, info, q_ref, segq_ref, segk_ref, k_refs, vt_refs, att_ref, lse_ref, scratch)
    base = base_ref[0].astype(F32)
    if not causal:
        base = base * vec_ref[0:1, :] + vec_ref[ROW + 3 : ROW + 4, :]
    shift = ROW + 2 if causal else ROW + 6
    unit, rstd = norm(base + nn(att_ref[0], w_out_ref[...]) + vec_ref[shift : shift + 1, :])
    unit_ref[0] = unit
    rstd_ref[0] = jnp.broadcast_to(rstd, rstd_ref.shape[1:])
    if causal:
        normed = (unit * vec_ref[0:1, :] + vec_ref[ROW + 3 : ROW + 4, :]).astype(BF)
        refs[4][0] = scaled(nn(normed, w_cq_ref[...]) + vec_ref[ROW + 4 : ROW + 5, :])


def attend_forward(causal, segs, info, q, segq, segk, base, w_kv, w_out, w_cq, vec, key, value_t, far):
    rows, block, width = q.shape
    key_block = key.shape[1]
    dims = Dims(rows, block, key_block, len(far) + 1, segs.shape[1], width)
    far_count = len(far[0]) if far else 1
    far_arrays = [a for arrays in far for a in arrays]
    base_spec = arg_spec(base.shape) if causal else row_spec(base.shape)
    far_specs = [row_spec(a.shape) if far_count == 1 else row_spec(a.shape, 0) for a in far_arrays]
    out_shape = [
        shape_of(q.shape, BF),
        shape_of((rows, HEADS, block), F32),
        shape_of(q.shape, F32),
        shape_of((rows, block, 128), F32),
    ] + [shape_of(q.shape, BF)] * causal
    keys = [shape_of((rows, key_block, width), BF)] * 2 + [shape_of((rows, width, key_block), BF)] * 2
    out_shape += keys * len(far)
    return call(
        functools.partial(forward_kernel, causal, dims, far_count),
        "attend_self" if causal else "attend_cross",
        14, (rows,),
        [row_spec(q.shape), arg_spec(segq.shape), arg_spec(segk.shape), base_spec]
        + [whole(w.shape) for w in (w_kv, w_out, w_cq, vec)]
        + [row_spec(key.shape), row_spec(value_t.shape)]
        + far_specs,
        [row_spec(s.shape) for s in out_shape],
        out_shape,
        forward_scratch(dims),
        52,
    )(segs, info, q, segq, segk, base, w_kv, w_out, w_cq, vec, key, value_t, *far_arrays)


def backward_scratch(dims):
    return [
        pltpu.VMEM((HEADS, dims.tile, 128), BF),
        pltpu.VMEM((HEADS, dims.tile, 128), BF),
        pltpu.VMEM((dims.step, dims.tile), F32),
        pltpu.VMEM((dims.width, dims.block), F32),
        pltpu.VMEM((dims.blocks, dims.key_block, dims.width), F32),
        pltpu.VMEM((dims.blocks, dims.key_block, dims.width), F32),
        pltpu.VMEM((HEADS, dims.step, dims.tile), F32),
        pltpu.VMEM((HEADS, dims.step, dims.tile), BF),
        pltpu.VMEM((HEADS, dims.step, dims.tile), BF),
    ]


def backward_tiles(causal, dims, row, segs, info, q_ref, do_ref, lse_ref, dd_ref, segq_ref, segk_ref, k_refs, kt_refs, v_refs, scratch):
    qm_ref, dm_ref, bias_ref, dq_ref, dk_ref, dv_ref, weight_ref, low_ref, ds_ref = scratch
    dk_ref[...] = jnp.zeros_like(dk_ref)
    dv_ref[...] = jnp.zeros_like(dv_ref)
    dq_ref[...] = jnp.zeros_like(dq_ref)

    def query_tile(i, carry):
        qin = pl.multiple_of(i * dims.tile, dims.tile)
        queries = pl.ds(qin, dims.tile)
        split_pairs(q_ref, qin, dims, qm_ref)
        split_pairs(do_ref, qin, dims, dm_ref)

        def body(source, inner):
            here = pl.ds(inner, dims.step)
            lse, dd = lse_ref[0, :, queries], dd_ref[0, :, queries]
            for h in range(HEADS):
                pair = slice(h // 2 * 128, h // 2 * 128 + 128)
                weights = jnp.exp(nt(k_refs[source][0, here, pair], qm_ref[h]) + bias_ref[...] - lse[h : h + 1, :])
                weight_ref[h] = weights
                low_ref[h] = weights.astype(BF)
            for h in range(HEADS):
                pair = slice(h // 2 * 128, h // 2 * 128 + 128)
                grads = nt(v_refs[source][0, here, pair], dm_ref[h])
                ds_ref[h] = (weight_ref[h] * (grads - dd[h : h + 1, :])).astype(BF)
            for h in range(0, HEADS, 2):
                pair = slice(h // 2 * 128, h // 2 * 128 + 128)
                dv_ref[source, here, pair] += nn(low_ref[h], dm_ref[h]) + nn(low_ref[h + 1], dm_ref[h + 1])
                dk_ref[source, here, pair] += nn(ds_ref[h], qm_ref[h]) + nn(ds_ref[h + 1], qm_ref[h + 1])
            for h in range(HEADS):
                heads = slice(h * 64, h * 64 + 64)
                dq_ref[heads, queries] += nn(kt_refs[source][0, heads, here], ds_ref[h])

        over_tiles(causal, dims, row, segs, info, segq_ref, segk_ref, bias_ref, qin, body)
        return carry

    lax.fori_loop(0, dims.block // dims.tile, query_tile, 0)
    return dq_ref[...].T * (dims.width // HEADS) ** -0.5


def head_products(a, b):
    turned = (a.astype(F32) * b.astype(F32)).T
    return jnp.concatenate([col_sum(turned[h * 64 : h * 64 + 64]) for h in range(HEADS)], 0)


def put(buffer, earlier, at, value, first, part):
    done = 0
    while done < value.shape[0]:
        b, inner = divmod(first + done, part)
        count = min(part - inner, value.shape[0] - done)
        rows = slice(at + inner, at + inner + count)
        piece = value[done : done + count]
        if earlier is not None:
            piece = piece + earlier[b, rows, :].astype(F32)
        buffer[b, rows, :] = piece.astype(BF)
        done += count


class Halves:
    def __init__(self, info, buffer, outs, sems):
        self.side, self.buffer, self.outs, self.sems = info[SIDE], buffer, outs, sems
        self.half = buffer.shape[1] // 2

    def each(self, h, what):
        source = self.buffer.at[:, h * self.half : (h + 1) * self.half, :]
        for k, here in enumerate((self.side == h, self.side != h)):
            pl.when(here)(what(pltpu.make_async_copy(source, self.outs[k], self.sems.at[h])))

    def start(self, h):
        self.each(h, lambda copy: copy.start)

    def wait(self):
        for h in range(2):
            self.each(h, lambda copy: copy.wait)


def sum_specs(buffer_shape, last):
    blocks, rows, lanes = buffer_shape
    if last:
        half = shape_of((blocks, rows // 2, lanes), BF)
        return [half] * 2, [pl.BlockSpec(memory_space=pl.ANY)] * 2, [pltpu.VMEM(buffer_shape, BF), pltpu.SemaphoreType.DMA((2,))]
    return [shape_of(buffer_shape, BF)], [whole(buffer_shape)], []


def backward_kernel(causal, dims, row, pickers, has_earlier, has_base, last, segs, info, *refs):
    take = iter(refs)

    def some(count):
        return [next(take) for _ in range(count)]

    blocks, width = dims.blocks, dims.width
    segq_ref, segk_ref, lse_ref, dd_ref, vec_ref, vec_in = some(6)
    sources = some(len(pickers))
    if has_base:
        next(take)
    outs = some((0 if causal else 3) + blocks + (1 if causal else 0))
    vec_out = next(take)
    sum_outs = some(2 if last else 1)
    scratch = some(9)
    acc_ref, buffer, in_sems, out_sems, sum_sems = some(5)
    places = some(len(pickers))
    out_refs = some(len(outs))

    needs = [None] + [far_needed(causal, dims, info, row, source) for source in range(1, blocks)]
    fetches = []
    for k, (source, place, picker) in enumerate(zip(sources, places, pickers)):
        index, of_source = picker
        if index == "arg":
            index = info[ORDER + row]
        fetches.append(Fetch(source, place, in_sems.at[k], index, None if of_source is None else needs[of_source]))
    take = iter(fetches)
    q_get, do_get = some(2)
    own = some(3)
    others = [some(3) for _ in range(1, blocks)]
    x_gets = some(blocks)
    early = 5 + 3 * (blocks - 1)
    for f in fetches[:early]:
        f.start()
    if not causal:
        w_kv_get, unit1_get, rstd1_get, wcq_get, gp2_get, att_get, wso_get = some(7)
    earlier_get = next(take) if has_earlier else None

    leaving = []

    def leave(k):
        out = outs[k]
        if not causal and k == 3:
            out = out.at[pl.ds(info[ORDER + row], 1)]
        leaving.append(pltpu.make_async_copy(out_refs[k], out, out_sems.at[k]))
        leaving[-1].start()

    vec_out[...] = vec_in[...]
    part = width // blocks
    dk_ref, dv_ref = scratch[4:6]
    q_ref, do_ref = q_get.wait(), do_get.wait()
    k_refs, v_refs, kt_refs = zip(*[[g.wait() for g in gets] for gets in (own, *others)])
    for f in fetches[early:]:
        f.start()
    dq = backward_tiles(causal, dims, row, segs, info, q_ref, do_ref, lse_ref, dd_ref, segq_ref, segk_ref, k_refs, kt_refs, v_refs, scratch)
    low_q = dq.astype(BF)
    x_refs = [g.wait() for g in x_gets]
    if causal:
        out_refs[blocks][0] = low_q
        leave(blocks)
        shift_v, first_dx, first = 1, 0, part
    else:
        shift_v, first_dx, first = 5, 3, 2 * part
        w_kv = w_kv_get.wait()

    for source in range(blocks):
        place = out_refs[first_dx + source]

        def back(source=source, place=place):
            x = x_refs[source][0]
            dv = dv_ref[source]
            low = jnp.concatenate([dk_ref[source].astype(BF), dv.astype(BF)], 1)
            vec_out[ROW + shift_v : ROW + shift_v + 1, :] += col_sum(dv)
            if causal:
                place[0] = low
            else:
                place[0] = nt(low, w_kv[...]).astype(place.dtype)
            more = tn(x, low)
            if source == 0:
                acc_ref[...] = more
            else:
                acc_ref[...] += more

        if source == 0:
            back()
        else:
            pl.when(needs[source])(back)

            @pl.when(jnp.logical_not(needs[source]))
            def _(place=place):
                place[...] = jnp.zeros_like(place)

        leave(first_dx + source)

    earlier = earlier_get.wait() if has_earlier else None
    for p in range(2 * width // 512):
        put(buffer, earlier, first + p * part, acc_ref[:, p * 512 : (p + 1) * 512], 0, part)
    if causal:
        vec_out[ROW : ROW + 1, :] += col_sum(dq)
        put(buffer, earlier, 0, tn(x_refs[0][0], low_q), 0, part)
    else:
        unit1 = unit1_get.wait()[0]
        rstd1 = rstd1_get.wait()[0]
        wcq, gp2 = wcq_get.wait(), gp2_get.wait()
        grad = gp2[0] + nt(low_q, wcq[...])
        gp1 = norm_back(grad, unit1, rstd1[:, :1], vec_ref[0:1, :])
        out_refs[0][0] = gp1
        leave(0)
        low_one = gp1.astype(BF)
        att, wso = att_get.wait()[0], wso_get.wait()
        put(buffer, earlier, part, tn(att, low_one), 0, part)
        normed = (unit1 * vec_ref[0:1, :] + vec_ref[ROW + 3 : ROW + 4, :]).astype(BF)
        put(buffer, earlier, 0, tn(normed, low_q), 0, part)
        if not last:
            leaving.append(pltpu.make_async_copy(buffer, sum_outs[0], sum_sems.at[0]))
            leaving[-1].start()
        datt = nt(low_one, wso[...]).astype(BF)
        out_refs[1][0] = datt
        leave(1)
        out_refs[2][0] = head_products(datt, att)
        leave(2)
        vec_out[0:1, :] += col_sum(grad * unit1)
        vec_out[ROW + 2 : ROW + 3, :] += col_sum(gp1)
        vec_out[ROW + 3 : ROW + 4, :] += col_sum(grad)
        vec_out[ROW + 4 : ROW + 5, :] += col_sum(dq)

    if causal and last:
        base = 3 * part * (width // 512)
        buffer[:, base:, :] = jnp.zeros((blocks, buffer.shape[1] - base, 512), BF)
        hidden_part = 4 * 512 // blocks
        for b in range(blocks):
            buffer[b, base : base + UP, :part] = vec_out[:UP, b * part : (b + 1) * part].astype(BF)
            for k in range(max(1, hidden_part // 512)):
                at = b * hidden_part + k * 512
                count = min(512, hidden_part)
                piece = vec_out[UP + at // 512 : UP + at // 512 + 1, at % 512 : at % 512 + count]
                buffer[b, base + UP + k : base + UP + k + 1, :count] = piece.astype(BF)
    if last:
        halves = Halves(info, buffer, sum_outs, sum_sems)
        halves.start(0)
        halves.start(1)
        halves.wait()
    elif causal:
        leaving.append(pltpu.make_async_copy(buffer, sum_outs[0], sum_sems.at[0]))
        leaving[-1].start()
    for c in leaving:
        c.wait()


def attend_backward(causal, row, last, us, segs, info, q, segq, segk, d_out, lse, dd, vec, vec_in, keys, keys_t, values, inputs, w_kv, extra, earlier, base):
    rows, block, width = q.shape
    blocks, key_block = len(keys), keys[0].shape[1]
    dims = Dims(rows, block, key_block, blocks, segs.shape[1], width)

    def at(a):
        return row if a.shape[0] == rows else 0

    def spec(a):
        return row_spec(a.shape, at(a))

    small = [segq, segk, lse, dd, vec, vec_in]
    small_specs = [arg_spec(segq.shape, row), arg_spec(segk.shape, row), spec(lse), spec(dd), whole(vec.shape), whole(vec_in.shape)]
    large = [(q, (row, None)), (d_out, (at(d_out), None))]
    for s in range(blocks):
        large += [(a[s], (row, None if s == 0 else s)) for a in (keys, values, keys_t)]
    large += [(a, ("arg" if s == 0 else at(a), None if s == 0 else s)) for s, a in enumerate(inputs)]
    if not causal:
        gp2, unit1, rstd1, att, wcq, wso = extra
        large += [(w_kv, (None, None)), (unit1, (row, None)), (rstd1, (row, None)), (wcq, (None, None))]
        large += [(gp2, (row, None)), (att, (row, None)), (wso, (None, None))]
    if earlier is not None:
        large.append((earlier, (None, None)))
    out_shape = []
    if not causal:
        out_shape += [shape_of((1, block, width), F32), shape_of((1, block, width), BF), shape_of((1, HEADS, block), F32)]
    if causal:
        out_shape += [shape_of((1, key_block, 2 * width), BF) for s in range(blocks)] + [shape_of((1, block, width), BF)]
    else:
        out_shape += [shape_of((1, key_block, width), F32 if s == 0 else BF) for s in range(blocks)]
    vec_shape = shape_of((VROWS, width), F32)
    buffer_rows = (3 if causal else 4) * width // blocks * (width // 512) + (VECTOR_ROWS if causal and last else 0)
    buffer_shape = (blocks, buffer_rows, 512)
    sum_shapes = [shape_of((blocks, buffer_rows // 2, 512), BF)] * 2 if last else [shape_of(buffer_shape, BF)]
    anywhere = pl.BlockSpec(memory_space=pl.ANY)
    out_places = [pltpu.VMEM(s.shape, s.dtype) for s in out_shape]
    if not causal:
        out_shape[3] = shape_of((rows, key_block, width), F32)
    bases = [] if base is None else [base]
    aliases = {2 + len(small) + len(large): 3} if bases else {}
    places = [pltpu.VMEM(a.shape if p[0] is None else (1, *a.shape[1:]), a.dtype) for a, p in large]
    return call(
        functools.partial(backward_kernel, causal, dims, row, [p for _, p in large], earlier is not None, base is not None, last),
        "attend_self_back" if causal else "attend_cross_back",
        us, (1,),
        small_specs + [anywhere] * (len(large) + len(bases)),
        [anywhere] * len(out_shape) + [whole(vec_shape.shape)] + [anywhere] * len(sum_shapes),
        out_shape + [vec_shape] + sum_shapes,
        backward_scratch(dims)
        + [
            pltpu.VMEM((width, 2 * width), F32),
            pltpu.VMEM(buffer_shape, BF),
            pltpu.SemaphoreType.DMA((len(large),)),
            pltpu.SemaphoreType.DMA((len(out_shape),)),
            pltpu.SemaphoreType.DMA((2,)),
        ]
        + places
        + out_places,
        SELF_MIB if causal else MIB,
        aliases,
    )(segs, info, *small, *[a for a, _ in large], *bases)


def tokens_back_kernel(rows, blocks, segs, info, *refs):
    take = iter(refs)
    per_row = [[next(take) for _ in range(2 + blocks)] for _ in range(rows)]
    w_ref, base_out = next(take), next(take)
    outs = [[next(take) for _ in range(1, blocks)] for _ in range(rows)]
    width = w_ref.shape[0]
    for r, (dq_ref, base_ref, *dkv_refs) in enumerate(per_row):
        for source in range(blocks):
            grad = nt(dkv_refs[source][0], w_ref[:, width:])
            if source == 0:
                base_out[info[ORDER + r]] = grad + nt(dq_ref[0], w_ref[:, :width]) + base_ref[0]
            else:
                outs[r][source - 1][0] = grad.astype(BF)


def tokens_back(segs, info, found, gp1, w):
    rows, blocks = len(found), len(found[0]) - 1
    args = []
    for (*dkv, dq), base in zip(found, gp1):
        args += [dq, base, *dkv]
    args.append(w)
    block = gp1[0].shape[1:]
    out_shape = [shape_of((rows, *block), F32)] + [shape_of((1, *block), BF)] * (rows * (blocks - 1))
    base, *got = call(
        functools.partial(tokens_back_kernel, rows, blocks), "tokens_back", 8, (1,),
        [whole(a.shape) for a in args], [whole(s.shape) for s in out_shape], out_shape, [], SELF_MIB,
    )(segs, info, *args)
    return base, *[got[r * (blocks - 1) : (r + 1) * (blocks - 1)] for r in range(rows)]


def feed_kernel(dims, far_count, segs, info, q_ref, segq_ref, segk_ref, unit1_ref, cot_ref, upshift_ref, vec_ref, k_ref, vt_ref, wckv_ref, wco_ref, wup_any, wdown_any, *refs):
    take = iter(refs)

    def some(count):
        return [next(take) for _ in range(count)]

    blocks = dims.blocks
    far_refs = some(far_count * (blocks - 1))
    lse_ref, out_ref, gp2_ref, dco_ref, dcross_ref, vec_out, keep_ref, send_ref = some(8)
    far_keys = [some(3) for _ in range(1, blocks)]
    hid_ref, slope_ref, low_up_ref, normed_ref, low3_ref, co_all_ref, low2_ref, buffer, sems = some(9)
    wup_ref, wdown_ref, w_sems, att_ref = some(4)
    far_vt = some(blocks - 1)
    scratch = some(7)
    width, hidden_width = wup_ref.shape
    panels = hidden_width // 512
    block = dims.block
    row = pl.program_id(0)
    here = pl.ds(pl.multiple_of(row * block, block), block)
    weights = [pltpu.make_async_copy(wup_any, wup_ref, w_sems.at[0]), pltpu.make_async_copy(wdown_any, wdown_ref, w_sems.at[1])]

    @pl.when(row == 0)
    def _():
        vec_out[...] = jnp.zeros_like(vec_out)
        for w in weights:
            w.start()

    k_refs, vt_refs = [k_ref], [vt_ref]
    for source in range(1, blocks):
        keys = (*far_keys[source - 1], far_vt[source - 1])
        for which in range(far_count):
            ref = far_refs[far_count * (source - 1) + which]
            need = far_needed(False, dims, info, which if far_count == 2 else 1, source)
            if far_count == 2:
                need = need & (row == which)

            @pl.when(need)
            def _(ref=ref, keys=keys):
                put_keys(nn(ref[0], wckv_ref[...]), vec_ref, 5, *keys)

        k_refs.append(keys[0])
        vt_refs.append(keys[3])
    forward_tiles(False, dims, row, segs, info, q_ref, segq_ref, segk_ref, k_refs, vt_refs, att_ref, lse_ref, scratch)
    co = att_ref[0]
    co_all_ref[here, :] = co
    normed_one = unit1_ref[0] * vec_ref[0:1, :] + vec_ref[ROW + 3 : ROW + 4, :]
    unit2, rstd2 = norm(normed_one + nn(co, wco_ref[...]) + vec_ref[ROW + 6 : ROW + 7, :])

    @pl.when(row == 0)
    def _():
        for w in weights:
            w.wait()

    normed = unit2 * vec_ref[1:2, :] + vec_ref[ROW + 7 : ROW + 8, :]
    normed_low = normed.astype(BF)
    normed_ref[here, :] = normed_low
    for p in range(panels):
        cols = slice(p * 512, (p + 1) * 512)
        up = nn(normed_low, wup_ref[:, cols]) + upshift_ref[p : p + 1, :]
        square = up * up
        bent = jnp.tanh(up * (GELU_A + GELU_B * square))
        half = 0.5 * up
        hid_ref[here, cols] = (half + half * bent).astype(BF)
        slope_ref[:, cols] = 0.5 + 0.5 * bent + half * (1.0 - bent * bent) * (GELU_A + 3 * GELU_B * square)
    pre = normed + nn(hid_ref[here, :], wdown_ref[...]) + vec_ref[ROW + 8 : ROW + 9, :]
    unit3, rstd3 = norm(pre)
    out_ref[0] = (unit3 * vec_ref[2:3, :] + vec_ref[ROW + 9 : ROW + 10, :]).astype(BF)
    cot = cot_ref[0].astype(F32)
    gp3 = norm_back(cot, unit3, rstd3, vec_ref[2:3, :])
    low3 = gp3.astype(BF)
    low3_ref[here, :] = low3
    vec_out[2:3, :] += col_sum(cot * unit3)
    vec_out[ROW + 8 : ROW + 9, :] += col_sum(gp3)
    vec_out[ROW + 9 : ROW + 10, :] += col_sum(cot)
    for p in range(panels):
        cols = slice(p * 512, (p + 1) * 512)
        grad_up = nt(low3, wdown_ref[cols, :]) * slope_ref[:, cols]
        low_up_ref[here, cols] = grad_up.astype(BF)
        vec_out[UP + p : UP + p + 1, :] += col_sum(grad_up)
    grad = gp3 + nt(low_up_ref[here, :], wup_ref[...])
    gp2 = norm_back(grad, unit2, rstd2, vec_ref[1:2, :])
    gp2_ref[0] = gp2
    low2 = gp2.astype(BF)
    low2_ref[here, :] = low2
    dco = nt(low2, wco_ref[...]).astype(BF)
    dco_ref[0] = dco
    dcross_ref[0] = head_products(dco, co)
    vec_out[1:2, :] += col_sum(grad * unit2)
    vec_out[ROW + 6 : ROW + 7, :] += col_sum(gp2)
    vec_out[ROW + 7 : ROW + 8, :] += col_sum(grad)

    @pl.when(row == pl.num_programs(0) - 1)
    def _():
        down, part = hidden_width // blocks, width // blocks
        halves = Halves(info, buffer, (keep_ref, send_ref), sems)
        started = False
        for p in range(panels):
            cols = slice(p * 512, (p + 1) * 512)
            put(buffer, None, 0, tn(hid_ref[:, cols], low3_ref[...]), p * 512, down)
        for p in range(panels):
            cols = slice(p * 512, (p + 1) * 512)
            put(buffer, None, down + p * part, tn(normed_ref[...], low_up_ref[:, cols]), 0, part)
            if not started and down + (p + 1) * part >= halves.half:
                halves.start(0)
                started = True
        put(buffer, None, down + panels * part, tn(co_all_ref[...], low2_ref[...]), 0, part)
        halves.start(1)
        halves.wait()


def feed(segs, info, q, segq, segk, unit1, cot, up_rows, vec, key, value_t, wckv, wco, wup, wdown, far):
    rows, block, width = unit1.shape
    hidden = wup.shape[1]
    tokens = rows * block
    key_block = key.shape[1]
    blocks = len(far) + 1
    dims = Dims(rows, block, key_block, blocks, segs.shape[1], width)
    far_count = len(far[0]) if far else 1
    far_arrays = [a for arrays in far for a in arrays]
    far_specs = [row_spec(a.shape) if far_count == 1 else row_spec(a.shape, 0) for a in far_arrays]
    buffer_shape = (blocks, (2 * hidden + width) // blocks, width)
    shapes, specs, more = sum_specs(buffer_shape, True)
    rest = [
        shape_of(unit1.shape, BF),
        shape_of(unit1.shape, F32),
        shape_of(unit1.shape, BF),
        shape_of((rows, HEADS, block), F32),
    ]
    lse_shape, vec_shape = shape_of((rows, HEADS, block), F32), shape_of((VROWS, width), F32)
    keys = ([shape_of((rows, key_block, width), BF)] * 2 + [shape_of((rows, width, key_block), BF)]) * (blocks - 1)
    anywhere = pl.BlockSpec(memory_space=pl.ANY)
    return call(
        functools.partial(feed_kernel, dims, far_count), "attend_cross_feed", 40, (rows,),
        [row_spec(q.shape), arg_spec(segq.shape), arg_spec(segk.shape), row_spec(unit1.shape), arg_spec(cot.shape)]
        + [whole(up_rows.shape), whole(vec.shape), row_spec(key.shape), row_spec(value_t.shape)]
        + [whole(wckv.shape), whole(wco.shape), anywhere, anywhere]
        + far_specs,
        [row_spec(lse_shape.shape), arg_spec(unit1.shape)]
        + [row_spec(s.shape) for s in rest[1:]]
        + [whole(vec_shape.shape)]
        + specs
        + [row_spec(s.shape) for s in keys],
        [lse_shape] + rest + [vec_shape] + shapes + keys,
        [
            pltpu.VMEM((tokens, hidden), BF),
            pltpu.VMEM((block, hidden), F32),
            pltpu.VMEM((tokens, hidden), BF),
            pltpu.VMEM((tokens, width), BF),
            pltpu.VMEM((tokens, width), BF),
            pltpu.VMEM((tokens, width), BF),
            pltpu.VMEM((tokens, width), BF),
        ]
        + more
        + [pltpu.VMEM(wup.shape, BF), pltpu.VMEM(wdown.shape, BF), pltpu.SemaphoreType.DMA((2,)), pltpu.VMEM((1, block, width), BF)]
        + [pltpu.VMEM((1, width, key_block), BF)] * (blocks - 1)
        + forward_scratch(dims),
        60,
    )(segs, info, q, segq, segk, unit1, cot, up_rows, vec, key, value_t, wckv, wco, wup, wdown, *far_arrays)


def bits(size):
    return size.bit_length() - 1


def all_pairs(mask):
    return [(i, i ^ mask) for i in range(lax.axis_size("dp") * lax.axis_size("blk"))]


def swap(values, mask):
    return lax.ppermute(values, ("dp", "blk"), all_pairs(mask))


def place():
    return lax.axis_index("dp") * lax.axis_size("blk") + lax.axis_index("blk")


def by_place(parts, at, count):
    for bit in range(count):
        side = ((at >> bit) & 1) == 1
        parts = [jnp.where(side, parts[j ^ (1 << bit)], parts[j]) for j in range(len(parts))]
    return parts


class Sum:
    def __init__(self, keep, send, urgent):
        self.values = [keep, send]
        self.near = bits(lax.axis_size("blk"))
        self.far = bits(lax.axis_size("dp")) - 2
        far = [self.far_gather] if urgent else [functools.partial(self.pair_gather, bit) for bit in reversed(range(self.far))]
        self.steps = [self.core, self.near_scatter, self.far_scatter, *far, self.near_gather, self.core_gather]

    def step(self):
        if self.steps:
            self.values = self.steps.pop(0)(*self.values)

    def core(self, keep, send):
        return [(keep.astype(F32) + swap(send, 1 << self.near).astype(F32)).astype(BF)]

    def near_scatter(self, now):
        blocks = now.shape[0]
        cut = now.reshape(blocks, 2, now.shape[1] // 2, now.shape[2])
        mine, side = lax.axis_index("blk"), (lax.axis_index("dp") >> 1) & 1

        def piece(b, s):
            return lax.dynamic_slice(cut, (mine ^ b, side ^ s, 0, 0), (1, 1, *cut.shape[2:]))[0, 0]

        total = piece(0, 0).astype(F32)
        for s in range(2):
            for b in range(blocks):
                if s or b:
                    total = total + swap(piece(b, s), (2 * s << self.near) | b).astype(F32)
        return [total.astype(BF)]

    def far_scatter(self, now):
        at = lax.axis_index("dp") >> 2
        cut = now.reshape(1 << self.far, -1, now.shape[1])
        total = lax.dynamic_index_in_dim(cut, at, 0, False).astype(F32)
        for k in range(1, 1 << self.far):
            piece = lax.dynamic_index_in_dim(cut, at ^ k, 0, False)
            total = total + swap(piece, (k << 2) << self.near).astype(F32)
        return [total.astype(BF)]

    def far_gather(self, now):
        at = lax.axis_index("dp") >> 2
        parts = [now] + [swap(now, (k << 2) << self.near) for k in range(1, 1 << self.far)]
        return [jnp.concatenate(by_place(parts, at, self.far), 0)]

    def pair_gather(self, bit, now):
        side = lax.axis_index("dp") >> 2 >> bit
        chunk = now.shape[0] >> (self.far - 1 - bit)
        parts = [p.reshape(-1, 1, chunk, now.shape[1]) for p in (now, swap(now, (4 << bit) << self.near))]
        return [jnp.concatenate(by_place(parts, side, 1), 1).reshape(-1, now.shape[1])]

    def near_gather(self, now):
        at = (lax.axis_index("dp") >> 1) & 1
        return [jnp.concatenate(by_place([now, swap(now, 2 << self.near)], at, 1), 0)]

    def core_gather(self, now):
        return [now, swap(now, 1 << self.near)]

    def rows(self):
        return jnp.concatenate(by_place(self.values, lax.axis_index("dp") & 1, 1), 0)


def advance(sums, anchor, begun=()):
    for s in sums:
        s.step()
    sums = [*sums, *begun]
    flat, anchor = lax.optimization_barrier(([s.values for s in sums], anchor))
    for s, values in zip(sums, flat):
        s.values = values
    return anchor


def from_next(values, step):
    size = lax.axis_size("blk")
    return lax.ppermute(values, "blk", [((i + step) % size, i) for i in range(size)])


def to_next(values, step):
    size = lax.axis_size("blk")
    return lax.ppermute(values, "blk", [(i, (i + step) % size) for i in range(size)])


def unpanel(part, columns):
    panels = columns // 512
    rows = part.shape[0] // panels
    return jnp.concatenate([part[p * rows : (p + 1) * rows] for p in range(panels)], 1).astype(F32)


def body(tokens, memory, segments, w_qkv, w_self_out, w_cross_q, w_cross_kv, w_cross_out, w_up, w_down, norm_gains, shifts, up_shift, cotangent):
    rows, block, width = tokens.shape
    mem_block = memory.shape[1]
    blocks = lax.axis_size("blk")
    mine = lax.axis_index("blk")
    seq_len = segments.shape[1]
    mem_len = mem_block * blocks
    hidden = w_up.shape[1]
    far = range(1, blocks)

    pick = rows == 2
    if pick:
        single = (segments[0, -1] != 0).astype(jnp.int32)
        order = jnp.stack([1 - single, single])
        edges = np.arange(1, blocks) * block
        crosses = jnp.any((segments[:, edges - 1] == segments[:, edges]) & (jnp.arange(2) != single)[:, None])
    else:
        order, crosses = jnp.arange(rows), jnp.array(True)
    head = jnp.stack([mine, lax.axis_index("dp") & 1, crosses.astype(jnp.int32)])
    info = jnp.concatenate([head, order]).astype(jnp.int32)

    def fetch(arrays):
        if not pick:
            return [[[from_next(a, k)] for k in far] for a in arrays]
        ones = [[from_next(lax.dynamic_index_in_dim(a, single, 0, True), k) for k in far] for a in arrays]
        others = [lax.dynamic_index_in_dim(a, 1 - single, 0, True) for a in arrays]
        others = lax.cond(
            crosses,
            lambda vs: [[from_next(v, k) for k in far] for v in vs],
            lambda vs: [[v for _ in far] for v in vs],
            others,
        )
        return [[[o, g] for o, g in zip(*pair)] for pair in zip(others, ones)]

    far_toks, far_mems = fetch([tokens, memory])

    vec = jnp.concatenate([norm_gains.T, shifts.T, jnp.zeros((3, width), F32)], 0)
    up_rows = up_shift.reshape(-1, 512)
    seg_rows = segments.astype(F32)[:, None, :]
    mem_seg = seg_rows[:, :, np.arange(mem_len) * seq_len // mem_len] if mem_len != seq_len else seg_rows

    q, k, v, kt, vt, ck, cv, ckt, cvt = project(segments, info, tokens, memory, w_qkv, w_cross_kv, vec)
    att, lse1, unit1, rstd1, cq, *keys = attend_forward(
        True, segments, info, q, seg_rows, seg_rows, tokens, w_qkv, w_self_out, w_cross_q, vec, k, vt, far_toks
    )
    k1, v1, kt1 = [[own] + keys[at::4] for at, own in enumerate((k, v, kt))]
    lse2, out, gp2, dco, dd2, vectors, keep, send, *keys = feed(
        segments, info, cq, seg_rows, mem_seg, unit1, cotangent, up_rows, vec, ck, cvt, w_cross_kv, w_cross_out, w_up, w_down, far_mems
    )
    k2, v2, kt2 = [[own] + keys[at::3] for at, own in enumerate((ck, cv, ckt))]
    sums = [Sum(keep, send, False)]

    def far_of(found, r):
        return [f[r] if len(f) > 1 else f[0] for f in found]

    def give(found):
        if not pick:
            return [[to_next(o, k) for k, o in zip(far, others)] for others in found]
        others, ones = found
        got = [to_next(o, k) for k, o in zip(far, ones)]
        more = lax.cond(
            crosses,
            lambda vs: [to_next(o, k) for k, o in zip(far, vs)],
            lambda vs: list(vs),
            list(others),
        )
        return [more, got]

    def total(base, got):
        if pick:
            is_one = (jnp.arange(2) == single)[:, None, None]
            parts = [jnp.where(is_one, one, other) for other, one in zip(*got)]
        else:
            parts = [jnp.concatenate([row[k] for row in got], 0) for k in range(blocks - 1)]
        return functools.reduce(lambda a, b: a + b.astype(F32), parts, base)

    earlier, rows_gp1, dmem, memory_base = None, [], [], None
    for r in range(rows):
        last = r == rows - 1
        gp1, datt, dd1, *rest = attend_backward(
            False, r, last, 24 if last else 14, segments, info, cq, seg_rows, mem_seg, dco, lse2, dd2, vec, vectors,
            k2, kt2, v2, [memory] + far_of(far_mems, r), w_cross_kv,
            [gp2, unit1, rstd1, att, w_cross_q, w_self_out], earlier, memory_base,
        )
        memory_base = rest[0]
        dmem.append(rest[1:blocks])
        vectors, earlier = rest[blocks], rest[-1]
        rows_gp1.append((gp1, datt, dd1))
        vectors = advance(sums, vectors)
    sums.append(Sum(*rest[-2:], False))
    got_mem = give(dmem)
    earlier, dkv = None, []
    for r in range(rows):
        last = r == rows - 1
        _, datt, dd1 = rows_gp1[r]
        rest = attend_backward(
            True, r, last, 14 if last else 11, segments, info, q, seg_rows, seg_rows, datt, lse1, dd1, vec, vectors,
            k1, kt1, v1, [tokens] + far_of(far_toks, r), None, [], earlier, None,
        )
        dkv.append(rest[: blocks + 1])
        vectors, earlier = rest[blocks + 1], rest[-1]
        if not last:
            vectors, got_mem = advance(sums, (vectors, got_mem))
    dkv = advance(sums, dkv)
    sums.append(Sum(*rest[-2:], True))
    tokens_base, *dtok = tokens_back(segments, info, dkv, [g[0] for g in rows_gp1], w_qkv)
    first, second, third = sums
    dtok = advance(sums, dtok)

    part, hidden_part = width // blocks, hidden // blocks
    dtok, got_mem = advance([second, third], (dtok, got_mem))
    got_tok = give(dtok)
    first.step()
    got_mem = advance([second, third], got_mem)
    got_mem = advance([second, third], got_mem, [first])
    while first.steps:
        first.step()
    up_at = hidden_part + (hidden // 512) * part
    feed_sum = first.rows()
    found = (
        total(memory_base, got_mem),
        feed_sum[up_at:].astype(F32),
        unpanel(feed_sum[hidden_part:up_at], hidden),
        feed_sum[:hidden_part].astype(F32),
    )
    (grad_memory, grad_cross_out, grad_up, grad_down), got_tok = advance([second, third], (found, got_tok))
    while second.steps:
        second.step()
    other_sum = second.rows()
    found = (
        total(tokens_base, got_tok),
        other_sum[part : 2 * part].astype(F32),
        other_sum[:part].astype(F32),
        unpanel(other_sum[2 * part :], 2 * width),
    )
    grad_tokens, grad_self_out, grad_cross_q, grad_cross_kv = advance([third], found)
    while third.steps:
        third.step()
    qkv_sum = third.rows()
    qkv_rows = 3 * part * (width // 512)
    vectors = qkv_sum[qkv_rows:].astype(F32)
    return (
        out,
        grad_tokens,
        grad_memory,
        unpanel(qkv_sum[:qkv_rows], 3 * width),
        grad_self_out,
        grad_cross_q,
        grad_cross_kv,
        grad_cross_out,
        grad_up,
        grad_down,
        vectors[:ROW, :part].T,
        vectors[ROW:UP, :part].T,
        vectors[UP : UP + max(1, hidden_part // 512), : min(512, hidden_part)].reshape(-1),
    )


def solution(mesh):
    split = P("dp", "blk", None)
    in_specs = (split, split, P("dp", None)) + (P(),) * 10 + (split,)
    out_specs = (split,) * 3 + (P("blk", None),) * 9 + (P("blk"),)
    return jax.shard_map(body, mesh=mesh, in_specs=in_specs, out_specs=out_specs, check_vma=False)
```

```python
import functools

import jax
import jax.numpy as jnp
import numpy as np
from jax import lax
from jax.experimental import pallas as pl
from jax.experimental.pallas import tpu as pltpu
from jax.sharding import PartitionSpec as P

HEADS = 8
NEG = -1e30
F32 = jnp.float32
BF = jnp.bfloat16
GELU_A = 0.7978845608028654
GELU_B = 0.7978845608028654 * 0.044715
ROW = 3
UP = 13
VROWS = 24
VECTOR_ROWS = 128


def nn(a, b):
    return jnp.dot(a, b, preferred_element_type=F32)


def nt(a, b):
    return lax.dot_general(a, b, (((1,), (1,)), ((), ())), preferred_element_type=F32)


def tn(a, b):
    return lax.dot_general(a, b, (((0,), (0,)), ((), ())), preferred_element_type=F32)


def norm(values):
    center = values - jnp.mean(values, -1, keepdims=True)
    rstd = lax.rsqrt(jnp.mean(center * center, -1, keepdims=True) + 1e-05)
    return center * rstd, rstd


def norm_back(grad, unit, rstd, gain):
    scaled = grad * gain
    return (
        scaled
        - jnp.mean(scaled, -1, keepdims=True)
        - unit * jnp.mean(scaled * unit, -1, keepdims=True)
    ) * rstd


def col_sum(values):
    return jnp.sum(values, 0, keepdims=True)


def whole(shape):
    zeros = (0,) * len(shape)
    return pl.BlockSpec(shape, lambda *_: zeros, pipeline_mode=pl.Buffered(1))


MIB, SELF_MIB = 54, 46


def cost(us):
    return pl.CostEstimate(flops=int(us * 1.1e9), bytes_accessed=0, transcendentals=0)


def shape_of(shape, kind):
    return jax.ShapeDtypeStruct(shape, kind)


PLACE, SIDE, CROSSES, ORDER = 0, 1, 2, 3


def row_spec(shape, row=None):
    block = (1, *shape[1:])
    rest = (0,) * (len(shape) - 1)
    if row is None:
        return pl.BlockSpec(block, lambda r, *_: (r, *rest))
    return pl.BlockSpec(block, lambda *_: (row, *rest))


def arg_spec(shape, row=None):
    block = (1, *shape[1:])
    rest = (0,) * (len(shape) - 1)
    if row is None:
        return pl.BlockSpec(block, lambda r, segs, info: (info[ORDER + r], *rest))
    return pl.BlockSpec(block, lambda r, segs, info: (info[ORDER + row], *rest))


def call(kernel, name, us, grid, in_specs, out_specs, out_shape, scratch, mib=60, aliases={}):
    return pl.pallas_call(
        kernel,
        grid_spec=pltpu.PrefetchScalarGridSpec(
            num_scalar_prefetch=2, grid=grid, in_specs=in_specs, out_specs=out_specs, scratch_shapes=scratch
        ),
        out_shape=out_shape,
        input_output_aliases=aliases,
        compiler_params=pltpu.CompilerParams(vmem_limit_bytes=mib * 1024 * 1024),
        cost_estimate=pl.CostEstimate(flops=int(us * 1.1e9), bytes_accessed=0, transcendentals=0),
        name=name,
    )


class Fetch:
    def __init__(self, source, ref, sem, index, need=None):
        if index is not None:
            source = source.at[pl.ds(index, 1)]
        self.copy, self.ref, self.need = pltpu.make_async_copy(source, ref, sem), ref, need

    def start(self):
        if self.need is None:
            self.copy.start()
        else:
            pl.when(self.need)(self.copy.start)

    def wait(self):
        if self.need is None:
            self.copy.wait()
        else:
            pl.when(self.need)(self.copy.wait)
        return self.ref


def put_keys(found, vec_ref, shift_v, k_ref, v_ref, kt_ref, vt_ref):
    width = found.shape[1] // 2
    k = found[:, :width]
    v = found[:, width:] + vec_ref[ROW + shift_v : ROW + shift_v + 1, :]
    k_ref[0] = k.astype(BF)
    v_ref[0] = v.astype(BF)
    kt_ref[0] = k.T.astype(BF)
    vt_ref[0] = v.T.astype(BF)


def scaled(queries):
    low = queries.astype(BF).astype(F32)
    return (low * (queries.shape[1] // HEADS) ** -0.5).astype(BF)


def project_kernel(segs, info, tok_ref, mem_ref, wqkv_ref, wckv_ref, vec_ref, q_ref, k_ref, v_ref, kt_ref, vt_ref, ck_ref, cv_ref, ckt_ref, cvt_ref):
    width = tok_ref.shape[2]
    found = nn(tok_ref[0], wqkv_ref[...])
    q_ref[0] = scaled(found[:, :width] + vec_ref[ROW : ROW + 1, :])
    put_keys(found[:, width:], vec_ref, 1, k_ref, v_ref, kt_ref, vt_ref)
    put_keys(nn(mem_ref[0], wckv_ref[...]), vec_ref, 5, ck_ref, cv_ref, ckt_ref, cvt_ref)


def project(segs, info, tokens, memory, wqkv, wckv, vec):
    rows, block, width = tokens.shape
    mem_block = memory.shape[1]
    shapes = [(rows, block, width)] * 3 + [(rows, width, block)] * 2
    shapes += [(rows, mem_block, width)] * 2 + [(rows, width, mem_block)] * 2
    return call(
        project_kernel, "project", 7, (rows,),
        [arg_spec(tokens.shape), arg_spec(memory.shape), whole(wqkv.shape), whole(wckv.shape), whole(vec.shape)],
        [row_spec(s) for s in shapes],
        [shape_of(s, BF) for s in shapes],
        [],
    )(segs, info, tokens, memory, wqkv, wckv, vec)


class Dims:
    def __init__(self, rows, block, key_block, blocks, seq_len, width):
        self.rows, self.block, self.key_block, self.blocks, self.seq_len = rows, block, key_block, blocks, seq_len
        self.width = width
        self.tile = min(256, block)
        self.step = min(256, key_block)


def split_pairs(ref, qoff, dims, keep_ref):
    lane = lax.broadcasted_iota(jnp.int32, (1, 128), 1)
    for h in range(HEADS):
        side = (lane < 64) if h % 2 == 0 else (lane >= 64)
        pair = slice(h // 2 * 128, h // 2 * 128 + 128)
        keep_ref[h] = ref[0, pl.ds(qoff, dims.tile), pair] * side.astype(F32).astype(BF)


def over_tiles(causal, dims, row, segs, info, segq_ref, segk_ref, bias_ref, qin, body):
    tile, step_size = dims.tile, dims.step
    mine, at = info[PLACE], info[ORDER + row]
    qoff = pl.multiple_of(mine * dims.block + qin, tile)
    q_first, q_last = segs[at, qoff], segs[at, qoff + tile - 1]
    keys_all = dims.key_block * dims.blocks
    for source in range(dims.blocks):
        owner = lax.rem(mine + source, dims.blocks)

        def step(kt, carry, source=source, owner=owner):
            inner = pl.multiple_of(kt * step_size, step_size)
            koff = pl.multiple_of(owner * dims.key_block + inner, step_size)
            k_first = segs[at, koff * dims.seq_len // keys_all]
            k_last = segs[at, (koff + step_size - 1) * dims.seq_len // keys_all]
            need = (k_first <= q_last) & (k_last >= q_first)
            if causal:
                need = need & (koff < qoff + tile)

            @pl.when(need)
            def _():
                across = jnp.broadcast_to(segk_ref[0, :, pl.ds(koff, step_size)], (tile, step_size))
                allowed = across.T == segq_ref[0, :, pl.ds(qoff, tile)]
                if causal:
                    kpos = lax.broadcasted_iota(jnp.int32, (step_size, tile), 0) + koff
                    qpos = lax.broadcasted_iota(jnp.int32, (step_size, tile), 1) + qoff
                    allowed = allowed & (kpos <= qpos)
                bias_ref[...] = jnp.where(allowed, 0.0, NEG)
                body(source, inner)

            return carry

        lax.fori_loop(0, dims.key_block // step_size, step, 0)


def far_needed(causal, dims, info, row, source):
    need = info[CROSSES] == 1 if dims.rows == 2 and row == 0 else info[CROSSES] >= 0
    if causal:
        need = need & (lax.rem(info[PLACE] + source, dims.blocks) < info[PLACE])
    return need


def forward_scratch(dims):
    return [
        pltpu.VMEM((HEADS, dims.tile, 128), BF),
        pltpu.VMEM((dims.step, dims.tile), F32),
        pltpu.VMEM((HEADS, dims.tile), F32),
        pltpu.VMEM((HEADS, dims.tile), F32),
        pltpu.VMEM((dims.width, dims.tile), F32),
        pltpu.VMEM((HEADS, dims.step, dims.tile), F32),
        pltpu.VMEM((HEADS, dims.step, dims.tile), BF),
    ]


def forward_tiles(causal, dims, row, segs, info, q_ref, segq_ref, segk_ref, k_refs, vt_refs, att_ref, lse_ref, scratch):
    qm_ref, bias_ref, top_ref, total_ref, acc_ref, score_ref, raised_ref = scratch

    def query_tile(i, carry):
        qin = pl.multiple_of(i * dims.tile, dims.tile)
        queries = pl.ds(qin, dims.tile)
        split_pairs(q_ref, qin, dims, qm_ref)
        top_ref[...] = jnp.full_like(top_ref, NEG)
        total_ref[...] = jnp.zeros_like(total_ref)
        acc_ref[...] = jnp.zeros_like(acc_ref)

        def body(source, inner):
            here = pl.ds(inner, dims.step)
            old = top_ref[...]
            new, fade, more = [], [], []
            for h in range(HEADS):
                pair = slice(h // 2 * 128, h // 2 * 128 + 128)
                scores = nt(k_refs[source][0, here, pair], qm_ref[h]) + bias_ref[...]
                score_ref[h] = scores
                new.append(jnp.maximum(old[h : h + 1, :], jnp.max(scores, 0, keepdims=True)))
                fade.append(jnp.exp(old[h : h + 1, :] - new[h]))
            for h in range(HEADS):
                raised = jnp.exp(score_ref[h] - new[h])
                raised_ref[h] = raised.astype(BF)
                more.append(col_sum(raised))
            for h in range(HEADS):
                heads = slice(h * 64, h * 64 + 64)
                acc_ref[heads, :] = acc_ref[heads, :] * fade[h] + nn(vt_refs[source][0, heads, here], raised_ref[h])
            top_ref[...] = jnp.concatenate(new, 0)
            total_ref[...] = total_ref[...] * jnp.concatenate(fade, 0) + jnp.concatenate(more, 0)

        over_tiles(causal, dims, row, segs, info, segq_ref, segk_ref, bias_ref, qin, body)
        total = total_ref[...]
        lse_ref[0, :, queries] = top_ref[...] + jnp.log(total)
        inverse = 1.0 / total
        for h in range(HEADS):
            heads = slice(h * 64, h * 64 + 64)
            acc_ref[heads, :] = acc_ref[heads, :] * inverse[h : h + 1, :]
        att_ref[0, queries, :] = acc_ref[...].T.astype(BF)
        return carry

    lax.fori_loop(0, dims.block // dims.tile, query_tile, 0)


def forward_kernel(causal, dims, far_count, segs, info, q_ref, segq_ref, segk_ref, base_ref, w_kv_ref, w_out_ref, w_cq_ref, vec_ref, k_ref, vt_ref, *refs):
    far_refs, refs = refs[: far_count * (dims.blocks - 1)], refs[far_count * (dims.blocks - 1) :]
    outs = 5 if causal else 4
    att_ref, lse_ref, unit_ref, rstd_ref = refs[:4]
    far_keys = refs[outs : outs + 4 * (dims.blocks - 1)]
    scratch = refs[outs + 4 * (dims.blocks - 1) :]
    row = pl.program_id(0)
    width = dims.width
    k_refs, vt_refs = [k_ref], [vt_ref]
    at = width if causal else 0
    for source in range(1, dims.blocks):
        keys = far_keys[4 * source - 4 : 4 * source]
        for which in range(far_count):
            ref = far_refs[far_count * (source - 1) + which]
            need = far_needed(causal, dims, info, which if far_count == 2 else 1, source)
            if far_count == 2:
                need = need & (row == which)

            @pl.when(need)
            def _(ref=ref, keys=keys):
                put_keys(nn(ref[0], w_kv_ref[:, at:]), vec_ref, 1 if causal else 5, *keys)

        k_refs.append(keys[0])
        vt_refs.append(keys[3])
    forward_tiles(causal, dims, row, segs, info, q_ref, segq_ref, segk_ref, k_refs, vt_refs, att_ref, lse_ref, scratch)
    base = base_ref[0].astype(F32)
    if not causal:
        base = base * vec_ref[0:1, :] + vec_ref[ROW + 3 : ROW + 4, :]
    shift = ROW + 2 if causal else ROW + 6
    unit, rstd = norm(base + nn(att_ref[0], w_out_ref[...]) + vec_ref[shift : shift + 1, :])
    unit_ref[0] = unit
    rstd_ref[0] = jnp.broadcast_to(rstd, rstd_ref.shape[1:])
    if causal:
        normed = (unit * vec_ref[0:1, :] + vec_ref[ROW + 3 : ROW + 4, :]).astype(BF)
        refs[4][0] = scaled(nn(normed, w_cq_ref[...]) + vec_ref[ROW + 4 : ROW + 5, :])


def attend_forward(causal, segs, info, q, segq, segk, base, w_kv, w_out, w_cq, vec, key, value_t, far):
    rows, block, width = q.shape
    key_block = key.shape[1]
    dims = Dims(rows, block, key_block, len(far) + 1, segs.shape[1], width)
    far_count = len(far[0]) if far else 1
    far_arrays = [a for arrays in far for a in arrays]
    base_spec = arg_spec(base.shape) if causal else row_spec(base.shape)
    far_specs = [row_spec(a.shape) if far_count == 1 else row_spec(a.shape, 0) for a in far_arrays]
    out_shape = [
        shape_of(q.shape, BF),
        shape_of((rows, HEADS, block), F32),
        shape_of(q.shape, F32),
        shape_of((rows, block, 128), F32),
    ] + [shape_of(q.shape, BF)] * causal
    keys = [shape_of((rows, key_block, width), BF)] * 2 + [shape_of((rows, width, key_block), BF)] * 2
    out_shape += keys * len(far)
    return call(
        functools.partial(forward_kernel, causal, dims, far_count),
        "attend_self" if causal else "attend_cross",
        14, (rows,),
        [row_spec(q.shape), arg_spec(segq.shape), arg_spec(segk.shape), base_spec]
        + [whole(w.shape) for w in (w_kv, w_out, w_cq, vec)]
        + [row_spec(key.shape), row_spec(value_t.shape)]
        + far_specs,
        [row_spec(s.shape) for s in out_shape],
        out_shape,
        forward_scratch(dims),
        52,
    )(segs, info, q, segq, segk, base, w_kv, w_out, w_cq, vec, key, value_t, *far_arrays)


def backward_scratch(dims):
    return [
        pltpu.VMEM((HEADS, dims.tile, 128), BF),
        pltpu.VMEM((HEADS, dims.tile, 128), BF),
        pltpu.VMEM((dims.step, dims.tile), F32),
        pltpu.VMEM((dims.width, dims.block), F32),
        pltpu.VMEM((dims.blocks, dims.key_block, dims.width), F32),
        pltpu.VMEM((dims.blocks, dims.key_block, dims.width), F32),
        pltpu.VMEM((HEADS, dims.step, dims.tile), F32),
        pltpu.VMEM((HEADS, dims.step, dims.tile), BF),
        pltpu.VMEM((HEADS, dims.step, dims.tile), BF),
    ]


def backward_tiles(causal, dims, row, segs, info, q_ref, do_ref, lse_ref, dd_ref, segq_ref, segk_ref, k_refs, kt_refs, v_refs, scratch):
    qm_ref, dm_ref, bias_ref, dq_ref, dk_ref, dv_ref, weight_ref, low_ref, ds_ref = scratch
    dk_ref[...] = jnp.zeros_like(dk_ref)
    dv_ref[...] = jnp.zeros_like(dv_ref)
    dq_ref[...] = jnp.zeros_like(dq_ref)

    def query_tile(i, carry):
        qin = pl.multiple_of(i * dims.tile, dims.tile)
        queries = pl.ds(qin, dims.tile)
        split_pairs(q_ref, qin, dims, qm_ref)
        split_pairs(do_ref, qin, dims, dm_ref)

        def body(source, inner):
            here = pl.ds(inner, dims.step)
            lse, dd = lse_ref[0, :, queries], dd_ref[0, :, queries]
            for h in range(HEADS):
                pair = slice(h // 2 * 128, h // 2 * 128 + 128)
                weights = jnp.exp(nt(k_refs[source][0, here, pair], qm_ref[h]) + bias_ref[...] - lse[h : h + 1, :])
                weight_ref[h] = weights
                low_ref[h] = weights.astype(BF)
            for h in range(HEADS):
                pair = slice(h // 2 * 128, h // 2 * 128 + 128)
                grads = nt(v_refs[source][0, here, pair], dm_ref[h])
                ds_ref[h] = (weight_ref[h] * (grads - dd[h : h + 1, :])).astype(BF)
            for h in range(0, HEADS, 2):
                pair = slice(h // 2 * 128, h // 2 * 128 + 128)
                dv_ref[source, here, pair] += nn(low_ref[h], dm_ref[h]) + nn(low_ref[h + 1], dm_ref[h + 1])
                dk_ref[source, here, pair] += nn(ds_ref[h], qm_ref[h]) + nn(ds_ref[h + 1], qm_ref[h + 1])
            for h in range(HEADS):
                heads = slice(h * 64, h * 64 + 64)
                dq_ref[heads, queries] += nn(kt_refs[source][0, heads, here], ds_ref[h])

        over_tiles(causal, dims, row, segs, info, segq_ref, segk_ref, bias_ref, qin, body)
        return carry

    lax.fori_loop(0, dims.block // dims.tile, query_tile, 0)
    return dq_ref[...].T * (dims.width // HEADS) ** -0.5


def head_products(a, b):
    turned = (a.astype(F32) * b.astype(F32)).T
    return jnp.concatenate([col_sum(turned[h * 64 : h * 64 + 64]) for h in range(HEADS)], 0)


def put(buffer, earlier, at, value, first, part):
    done = 0
    while done < value.shape[0]:
        b, inner = divmod(first + done, part)
        count = min(part - inner, value.shape[0] - done)
        rows = slice(at + inner, at + inner + count)
        piece = value[done : done + count]
        if earlier is not None:
            piece = piece + earlier[b, rows, :].astype(F32)
        buffer[b, rows, :] = piece.astype(BF)
        done += count


class Halves:
    def __init__(self, info, buffer, outs, sems):
        self.side, self.buffer, self.outs, self.sems = info[SIDE], buffer, outs, sems
        self.half = buffer.shape[1] // 2

    def each(self, h, what):
        source = self.buffer.at[:, h * self.half : (h + 1) * self.half, :]
        for k, here in enumerate((self.side == h, self.side != h)):
            pl.when(here)(what(pltpu.make_async_copy(source, self.outs[k], self.sems.at[h])))

    def start(self, h):
        self.each(h, lambda copy: copy.start)

    def wait(self):
        for h in range(2):
            self.each(h, lambda copy: copy.wait)


def sum_specs(buffer_shape, last):
    blocks, rows, lanes = buffer_shape
    if last:
        half = shape_of((blocks, rows // 2, lanes), BF)
        return [half] * 2, [pl.BlockSpec(memory_space=pl.ANY)] * 2, [pltpu.VMEM(buffer_shape, BF), pltpu.SemaphoreType.DMA((2,))]
    return [shape_of(buffer_shape, BF)], [whole(buffer_shape)], []


def backward_kernel(causal, dims, row, pickers, has_earlier, has_base, last, segs, info, *refs):
    take = iter(refs)

    def some(count):
        return [next(take) for _ in range(count)]

    blocks, width = dims.blocks, dims.width
    segq_ref, segk_ref, lse_ref, dd_ref, vec_ref, vec_in = some(6)
    sources = some(len(pickers))
    if has_base:
        next(take)
    outs = some((0 if causal else 3) + blocks + (1 if causal else 0))
    vec_out = next(take)
    sum_outs = some(2 if last else 1)
    scratch = some(9)
    acc_ref, buffer, in_sems, out_sems, sum_sems = some(5)
    places = some(len(pickers))
    out_refs = some(len(outs))

    needs = [None] + [far_needed(causal, dims, info, row, source) for source in range(1, blocks)]
    fetches = []
    for k, (source, place, picker) in enumerate(zip(sources, places, pickers)):
        index, of_source = picker
        if index == "arg":
            index = info[ORDER + row]
        fetches.append(Fetch(source, place, in_sems.at[k], index, None if of_source is None else needs[of_source]))
    take = iter(fetches)
    q_get, do_get = some(2)
    own = some(3)
    others = [some(3) for _ in range(1, blocks)]
    x_gets = some(blocks)
    early = 5 + 3 * (blocks - 1)
    for f in fetches[:early]:
        f.start()
    if not causal:
        w_kv_get, unit1_get, rstd1_get, wcq_get, gp2_get, att_get, wso_get = some(7)
    earlier_get = next(take) if has_earlier else None

    leaving = []

    def leave(k):
        out = outs[k]
        if not causal and k == 3:
            out = out.at[pl.ds(info[ORDER + row], 1)]
        leaving.append(pltpu.make_async_copy(out_refs[k], out, out_sems.at[k]))
        leaving[-1].start()

    vec_out[...] = vec_in[...]
    part = width // blocks
    dk_ref, dv_ref = scratch[4:6]
    q_ref, do_ref = q_get.wait(), do_get.wait()
    k_refs, v_refs, kt_refs = zip(*[[g.wait() for g in gets] for gets in (own, *others)])
    for f in fetches[early:]:
        f.start()
    dq = backward_tiles(causal, dims, row, segs, info, q_ref, do_ref, lse_ref, dd_ref, segq_ref, segk_ref, k_refs, kt_refs, v_refs, scratch)
    low_q = dq.astype(BF)
    x_refs = [g.wait() for g in x_gets]
    if causal:
        out_refs[blocks][0] = low_q
        leave(blocks)
        shift_v, first_dx, first = 1, 0, part
    else:
        shift_v, first_dx, first = 5, 3, 2 * part
        w_kv = w_kv_get.wait()

    for source in range(blocks):
        place = out_refs[first_dx + source]

        def back(source=source, place=place):
            x = x_refs[source][0]
            dv = dv_ref[source]
            low = jnp.concatenate([dk_ref[source].astype(BF), dv.astype(BF)], 1)
            vec_out[ROW + shift_v : ROW + shift_v + 1, :] += col_sum(dv)
            if causal:
                place[0] = low
            else:
                place[0] = nt(low, w_kv[...]).astype(place.dtype)
            more = tn(x, low)
            if source == 0:
                acc_ref[...] = more
            else:
                acc_ref[...] += more

        if source == 0:
            back()
        else:
            pl.when(needs[source])(back)

            @pl.when(jnp.logical_not(needs[source]))
            def _(place=place):
                place[...] = jnp.zeros_like(place)

        leave(first_dx + source)

    earlier = earlier_get.wait() if has_earlier else None
    for p in range(2 * width // 512):
        put(buffer, earlier, first + p * part, acc_ref[:, p * 512 : (p + 1) * 512], 0, part)
    if causal:
        vec_out[ROW : ROW + 1, :] += col_sum(dq)
        put(buffer, earlier, 0, tn(x_refs[0][0], low_q), 0, part)
    else:
        unit1 = unit1_get.wait()[0]
        rstd1 = rstd1_get.wait()[0]
        wcq, gp2 = wcq_get.wait(), gp2_get.wait()
        grad = gp2[0] + nt(low_q, wcq[...])
        gp1 = norm_back(grad, unit1, rstd1[:, :1], vec_ref[0:1, :])
        out_refs[0][0] = gp1
        leave(0)
        low_one = gp1.astype(BF)
        att, wso = att_get.wait()[0], wso_get.wait()
        put(buffer, earlier, part, tn(att, low_one), 0, part)
        normed = (unit1 * vec_ref[0:1, :] + vec_ref[ROW + 3 : ROW + 4, :]).astype(BF)
        put(buffer, earlier, 0, tn(normed, low_q), 0, part)
        if not last:
            leaving.append(pltpu.make_async_copy(buffer, sum_outs[0], sum_sems.at[0]))
            leaving[-1].start()
        datt = nt(low_one, wso[...]).astype(BF)
        out_refs[1][0] = datt
        leave(1)
        out_refs[2][0] = head_products(datt, att)
        leave(2)
        vec_out[0:1, :] += col_sum(grad * unit1)
        vec_out[ROW + 2 : ROW + 3, :] += col_sum(gp1)
        vec_out[ROW + 3 : ROW + 4, :] += col_sum(grad)
        vec_out[ROW + 4 : ROW + 5, :] += col_sum(dq)

    if causal and last:
        base = 3 * part * (width // 512)
        buffer[:, base:, :] = jnp.zeros((blocks, buffer.shape[1] - base, 512), BF)
        hidden_part = 4 * 512 // blocks
        for b in range(blocks):
            buffer[b, base : base + UP, :part] = vec_out[:UP, b * part : (b + 1) * part].astype(BF)
            for k in range(max(1, hidden_part // 512)):
                at = b * hidden_part + k * 512
                count = min(512, hidden_part)
                piece = vec_out[UP + at // 512 : UP + at // 512 + 1, at % 512 : at % 512 + count]
                buffer[b, base + UP + k : base + UP + k + 1, :count] = piece.astype(BF)
    if last:
        halves = Halves(info, buffer, sum_outs, sum_sems)
        halves.start(0)
        halves.start(1)
        halves.wait()
    elif causal:
        leaving.append(pltpu.make_async_copy(buffer, sum_outs[0], sum_sems.at[0]))
        leaving[-1].start()
    for c in leaving:
        c.wait()


def attend_backward(causal, row, last, us, segs, info, q, segq, segk, d_out, lse, dd, vec, vec_in, keys, keys_t, values, inputs, w_kv, extra, earlier, base):
    rows, block, width = q.shape
    blocks, key_block = len(keys), keys[0].shape[1]
    dims = Dims(rows, block, key_block, blocks, segs.shape[1], width)

    def at(a):
        return row if a.shape[0] == rows else 0

    def spec(a):
        return row_spec(a.shape, at(a))

    small = [segq, segk, lse, dd, vec, vec_in]
    small_specs = [arg_spec(segq.shape, row), arg_spec(segk.shape, row), spec(lse), spec(dd), whole(vec.shape), whole(vec_in.shape)]
    large = [(q, (row, None)), (d_out, (at(d_out), None))]
    for s in range(blocks):
        large += [(a[s], (row, None if s == 0 else s)) for a in (keys, values, keys_t)]
    large += [(a, ("arg" if s == 0 else at(a), None if s == 0 else s)) for s, a in enumerate(inputs)]
    if not causal:
        gp2, unit1, rstd1, att, wcq, wso = extra
        large += [(w_kv, (None, None)), (unit1, (row, None)), (rstd1, (row, None)), (wcq, (None, None))]
        large += [(gp2, (row, None)), (att, (row, None)), (wso, (None, None))]
    if earlier is not None:
        large.append((earlier, (None, None)))
    out_shape = []
    if not causal:
        out_shape += [shape_of((1, block, width), F32), shape_of((1, block, width), BF), shape_of((1, HEADS, block), F32)]
    if causal:
        out_shape += [shape_of((1, key_block, 2 * width), BF) for s in range(blocks)] + [shape_of((1, block, width), BF)]
    else:
        out_shape += [shape_of((1, key_block, width), F32 if s == 0 else BF) for s in range(blocks)]
    vec_shape = shape_of((VROWS, width), F32)
    buffer_rows = (3 if causal else 4) * width // blocks * (width // 512) + (VECTOR_ROWS if causal and last else 0)
    buffer_shape = (blocks, buffer_rows, 512)
    sum_shapes = [shape_of((blocks, buffer_rows // 2, 512), BF)] * 2 if last else [shape_of(buffer_shape, BF)]
    anywhere = pl.BlockSpec(memory_space=pl.ANY)
    out_places = [pltpu.VMEM(s.shape, s.dtype) for s in out_shape]
    if not causal:
        out_shape[3] = shape_of((rows, key_block, width), F32)
    bases = [] if base is None else [base]
    aliases = {2 + len(small) + len(large): 3} if bases else {}
    places = [pltpu.VMEM(a.shape if p[0] is None else (1, *a.shape[1:]), a.dtype) for a, p in large]
    return call(
        functools.partial(backward_kernel, causal, dims, row, [p for _, p in large], earlier is not None, base is not None, last),
        "attend_self_back" if causal else "attend_cross_back",
        us, (1,),
        small_specs + [anywhere] * (len(large) + len(bases)),
        [anywhere] * len(out_shape) + [whole(vec_shape.shape)] + [anywhere] * len(sum_shapes),
        out_shape + [vec_shape] + sum_shapes,
        backward_scratch(dims)
        + [
            pltpu.VMEM((width, 2 * width), F32),
            pltpu.VMEM(buffer_shape, BF),
            pltpu.SemaphoreType.DMA((len(large),)),
            pltpu.SemaphoreType.DMA((len(out_shape),)),
            pltpu.SemaphoreType.DMA((2,)),
        ]
        + places
        + out_places,
        SELF_MIB if causal else MIB,
        aliases,
    )(segs, info, *small, *[a for a, _ in large], *bases)


def tokens_back_kernel(rows, blocks, segs, info, *refs):
    take = iter(refs)
    per_row = [[next(take) for _ in range(2 + blocks)] for _ in range(rows)]
    w_ref, base_out = next(take), next(take)
    outs = [[next(take) for _ in range(1, blocks)] for _ in range(rows)]
    width = w_ref.shape[0]
    for r, (dq_ref, base_ref, *dkv_refs) in enumerate(per_row):
        for source in range(blocks):
            grad = nt(dkv_refs[source][0], w_ref[:, width:])
            if source == 0:
                base_out[info[ORDER + r]] = grad + nt(dq_ref[0], w_ref[:, :width]) + base_ref[0]
            else:
                outs[r][source - 1][0] = grad.astype(BF)


def tokens_back(segs, info, found, gp1, w):
    rows, blocks = len(found), len(found[0]) - 1
    args = []
    for (*dkv, dq), base in zip(found, gp1):
        args += [dq, base, *dkv]
    args.append(w)
    block = gp1[0].shape[1:]
    out_shape = [shape_of((rows, *block), F32)] + [shape_of((1, *block), BF)] * (rows * (blocks - 1))
    base, *got = call(
        functools.partial(tokens_back_kernel, rows, blocks), "tokens_back", 8, (1,),
        [whole(a.shape) for a in args], [whole(s.shape) for s in out_shape], out_shape, [], SELF_MIB,
    )(segs, info, *args)
    return base, *[got[r * (blocks - 1) : (r + 1) * (blocks - 1)] for r in range(rows)]


def feed_kernel(dims, far_count, segs, info, q_ref, segq_ref, segk_ref, unit1_ref, cot_ref, upshift_ref, vec_ref, k_ref, vt_ref, wckv_ref, wco_ref, wup_any, wdown_any, *refs):
    take = iter(refs)

    def some(count):
        return [next(take) for _ in range(count)]

    blocks = dims.blocks
    far_refs = some(far_count * (blocks - 1))
    lse_ref, out_ref, gp2_ref, dco_ref, dcross_ref, vec_out, keep_ref, send_ref = some(8)
    far_keys = [some(3) for _ in range(1, blocks)]
    hid_ref, slope_ref, low_up_ref, normed_ref, low3_ref, co_all_ref, low2_ref, buffer, sems = some(9)
    wup_ref, wdown_ref, w_sems, att_ref = some(4)
    far_vt = some(blocks - 1)
    scratch = some(7)
    width, hidden_width = wup_ref.shape
    panels = hidden_width // 512
    block = dims.block
    row = pl.program_id(0)
    here = pl.ds(pl.multiple_of(row * block, block), block)
    weights = [pltpu.make_async_copy(wup_any, wup_ref, w_sems.at[0]), pltpu.make_async_copy(wdown_any, wdown_ref, w_sems.at[1])]

    @pl.when(row == 0)
    def _():
        vec_out[...] = jnp.zeros_like(vec_out)
        for w in weights:
            w.start()

    k_refs, vt_refs = [k_ref], [vt_ref]
    for source in range(1, blocks):
        keys = (*far_keys[source - 1], far_vt[source - 1])
        for which in range(far_count):
            ref = far_refs[far_count * (source - 1) + which]
            need = far_needed(False, dims, info, which if far_count == 2 else 1, source)
            if far_count == 2:
                need = need & (row == which)

            @pl.when(need)
            def _(ref=ref, keys=keys):
                put_keys(nn(ref[0], wckv_ref[...]), vec_ref, 5, *keys)

        k_refs.append(keys[0])
        vt_refs.append(keys[3])
    forward_tiles(False, dims, row, segs, info, q_ref, segq_ref, segk_ref, k_refs, vt_refs, att_ref, lse_ref, scratch)
    co = att_ref[0]
    co_all_ref[here, :] = co
    normed_one = unit1_ref[0] * vec_ref[0:1, :] + vec_ref[ROW + 3 : ROW + 4, :]
    unit2, rstd2 = norm(normed_one + nn(co, wco_ref[...]) + vec_ref[ROW + 6 : ROW + 7, :])

    @pl.when(row == 0)
    def _():
        for w in weights:
            w.wait()

    normed = unit2 * vec_ref[1:2, :] + vec_ref[ROW + 7 : ROW + 8, :]
    normed_low = normed.astype(BF)
    normed_ref[here, :] = normed_low
    for p in range(panels):
        cols = slice(p * 512, (p + 1) * 512)
        up = nn(normed_low, wup_ref[:, cols]) + upshift_ref[p : p + 1, :]
        square = up * up
        bent = jnp.tanh(up * (GELU_A + GELU_B * square))
        half = 0.5 * up
        hid_ref[here, cols] = (half + half * bent).astype(BF)
        slope_ref[:, cols] = 0.5 + 0.5 * bent + half * (1.0 - bent * bent) * (GELU_A + 3 * GELU_B * square)
    pre = normed + nn(hid_ref[here, :], wdown_ref[...]) + vec_ref[ROW + 8 : ROW + 9, :]
    unit3, rstd3 = norm(pre)
    out_ref[0] = (unit3 * vec_ref[2:3, :] + vec_ref[ROW + 9 : ROW + 10, :]).astype(BF)
    cot = cot_ref[0].astype(F32)
    gp3 = norm_back(cot, unit3, rstd3, vec_ref[2:3, :])
    low3 = gp3.astype(BF)
    low3_ref[here, :] = low3
    vec_out[2:3, :] += col_sum(cot * unit3)
    vec_out[ROW + 8 : ROW + 9, :] += col_sum(gp3)
    vec_out[ROW + 9 : ROW + 10, :] += col_sum(cot)
    for p in range(panels):
        cols = slice(p * 512, (p + 1) * 512)
        grad_up = nt(low3, wdown_ref[cols, :]) * slope_ref[:, cols]
        low_up_ref[here, cols] = grad_up.astype(BF)
        vec_out[UP + p : UP + p + 1, :] += col_sum(grad_up)
    grad = gp3 + nt(low_up_ref[here, :], wup_ref[...])
    gp2 = norm_back(grad, unit2, rstd2, vec_ref[1:2, :])
    gp2_ref[0] = gp2
    low2 = gp2.astype(BF)
    low2_ref[here, :] = low2
    dco = nt(low2, wco_ref[...]).astype(BF)
    dco_ref[0] = dco
    dcross_ref[0] = head_products(dco, co)
    vec_out[1:2, :] += col_sum(grad * unit2)
    vec_out[ROW + 6 : ROW + 7, :] += col_sum(gp2)
    vec_out[ROW + 7 : ROW + 8, :] += col_sum(grad)

    @pl.when(row == pl.num_programs(0) - 1)
    def _():
        down, part = hidden_width // blocks, width // blocks
        halves = Halves(info, buffer, (keep_ref, send_ref), sems)
        started = False
        for p in range(panels):
            cols = slice(p * 512, (p + 1) * 512)
            put(buffer, None, 0, tn(hid_ref[:, cols], low3_ref[...]), p * 512, down)
        for p in range(panels):
            cols = slice(p * 512, (p + 1) * 512)
            put(buffer, None, down + p * part, tn(normed_ref[...], low_up_ref[:, cols]), 0, part)
            if not started and down + (p + 1) * part >= halves.half:
                halves.start(0)
                started = True
        put(buffer, None, down + panels * part, tn(co_all_ref[...], low2_ref[...]), 0, part)
        halves.start(1)
        halves.wait()


def feed(segs, info, q, segq, segk, unit1, cot, up_rows, vec, key, value_t, wckv, wco, wup, wdown, far):
    rows, block, width = unit1.shape
    hidden = wup.shape[1]
    tokens = rows * block
    key_block = key.shape[1]
    blocks = len(far) + 1
    dims = Dims(rows, block, key_block, blocks, segs.shape[1], width)
    far_count = len(far[0]) if far else 1
    far_arrays = [a for arrays in far for a in arrays]
    far_specs = [row_spec(a.shape) if far_count == 1 else row_spec(a.shape, 0) for a in far_arrays]
    buffer_shape = (blocks, (2 * hidden + width) // blocks, width)
    shapes, specs, more = sum_specs(buffer_shape, True)
    rest = [
        shape_of(unit1.shape, BF),
        shape_of(unit1.shape, F32),
        shape_of(unit1.shape, BF),
        shape_of((rows, HEADS, block), F32),
    ]
    lse_shape, vec_shape = shape_of((rows, HEADS, block), F32), shape_of((VROWS, width), F32)
    keys = ([shape_of((rows, key_block, width), BF)] * 2 + [shape_of((rows, width, key_block), BF)]) * (blocks - 1)
    anywhere = pl.BlockSpec(memory_space=pl.ANY)
    return call(
        functools.partial(feed_kernel, dims, far_count), "attend_cross_feed", 40, (rows,),
        [row_spec(q.shape), arg_spec(segq.shape), arg_spec(segk.shape), row_spec(unit1.shape), arg_spec(cot.shape)]
        + [whole(up_rows.shape), whole(vec.shape), row_spec(key.shape), row_spec(value_t.shape)]
        + [whole(wckv.shape), whole(wco.shape), anywhere, anywhere]
        + far_specs,
        [row_spec(lse_shape.shape), arg_spec(unit1.shape)]
        + [row_spec(s.shape) for s in rest[1:]]
        + [whole(vec_shape.shape)]
        + specs
        + [row_spec(s.shape) for s in keys],
        [lse_shape] + rest + [vec_shape] + shapes + keys,
        [
            pltpu.VMEM((tokens, hidden), BF),
            pltpu.VMEM((block, hidden), F32),
            pltpu.VMEM((tokens, hidden), BF),
            pltpu.VMEM((tokens, width), BF),
            pltpu.VMEM((tokens, width), BF),
            pltpu.VMEM((tokens, width), BF),
            pltpu.VMEM((tokens, width), BF),
        ]
        + more
        + [pltpu.VMEM(wup.shape, BF), pltpu.VMEM(wdown.shape, BF), pltpu.SemaphoreType.DMA((2,)), pltpu.VMEM((1, block, width), BF)]
        + [pltpu.VMEM((1, width, key_block), BF)] * (blocks - 1)
        + forward_scratch(dims),
        60,
    )(segs, info, q, segq, segk, unit1, cot, up_rows, vec, key, value_t, wckv, wco, wup, wdown, *far_arrays)


def bits(size):
    return size.bit_length() - 1


def all_pairs(mask):
    return [(i, i ^ mask) for i in range(lax.axis_size("dp") * lax.axis_size("blk"))]


def swap(values, mask):
    return lax.ppermute(values, ("dp", "blk"), all_pairs(mask))


def place():
    return lax.axis_index("dp") * lax.axis_size("blk") + lax.axis_index("blk")


def by_place(parts, at, count):
    for bit in range(count):
        side = ((at >> bit) & 1) == 1
        parts = [jnp.where(side, parts[j ^ (1 << bit)], parts[j]) for j in range(len(parts))]
    return parts


class Sum:
    def __init__(self, keep, send, urgent):
        self.values = [keep, send]
        self.near = bits(lax.axis_size("blk"))
        self.far = bits(lax.axis_size("dp")) - 2
        far = [self.far_gather] if urgent else [functools.partial(self.pair_gather, bit) for bit in reversed(range(self.far))]
        self.steps = [self.core, self.near_scatter, self.far_scatter, *far, self.near_gather, self.core_gather]

    def step(self):
        if self.steps:
            self.values = self.steps.pop(0)(*self.values)

    def core(self, keep, send):
        return [(keep.astype(F32) + swap(send, 1 << self.near).astype(F32)).astype(BF)]

    def near_scatter(self, now):
        blocks = now.shape[0]
        cut = now.reshape(blocks, 2, now.shape[1] // 2, now.shape[2])
        mine, side = lax.axis_index("blk"), (lax.axis_index("dp") >> 1) & 1

        def piece(b, s):
            return lax.dynamic_slice(cut, (mine ^ b, side ^ s, 0, 0), (1, 1, *cut.shape[2:]))[0, 0]

        total = piece(0, 0).astype(F32)
        for s in range(2):
            for b in range(blocks):
                if s or b:
                    total = total + swap(piece(b, s), (2 * s << self.near) | b).astype(F32)
        return [total.astype(BF)]

    def far_scatter(self, now):
        at = lax.axis_index("dp") >> 2
        cut = now.reshape(1 << self.far, -1, now.shape[1])
        total = lax.dynamic_index_in_dim(cut, at, 0, False).astype(F32)
        for k in range(1, 1 << self.far):
            piece = lax.dynamic_index_in_dim(cut, at ^ k, 0, False)
            total = total + swap(piece, (k << 2) << self.near).astype(F32)
        return [total.astype(BF)]

    def far_gather(self, now):
        at = lax.axis_index("dp") >> 2
        parts = [now] + [swap(now, (k << 2) << self.near) for k in range(1, 1 << self.far)]
        return [jnp.concatenate(by_place(parts, at, self.far), 0)]

    def pair_gather(self, bit, now):
        side = lax.axis_index("dp") >> 2 >> bit
        chunk = now.shape[0] >> (self.far - 1 - bit)
        parts = [p.reshape(-1, 1, chunk, now.shape[1]) for p in (now, swap(now, (4 << bit) << self.near))]
        return [jnp.concatenate(by_place(parts, side, 1), 1).reshape(-1, now.shape[1])]

    def near_gather(self, now):
        at = (lax.axis_index("dp") >> 1) & 1
        return [jnp.concatenate(by_place([now, swap(now, 2 << self.near)], at, 1), 0)]

    def core_gather(self, now):
        return [now, swap(now, 1 << self.near)]

    def rows(self):
        return jnp.concatenate(by_place(self.values, lax.axis_index("dp") & 1, 1), 0)


def advance(sums, anchor, begun=()):
    for s in sums:
        s.step()
    sums = [*sums, *begun]
    flat, anchor = lax.optimization_barrier(([s.values for s in sums], anchor))
    for s, values in zip(sums, flat):
        s.values = values
    return anchor


def from_next(values, step):
    size = lax.axis_size("blk")
    return lax.ppermute(values, "blk", [((i + step) % size, i) for i in range(size)])


def to_next(values, step):
    size = lax.axis_size("blk")
    return lax.ppermute(values, "blk", [(i, (i + step) % size) for i in range(size)])


def unpanel(part, columns):
    panels = columns // 512
    rows = part.shape[0] // panels
    return jnp.concatenate([part[p * rows : (p + 1) * rows] for p in range(panels)], 1).astype(F32)


def body(tokens, memory, segments, w_qkv, w_self_out, w_cross_q, w_cross_kv, w_cross_out, w_up, w_down, norm_gains, shifts, up_shift, cotangent):
    rows, block, width = tokens.shape
    mem_block = memory.shape[1]
    blocks = lax.axis_size("blk")
    mine = lax.axis_index("blk")
    seq_len = segments.shape[1]
    mem_len = mem_block * blocks
    hidden = w_up.shape[1]
    far = range(1, blocks)

    pick = rows == 2
    if pick:
        single = (segments[0, -1] != 0).astype(jnp.int32)
        order = jnp.stack([1 - single, single])
        edges = np.arange(1, blocks) * block
        crosses = jnp.any((segments[:, edges - 1] == segments[:, edges]) & (jnp.arange(2) != single)[:, None])
    else:
        order, crosses = jnp.arange(rows), jnp.array(True)
    head = jnp.stack([mine, lax.axis_index("dp") & 1, crosses.astype(jnp.int32)])
    info = jnp.concatenate([head, order]).astype(jnp.int32)

    def fetch(arrays):
        if not pick:
            return [[[from_next(a, k)] for k in far] for a in arrays]
        ones = [[from_next(lax.dynamic_index_in_dim(a, single, 0, True), k) for k in far] for a in arrays]
        others = [lax.dynamic_index_in_dim(a, 1 - single, 0, True) for a in arrays]
        others = lax.cond(
            crosses,
            lambda vs: [[from_next(v, k) for k in far] for v in vs],
            lambda vs: [[v for _ in far] for v in vs],
            others,
        )
        return [[[o, g] for o, g in zip(*pair)] for pair in zip(others, ones)]

    far_toks, far_mems = fetch([tokens, memory])

    vec = jnp.concatenate([norm_gains.T, shifts.T, jnp.zeros((3, width), F32)], 0)
    up_rows = up_shift.reshape(-1, 512)
    seg_rows = segments.astype(F32)[:, None, :]
    mem_seg = seg_rows[:, :, np.arange(mem_len) * seq_len // mem_len] if mem_len != seq_len else seg_rows

    q, k, v, kt, vt, ck, cv, ckt, cvt = project(segments, info, tokens, memory, w_qkv, w_cross_kv, vec)
    att, lse1, unit1, rstd1, cq, *keys = attend_forward(
        True, segments, info, q, seg_rows, seg_rows, tokens, w_qkv, w_self_out, w_cross_q, vec, k, vt, far_toks
    )
    k1, v1, kt1 = [[own] + keys[at::4] for at, own in enumerate((k, v, kt))]
    lse2, out, gp2, dco, dd2, vectors, keep, send, *keys = feed(
        segments, info, cq, seg_rows, mem_seg, unit1, cotangent, up_rows, vec, ck, cvt, w_cross_kv, w_cross_out, w_up, w_down, far_mems
    )
    k2, v2, kt2 = [[own] + keys[at::3] for at, own in enumerate((ck, cv, ckt))]
    sums = [Sum(keep, send, False)]

    def far_of(found, r):
        return [f[r] if len(f) > 1 else f[0] for f in found]

    def give(found):
        if not pick:
            return [[to_next(o, k) for k, o in zip(far, others)] for others in found]
        return [None, [to_next(o, k) for k, o in zip(far, found[1])]]

    def give_others(founds):
        return lax.cond(
            crosses,
            lambda many: [[to_next(o, k) for k, o in zip(far, vs)] for vs in many],
            lambda many: [list(vs) for vs in many],
            [list(found[0]) for found in founds],
        )

    def total(base, got):
        if pick:
            is_one = (jnp.arange(2) == single)[:, None, None]
            parts = [jnp.where(is_one, one, other) for other, one in zip(*got)]
        else:
            parts = [jnp.concatenate([row[k] for row in got], 0) for k in range(blocks - 1)]
        return functools.reduce(lambda a, b: a + b.astype(F32), parts, base)

    earlier, rows_gp1, dmem, memory_base = None, [], [], None
    for r in range(rows):
        last = r == rows - 1
        gp1, datt, dd1, *rest = attend_backward(
            False, r, last, 24 if last else 14, segments, info, cq, seg_rows, mem_seg, dco, lse2, dd2, vec, vectors,
            k2, kt2, v2, [memory] + far_of(far_mems, r), w_cross_kv,
            [gp2, unit1, rstd1, att, w_cross_q, w_self_out], earlier, memory_base,
        )
        memory_base = rest[0]
        dmem.append(rest[1:blocks])
        vectors, earlier = rest[blocks], rest[-1]
        rows_gp1.append((gp1, datt, dd1))
        vectors = advance(sums, vectors)
    sums.append(Sum(*rest[-2:], False))
    got_mem = give(dmem)
    earlier, dkv = None, []
    for r in range(rows):
        last = r == rows - 1
        _, datt, dd1 = rows_gp1[r]
        rest = attend_backward(
            True, r, last, 14 if last else 11, segments, info, q, seg_rows, seg_rows, datt, lse1, dd1, vec, vectors,
            k1, kt1, v1, [tokens] + far_of(far_toks, r), None, [], earlier, None,
        )
        dkv.append(rest[: blocks + 1])
        vectors, earlier = rest[blocks + 1], rest[-1]
        if not last:
            vectors, got_mem = advance(sums, (vectors, got_mem))
    dkv = advance(sums, dkv)
    sums.append(Sum(*rest[-2:], True))
    tokens_base, *dtok = tokens_back(segments, info, dkv, [g[0] for g in rows_gp1], w_qkv)
    first, second, third = sums
    dtok = advance(sums, dtok)

    part, hidden_part = width // blocks, hidden // blocks
    dtok, got_mem = advance([second, third], (dtok, got_mem))
    got_tok = give(dtok)
    if pick:
        got_mem[0], got_tok[0] = give_others([dmem, dtok])
    first.step()
    got_mem = advance([second, third], got_mem)
    got_mem = advance([second, third], got_mem, [first])
    while first.steps:
        first.step()
    up_at = hidden_part + (hidden // 512) * part
    feed_sum = first.rows()
    found = (
        total(memory_base, got_mem),
        feed_sum[up_at:].astype(F32),
        unpanel(feed_sum[hidden_part:up_at], hidden),
        feed_sum[:hidden_part].astype(F32),
    )
    (grad_memory, grad_cross_out, grad_up, grad_down), got_tok = advance([second, third], (found, got_tok))
    while second.steps:
        second.step()
    other_sum = second.rows()
    found = (
        total(tokens_base, got_tok),
        other_sum[part : 2 * part].astype(F32),
        other_sum[:part].astype(F32),
        unpanel(other_sum[2 * part :], 2 * width),
    )
    grad_tokens, grad_self_out, grad_cross_q, grad_cross_kv = advance([third], found)
    while third.steps:
        third.step()
    qkv_sum = third.rows()
    qkv_rows = 3 * part * (width // 512)
    vectors = qkv_sum[qkv_rows:].astype(F32)
    return (
        out,
        grad_tokens,
        grad_memory,
        unpanel(qkv_sum[:qkv_rows], 3 * width),
        grad_self_out,
        grad_cross_q,
        grad_cross_kv,
        grad_cross_out,
        grad_up,
        grad_down,
        vectors[:ROW, :part].T,
        vectors[ROW:UP, :part].T,
        vectors[UP : UP + max(1, hidden_part // 512), : min(512, hidden_part)].reshape(-1),
    )


def solution(mesh):
    split = P("dp", "blk", None)
    in_specs = (split, split, P("dp", None)) + (P(),) * 10 + (split,)
    out_specs = (split,) * 3 + (P("blk", None),) * 9 + (P("blk"),)
    return jax.shard_map(body, mesh=mesh, in_specs=in_specs, out_specs=out_specs, check_vma=False)
```
